32 devices in a mesh: dp: 8 (over y, x, core), tensor: 4 (over z).
Axes of the slice: x: 2, y: 2, z: 4, core: 2. Of those that a mesh axis runs over, the one named last changes fastest.
Arguments:
- tokens: bfloat16 [16, 1568, 1024], P('dp', 'tensor'), may hold values from -6 to 6
- cotangent: bfloat16 [16, 1568, 1024], P('dp', 'tensor'), may hold values from -6 to 6
- clip_live: int32 [16], P('dp'), may hold values from 0 to 1, as said below
- adapter_index: int32 [16], P('dp'), may hold values from 0 to 7
- gain_one: float32 [1024], replicated, may hold values from 0.25 to 1.75
- gain_two: float32 [1024], replicated, may hold values from 0.25 to 1.75
- weight_qkv: bfloat16 [3, 1024, 1024], P(None, 'dp', 'tensor'), may hold values from -0.1875 to 0.1875
- weight_out: bfloat16 [1024, 1024], P('tensor', 'dp'), may hold values from -6 to 6
- weight_fc1: bfloat16 [1024, 4096], P('dp', 'tensor'), may hold values from -0.1875 to 0.1875
- weight_fc2: bfloat16 [4096, 1024], P('tensor', 'dp'), may hold values from -0.09375 to 0.09375
- qkv_down: bfloat16 [8, 16, 1024], replicated, may hold values from -0.1875 to 0.1875
- qkv_up: bfloat16 [8, 3, 16, 1024], replicated, may hold values from -0.75 to 0.75
- out_down: bfloat16 [8, 16, 1024], replicated, may hold values from -6 to 6
- out_up: bfloat16 [8, 16, 1024], replicated, may hold values from -0.75 to 0.75
- fc1_down: bfloat16 [8, 16, 1024], replicated, may hold values from -0.1875 to 0.1875
- fc1_up: bfloat16 [8, 16, 4096], replicated, may hold values from -0.75 to 0.75
- fc2_down: bfloat16 [8, 16, 4096], replicated, may hold values from -0.09375 to 0.09375
- fc2_up: bfloat16 [8, 16, 1024], replicated, may hold values from -0.75 to 0.75
Outputs:
- layer_out: bfloat16 [16, 1568, 1024], P('dp', 'tensor')
- grad_tokens: bfloat16 [16, 1568, 1024], P('dp', 'tensor')
- grad_qkv_down: float32 [8, 16, 1024], replicated
- grad_qkv_up: float32 [8, 3, 16, 1024], replicated
- grad_out_down: float32 [8, 16, 1024], replicated
- grad_out_up: float32 [8, 16, 1024], replicated
- grad_fc1_down: float32 [8, 16, 1024], replicated
- grad_fc1_up: float32 [8, 16, 4096], replicated
- grad_fc2_down: float32 [8, 16, 4096], replicated
- grad_fc2_up: float32 [8, 16, 1024], replicated
The draws below stay inside these ranges and needn't reach their ends.
Inputs may be any that keep to these rules, and one draw needn't show every extreme that they name: `clip_live`: 1 where the slot holds a clip; the first of the 2 slots of every index of dp always does, index 0 of dp holds 2 clips and index 1 holds one.
All inputs are finite; a program needn't handle non-finite values.
Results may differ from the reference program's by a relative error of at most 0.018.
Values may be sent and summed in bfloat16 or wider, within the bound.
A program may use at most 256 MiB of HBM per device.

```python
import jax
import jax.numpy as jnp
from jax import lax

D = 1024
HEADS = 16
HEAD_DIM = 64
FF = 4096
RANK = 16
ADAPTERS = 8
CLIP_LEN = 1568
SLOTS = 2
CLIPS = 16


def draw_clip_live(key, part):
    key = jax.random.fold_in(key, 11)
    tosses = jax.random.randint(key, (CLIPS,), 0, 2)
    position = jnp.arange(CLIPS, dtype=jnp.int32)
    leading = position % SLOTS == 0
    tosses = jnp.where(leading, 1, tosses)
    tosses = jnp.where(position == SLOTS - 1, 1, tosses)
    tosses = jnp.where(position == 2 * SLOTS - 1, 0, tosses)
    return tosses.astype(jnp.int32)


def plant(entries, rng, low, largest):
    extent = entries.shape
    place = [jax.random.randint(jax.random.fold_in(rng, axis), (), 0, extent[axis]) for axis in range(len(extent))]
    entries = entries.at[tuple(place)].set(low)
    longest = extent.index(max(extent))
    place[longest] = (place[longest] + 1) % extent[longest]
    return entries.at[tuple(place)].set(largest)


def level_of(key, extent, pieces, least, largest):
    def one(dim, shards_of):
        heights = jax.random.uniform(jax.random.fold_in(jax.random.fold_in(key, 6), dim), (shards_of,), jnp.float32, least / len(pieces), largest / len(pieces))
        return jnp.repeat(jnp.exp(heights), extent[dim] // shards_of).reshape((-1,) + (1,) * (len(extent) - dim - 1))

    level = one(*pieces[0])
    for cut in pieces[1:]:
        level = level * one(*cut)
    return level


def normal_values(own_key, dims, spread, reach, split=(), held_as=jnp.bfloat16):
    drawn = jax.random.normal(own_key, dims, jnp.float32) * spread
    if len(split) > 0:
        drawn = level_of(own_key, dims, split, -0.22, 0.18) * drawn
    return jnp.clip(drawn, min=-reach, max=reach).astype(held_as)


def setup_inputs(seed: int = 0) -> dict:
    key_list = jax.random.split(jax.random.key(seed), 19)
    tokens = normal_values(key_list[0], (CLIPS, CLIP_LEN, D), 1.0, 6.0, ((0, 8), (1, 4)))
    cotangent = normal_values(key_list[1], (CLIPS, CLIP_LEN, D), 1.0, 6.0, ((0, 8), (1, 4)))
    clip_live = draw_clip_live(jax.random.fold_in(key_list[18], 71), 0)
    adapter_index = plant(jax.random.randint(key_list[3], (CLIPS,), 0, ADAPTERS), jax.random.fold_in(key_list[3], 1), 0, ADAPTERS - 1).astype(jnp.int32)
    gain_one = jnp.clip(1.0 + 0.15 * jax.random.normal(key_list[4], (D,), jnp.float32), 0.25, 1.75)
    gain_two = jnp.clip(1.0 + 0.15 * jax.random.normal(key_list[5], (D,), jnp.float32), 0.25, 1.75)
    weight_qkv = normal_values(key_list[6], (3, D, D), D ** -0.5, 0.1875, ((1, 8), (2, 4)))
    weight_out = normal_values(key_list[7], (D, D), (max(3 * D // CLIP_LEN, 1)) ** -0.5, 6.0, ((0, 4), (1, 8)))
    weight_fc1 = normal_values(key_list[8], (D, FF), D ** -0.5, 0.1875, ((0, 8), (1, 4)))
    weight_fc2 = normal_values(key_list[9], (FF, D), FF ** -0.5, 0.09375, ((0, 4), (1, 8)))
    qkv_down = normal_values(key_list[10], (ADAPTERS, RANK, D), D ** -0.5, 0.1875)
    qkv_up = normal_values(key_list[11], (ADAPTERS, 3, RANK, D), (4 * RANK) ** -0.5, 0.75)
    out_down = normal_values(key_list[12], (ADAPTERS, RANK, D), (max(3 * D // CLIP_LEN, 1)) ** -0.5, 6.0)
    out_up = normal_values(key_list[13], (ADAPTERS, RANK, D), (4 * RANK) ** -0.5, 0.75)
    fc1_down = normal_values(key_list[14], (ADAPTERS, RANK, D), D ** -0.5, 0.1875)
    fc1_up = normal_values(key_list[15], (ADAPTERS, RANK, FF), (4 * RANK) ** -0.5, 0.75)
    fc2_down = normal_values(key_list[16], (ADAPTERS, RANK, FF), FF ** -0.5, 0.09375)
    fc2_up = normal_values(key_list[17], (ADAPTERS, RANK, D), (4 * RANK) ** -0.5, 0.75)
    return {"tokens": tokens, "cotangent": cotangent, "clip_live": clip_live, "adapter_index": adapter_index, "gain_one": gain_one, "gain_two": gain_two, "weight_qkv": weight_qkv, "weight_out": weight_out, "weight_fc1": weight_fc1, "weight_fc2": weight_fc2, "qkv_down": qkv_down, "qkv_up": qkv_up, "out_down": out_down, "out_up": out_up, "fc1_down": fc1_down, "fc1_up": fc1_up, "fc2_down": fc2_down, "fc2_up": fc2_up}


@jax.custom_vjp
def low(v):
    return lax.optimization_barrier(v.astype(jnp.bfloat16)).astype(jnp.float32)

@jax.custom_vjp
def low_back(v):
    return v

def low_keep(v):
    return (low(v), None)

def low_pass(kept, grad):
    return (grad,)

def back_keep(v):
    return (v, None)

def back_low(kept, grad):
    return (low(grad),)
low.defvjp(low_keep, low_pass)
low_back.defvjp(back_keep, back_low)
highest_precision = lax.Precision.HIGHEST
eps_norm = 1e-06

def block_count(length):
    number = max(1, length // 512)
    while length % number:
        number -= 1
    return number

def normalize(field, gain_vec):
    average = lax.optimization_barrier(jnp.mean(field, axis=-1, keepdims=True))
    centered = field - average
    variance = lax.optimization_barrier(jnp.mean(centered * centered, axis=-1, keepdims=True))
    return centered * lax.rsqrt(variance + eps_norm) * gain_vec

def attend(queries, all_keys, all_values):
    score_scale = HEAD_DIM ** (-0.5)
    blocks = block_count(CLIP_LEN)
    block_rows = CLIP_LEN // blocks

    def one_block(query_block):
        scores = jnp.einsum('qhc,khc->hqk', query_block, all_keys, precision=highest_precision) * score_scale
        soft_weights = jax.nn.softmax(low_back(scores), axis=-1)
        return jnp.einsum('hqk,khc->qhc', low(soft_weights), all_values, precision=highest_precision)
    query_blocks = queries.reshape(blocks, block_rows, HEADS, HEAD_DIM)
    return lax.map(jax.checkpoint(one_block), query_blocks).reshape(CLIP_LEN, D)

def clip_layer(clip_rows, live_flag, frozen, picked):
    gain_first, gain_second, complete_query_key_value, complete_output_projection, complete_first_linear, complete_second_linear = frozen
    down_qkv, up_qkv, down_out, up_out, down_fc1, up_fc1, down_fc2, up_fc2 = picked
    normed_one = low(normalize(clip_rows, gain_first))
    low_qkv = jnp.dot(normed_one, down_qkv.T, precision=highest_precision)
    projected_rows = jnp.einsum('ld,jdc->jlc', normed_one, complete_query_key_value, precision=highest_precision)
    projected_rows = projected_rows + jnp.einsum('lr,jrc->jlc', low_qkv, up_qkv, precision=highest_precision)
    projected_rows = low(low_back(projected_rows)).reshape(3, CLIP_LEN, HEADS, HEAD_DIM)
    attention_context = low(low_back(attend(projected_rows[0], projected_rows[1], projected_rows[2])))
    lowrank_output = jnp.dot(attention_context, down_out.T, precision=highest_precision)
    attention = jnp.dot(attention_context, complete_output_projection, precision=highest_precision) + jnp.dot(lowrank_output, up_out, precision=highest_precision)
    middle = clip_rows + low_back(attention)
    normed_two = low(normalize(middle, gain_second))
    low_fc1 = jnp.dot(normed_two, down_fc1.T, precision=highest_precision)
    preactivation = jnp.dot(normed_two, complete_first_linear, precision=highest_precision) + jnp.dot(low_fc1, up_fc1, precision=highest_precision)
    preactivation = low_back(preactivation)
    hidden_state = low(jax.nn.gelu(preactivation, approximate=False))
    lowrank_second_linear = jnp.dot(hidden_state, down_fc2.T, precision=highest_precision)
    feed = jnp.dot(hidden_state, complete_second_linear, precision=highest_precision) + jnp.dot(lowrank_second_linear, up_fc2, precision=highest_precision)
    return live_flag * (middle + low_back(feed))

def reference(tokens, cotangent, clip_live, adapter_index, gain_one, gain_two, weight_qkv, weight_out, weight_fc1, weight_fc2, qkv_down, qkv_up, out_down, out_up, fc1_down, fc1_up, fc2_down, fc2_up):
    frozen = (gain_one.astype(jnp.float32), gain_two.astype(jnp.float32), weight_qkv.astype(jnp.float32), weight_out.astype(jnp.float32), weight_fc1.astype(jnp.float32), weight_fc2.astype(jnp.float32))
    adapters = tuple((source.astype(jnp.float32) for source in (qkv_down, qkv_up, out_down, out_up, fc1_down, fc1_up, fc2_down, fc2_up)))

    def clip_step(running, inputs):
        clip_rows, clip_cot, live_flag, chosen_index = inputs
        chosen = tuple((source[chosen_index] for source in adapters))

        def forward(rows_in, picked):
            return clip_layer(rows_in, live_flag.astype(jnp.float32), frozen, picked)
        outcome, pullback = jax.vjp(forward, clip_rows.astype(jnp.float32), chosen)
        grad_rows, grad_picked = pullback(clip_cot.astype(jnp.float32))
        running = tuple((summed.at[chosen_index].add(piece) for summed, piece in zip(running, grad_picked)))
        return (running, (outcome.astype(jnp.bfloat16), grad_rows.astype(jnp.bfloat16)))
    initial = tuple((jnp.zeros_like(source) for source in adapters))
    totals, (outputs, grad_inputs) = lax.scan(clip_step, initial, (tokens, cotangent, clip_live, adapter_index))
    return (outputs, grad_inputs, totals[0], totals[1], totals[2], totals[3], totals[4], totals[5], totals[6], totals[7])
```

```python
import functools
import math

import jax
import jax.numpy as jnp
from jax import lax
from jax.experimental import pallas as pl
from jax.experimental.pallas import tpu as pltpu
from jax.sharding import PartitionSpec as P

HEAD_DIM = 64
EPS = 1e-06
F32 = jnp.float32
BF16 = jnp.bfloat16
NT = (((1,), (1,)), ((), ()))
TN = (((0,), (0,)), ((), ()))
VMEM_BYTES = 58 << 20
SAFE_SCORE = 60.0


def mm(a, b):
    return jnp.dot(a, b, preferred_element_type=F32)


def mm_nt(a, b):
    return lax.dot_general(a, b, NT, preferred_element_type=F32)


def mm_tn(a, b):
    return lax.dot_general(a, b, TN, preferred_element_type=F32)


def norm_parts(field):
    centered = field - jnp.mean(field, axis=-1, keepdims=True)
    scale = lax.rsqrt(jnp.mean(centered * centered, axis=-1, keepdims=True) + EPS)
    return centered * scale, scale


def norm_back(normed, scale, gain, incoming):
    weighted = incoming * gain
    return scale * (
        weighted
        - jnp.mean(weighted, axis=-1, keepdims=True)
        - normed * jnp.mean(weighted * normed, axis=-1, keepdims=True)
    )


def params(*semantics):
    return pltpu.CompilerParams(vmem_limit_bytes=VMEM_BYTES)


class Plan:
    def __init__(self, dps, tens):
        self.tens = tens
        bits = [1 << i for i in range(1, dps.bit_length() - 1)]
        self.orders = (bits + [1], bits[::-1] + [1])
        self.hops = dps - 1
        self.ways = []
        for order in self.orders:
            blocks = [0]
            for bit in order:
                blocks = blocks + [r | bit for r in blocks]
            tops = {r: max([j for j, bit in enumerate(order) if r & bit], default=-1) for r in blocks}
            sends = {r: range(tops[r] + 1, len(order)) for r in blocks}
            ids = {}
            for r in blocks:
                for j in sends[r]:
                    ids[(r, j)] = len(ids)
            blocks.sort(key=lambda r: bin(r).count("1"))
            self.ways.append((order, blocks, tops, sends, ids))

    def semaphores(self, items):
        dma = lambda *shape: pltpu.SemaphoreType.DMA(shape)
        near = self.tens - 1
        return [dma(items), dma(items, near), dma(items, near), dma(items, self.hops), dma(items, self.hops)]

    def greet(self):
        me, t = lax.axis_index("dp"), lax.axis_index("tensor")
        peers = [(me, lax.rem(t + k, self.tens)) for k in range(1, self.tens)]
        peers += [(me ^ bit, t) for bit in self.orders[0]]
        barrier = pltpu.get_barrier_semaphore()
        for peer in peers:
            pl.semaphore_signal(barrier, inc=1, device_id=peer, device_id_type=pl.DeviceIdType.MESH)
        pl.semaphore_wait(barrier, len(peers))


class Item:
    def __init__(self, plan, sems, number, src, spot, order):
        self.plan, self.src, self.spot = plan, src, spot
        self.local, self.zs, self.zr, self.ss, self.rs = [s.at[number] for s in sems]
        self.order, self.blocks, self.tops, self.sends, self.ids = plan.ways[order]
        self.me, self.t = lax.axis_index("dp"), lax.axis_index("tensor")
        self.stages = [r for r in self.blocks if len(self.sends[r])]

    def keep(self):
        return pltpu.make_async_copy(self.src, self.spot(self.me, self.t), self.local)

    def along(self, d, arriving=False):
        n = self.plan.tens
        return pltpu.make_async_remote_copy(
            src_ref=self.src,
            dst_ref=self.spot(self.me, lax.rem(self.t + n - d, n) if arriving else self.t),
            send_sem=self.zs.at[d - 1],
            recv_sem=self.zr.at[d - 1],
            device_id=(self.me, lax.rem(self.t + d, n)),
            device_id_type=pl.DeviceIdType.MESH,
        )

    def across(self, r, j, arriving=False):
        bit, n = self.order[j], self.ids[(r, j)]
        block = self.me ^ r
        return pltpu.make_async_remote_copy(
            src_ref=self.spot(block, None),
            dst_ref=self.spot(block ^ bit if arriving else block, None),
            send_sem=self.ss.at[n],
            recv_sem=self.rs.at[n],
            device_id=(self.me ^ bit, self.t),
            device_id_type=pl.DeviceIdType.MESH,
        )

    def start(self):
        self.keep().start()
        for d in range(1, self.plan.tens):
            self.along(d).start()

    def arrived(self, r):
        if r == 0:
            self.keep().wait()
            for d in range(1, self.plan.tens):
                self.along(d, True).wait_recv()
        else:
            j = self.tops[r]
            self.across(r ^ self.order[j], j, True).wait_recv()

    def advance(self, stage):
        r = self.stages[stage]
        self.arrived(r)
        for j in self.sends[r]:
            self.across(r, j).start()

    def finish(self):
        for r in self.blocks:
            if not len(self.sends[r]):
                self.arrived(r)
        for d in range(1, self.plan.tens):
            self.along(d).wait_send()
        for r in self.blocks:
            for j in self.sends[r]:
                self.across(r, j).wait_send()


def schedule(items):
    pairs = [items[k : k + 2] for k in range(0, len(items), 2)]
    stages = len(items[0].stages)
    steps = []
    for s in range(len(pairs) + stages):
        def step(s=s):
            for item in (pairs[:2] if s == 0 else pairs[s + 1 : s + 2]):
                for one in item:
                    one.start()
            for n, pair in enumerate(pairs):
                if 0 <= s - n < stages:
                    for one in pair:
                        one.advance(s - n)
        steps.append(step)
    def close():
        for item in items:
            item.finish()
    return steps + [close]


def at(ref, cut):
    return lambda a, t: ref.at[a, :, cut] if t is None else ref.at[a, t, cut]


def gather_kernel(plan, cuts, x_ref, o_ref, *sems):
    plan.greet()
    size = x_ref.shape[0] // cuts
    items = []
    for k in range(cuts):
        cut = pl.ds(k * size, size)
        items.append(Item(plan, sems, k, x_ref.at[cut], at(o_ref, cut), k % 2))
    for step in schedule(items):
        step()


def gather(plan, dps, x, cuts, number):
    return pl.pallas_call(
        functools.partial(gather_kernel, plan, cuts),
        in_specs=[pl.BlockSpec(memory_space=pl.ANY)],
        out_specs=pl.BlockSpec(memory_space=pl.ANY),
        out_shape=jax.ShapeDtypeStruct((dps, plan.tens) + x.shape, x.dtype),
        scratch_shapes=plan.semaphores(cuts),
        compiler_params=pltpu.CompilerParams(collective_id=number, has_side_effects=True),
        name="gather",
    )(x)


def share_kernel(plan, x_ref, o_ref, got, src, swap_send, swap_recv, *sems):
    plan.greet()
    me, t = lax.axis_index("dp"), lax.axis_index("tensor")
    mine = lax.rem(me, 2)
    swap = pltpu.make_async_remote_copy(
        src_ref=x_ref.at[1 - mine], dst_ref=got, send_sem=swap_send, recv_sem=swap_recv,
        device_id=(me ^ 1, t), device_id_type=pl.DeviceIdType.MESH,
    )
    swap.start()
    swap.wait()
    src[...] = (x_ref[mine].astype(F32) + got[...].astype(F32)).astype(BF16)
    cuts = src.shape[0]
    items = [Item(plan, sems, k, src.at[pl.ds(k, 1)], at(o_ref, pl.ds(k, 1)), k % 2) for k in range(cuts)]
    for step in schedule(items):
        step()


def share(plan, dps, pieces, cuts, number):
    flat = jnp.concatenate(pieces, axis=-1).astype(BF16)
    rank, cols = flat.shape
    cols = cols // (2 * cuts)
    flat = flat.reshape(rank, 2, cuts, cols).transpose(1, 2, 0, 3)
    return pl.pallas_call(
        functools.partial(share_kernel, plan),
        in_specs=[pl.BlockSpec(memory_space=pltpu.VMEM)],
        out_specs=pl.BlockSpec(memory_space=pl.ANY),
        out_shape=jax.ShapeDtypeStruct((dps, plan.tens, cuts, rank, cols), BF16),
        scratch_shapes=[pltpu.VMEM((cuts, rank, cols), BF16), pltpu.VMEM((cuts, rank, cols), BF16),
                        pltpu.SemaphoreType.DMA, pltpu.SemaphoreType.DMA] + plan.semaphores(cuts),
        compiler_params=pltpu.CompilerParams(collective_id=number, has_side_effects=True),
        name="share",
    )(flat)


def qkv_kernel(info, xa_ref, xb_ref, gain_ref, w_ref, down_ref, up_ref, q_ref, kv_ref, low_ref, n_s, low_s):
    half = xa_ref.shape[0]
    parts, width = w_ref.shape[1], w_ref.shape[4]
    depth = n_s.shape[1]
    step = pl.program_id(0)

    @pl.when(step == 0)
    def _():
        for part, ref in enumerate((xa_ref, xb_ref)):
            normed, _ = norm_parts(ref[...].astype(F32))
            n_s[part * half : (part + 1) * half, :] = normed * gain_ref[...]

    n = n_s[...].astype(BF16)

    @pl.when(step == 0)
    def _():
        low = mm_nt(n, down_ref[0])
        low_ref[...] = low
        low_s[...] = low

    low = low_s[...].astype(BF16)
    for part in range(parts):
        cols = slice(part * width, (part + 1) * width)
        res = mm(n, w_ref[:, part, 0].reshape(depth, width)) + mm(low, up_ref[0, 0, :, cols])
        res = res.astype(BF16)

        @pl.when(step == 0)
        def _():
            q_ref[:, cols] = res

        @pl.when(step > 0)
        def _():
            kv_ref[0, :, cols] = res


def project(info, xa, xb, gain, w, down, up):
    half, depth = xa.shape
    rows = 2 * half
    rank = down.shape[1]
    dp, tens, _, wr, wc = w.shape
    whole = lambda *shape: pl.BlockSpec(shape, lambda j, info: (0,) * len(shape))
    return pl.pallas_call(
        qkv_kernel,
        grid_spec=pltpu.PrefetchScalarGridSpec(
            num_scalar_prefetch=1,
            grid=(3,),
            in_specs=[
                whole(half, depth),
                whole(half, depth),
                whole(1, depth),
                pl.BlockSpec((dp, tens, 1, wr, wc), lambda j, info: (0, 0, j, 0, 0)),
                pl.BlockSpec((1, rank, depth), lambda j, info: (info[0], 0, 0)),
                pl.BlockSpec((1, 1, rank, depth), lambda j, info: (info[0], j, 0, 0)),
            ],
            out_specs=[
                whole(rows, depth),
                pl.BlockSpec((1, rows, depth), lambda j, info: (jnp.maximum(j - 1, 0), 0, 0)),
                whole(rows, rank),
            ],
            scratch_shapes=[pltpu.VMEM((rows, depth), F32), pltpu.VMEM((rows, rank), F32)],
        ),
        out_shape=[
            jax.ShapeDtypeStruct((rows, depth), BF16),
            jax.ShapeDtypeStruct((2, rows, depth), BF16),
            jax.ShapeDtypeStruct((rows, rank), F32),
        ],
        compiler_params=params(),
        name="project",
    )(info, xa, xb, gain, w, down, up)


def attend_pair(q2, ks, vs, shifted):
    lane = lax.broadcasted_iota(jnp.int32, (1, 128), 1)
    outs, lses = [], []
    for h in range(2):
        mine = (lane // HEAD_DIM) == h
        s = mm_nt(jnp.where(mine, q2, BF16(0)), ks[...])
        if shifted:
            m = jnp.max(s, axis=1, keepdims=True)
            p = jnp.exp(s - m).astype(BF16)
        else:
            p = jnp.exp(s).astype(BF16)
        o = mm(p, vs[h])
        total = pltpu.roll(o, HEAD_DIM, 1)
        outs.append(o / total)
        lse = jnp.log(jnp.where(mine, total, o))
        lses.append(lse + m if shifted else lse)
    return (
        jnp.where(lane < HEAD_DIM, outs[0], outs[1]).astype(BF16),
        jnp.where(lane < HEAD_DIM, lses[0], lses[1]),
    )


def stage_keys(k_ref, v_ref, k2_ref, v2_ref, ks, vs):
    rows = k_ref.shape[1]
    lane = lax.broadcasted_iota(jnp.int32, (1, 128), 1)
    ks[0:rows, :] = k_ref[0]
    ks[rows:, :] = k2_ref[0]
    for h in range(2):
        mine = (lane // HEAD_DIM) == h
        vs[h, 0:rows, :] = jnp.where(mine, v_ref[0], BF16(1))
        vs[h, rows:, :] = jnp.where(mine, v2_ref[0], BF16(1))


def attend_exact_kernel(q_ref, k_ref, v_ref, k2_ref, v2_ref, o_ref, lse_ref, ks, vs):
    stage_keys(k_ref, v_ref, k2_ref, v2_ref, ks, vs)
    o_ref[...], lse_ref[...] = attend_pair(q_ref[...] * BF16(HEAD_DIM ** -0.5), ks, vs, True)


def attend_specs(rows):
    flat = pl.BlockSpec((rows, 128), lambda i: (0, i))
    part = lambda j: pl.BlockSpec((1, rows, 128), lambda i: (j, 0, i))
    return flat, [flat, part(0), part(1), part(0), part(1)]


def attend_exact(q, kv, kv2):
    rows, depth = q.shape
    flat, blocks = attend_specs(rows)
    return pl.pallas_call(
        attend_exact_kernel,
        grid=(depth // 128,),
        in_specs=blocks,
        out_specs=[flat, flat],
        out_shape=[jax.ShapeDtypeStruct((rows, depth), BF16), jax.ShapeDtypeStruct((rows, depth), F32)],
        scratch_shapes=[pltpu.VMEM((2 * rows, 128), BF16), pltpu.VMEM((2, 2 * rows, 128), BF16)],
        compiler_params=params(),
        name="attend_exact",
    )(q, kv, kv, kv2, kv2)


def attend_gather_kernel(
    plan, cuts, heads_of, q_ref, k_ref, v_ref, k2_ref, v2_ref, wo_ref, w1_ref, w2_ref,
    o_ref, lse_ref, reach_ref, go_ref, g1_ref, g2_ref, ks, vs, *sems
):
    step, last = pl.program_id(0), pl.num_programs(0) - 1
    items = []
    for ref, out in ((wo_ref, go_ref), (w1_ref, g1_ref), (w2_ref, g2_ref)):
        n = 2 if ref is wo_ref else cuts
        size = ref.shape[0] // n
        for k in range(n):
            cut = pl.ds(k * size, size)
            items.append((ref.at[cut], at(out, cut)))
    items = items[:2] + [one for k in range(cuts) for one in (items[2 + k], items[2 + cuts + k])]
    items = [Item(plan, sems, n, src, spot, n % 2) for n, (src, spot) in enumerate(items)]
    steps = schedule(items)
    steps = [lambda first=steps[0]: (plan.greet(), first())] + steps[1:]
    heads = heads_of
    for n in range(heads):
        @pl.when(step == n)
        def _():
            if n < len(steps):
                steps[n]()

    stage_keys(k_ref, v_ref, k2_ref, v2_ref, ks, vs)
    q2 = q_ref[...] * BF16(HEAD_DIM ** -0.5)
    lane = lax.broadcasted_iota(jnp.int32, (1, 128), 1)
    reach = jnp.zeros((), F32)
    qf, kf = q2.astype(F32), ks[...].astype(F32)
    for h in range(2):
        mine = (lane // HEAD_DIM) == h
        far = lambda x: jnp.max(jnp.sum(jnp.where(mine, x * x, 0.0), axis=1, keepdims=True), axis=0, keepdims=True)
        reach = jnp.maximum(reach, far(qf) * far(kf))
    reach_ref[...] = jnp.broadcast_to(reach, reach_ref.shape)
    o_ref[...], lse_ref[...] = attend_pair(q2, ks, vs, False)

    @pl.when(step == last)
    def _():
        for one in steps[heads:]:
            one()


def attend_gather(plan, dps, q, kv, kv2, wo, w1, w2, cuts, number):
    rows, depth = q.shape
    flat, blocks = attend_specs(rows)
    hbm = pl.BlockSpec(memory_space=pl.ANY)
    big = lambda w: jax.ShapeDtypeStruct((dps, plan.tens) + w.shape, w.dtype)
    grid = depth // 128
    kernel = functools.partial(attend_gather_kernel, plan, cuts, grid)
    ctx, lse, reach, go, g1, g2 = pl.pallas_call(
        kernel,
        grid=(grid,),
        in_specs=blocks + [hbm] * 3,
        out_specs=[flat, flat, pl.BlockSpec((1, 8, 128), lambda i: (i, 0, 0)), hbm, hbm, hbm],
        out_shape=[jax.ShapeDtypeStruct((rows, depth), BF16), jax.ShapeDtypeStruct((rows, depth), F32),
                   jax.ShapeDtypeStruct((grid, 8, 128), F32), big(wo), big(w1), big(w2)],
        scratch_shapes=[pltpu.VMEM((2 * rows, 128), BF16), pltpu.VMEM((2, 2 * rows, 128), BF16)]
        + plan.semaphores(2 + 2 * cuts),
        compiler_params=pltpu.CompilerParams(
            vmem_limit_bytes=VMEM_BYTES, collective_id=number, has_side_effects=True
        ),
        name="attend_gather",
    )(q, kv, kv, kv2, kv2, wo, w1, w2)
    safe = jnp.max(reach) <= SAFE_SCORE * SAFE_SCORE
    ctx, lse = lax.cond(safe, lambda: (ctx, lse), lambda: tuple(attend_exact(q, kv, kv2)))
    return ctx, lse, go, g1, g2


def gelu_both(x):
    cdf = 0.5 * (1.0 + lax.erf(x * (2.0 ** -0.5)))
    pdf = jnp.exp(-0.5 * x * x) * ((2.0 * math.pi) ** -0.5)
    return x * cdf, cdf + x * pdf


def feed_kernel(
    info, xa_ref, xb_ref, ca_ref, cb_ref, ctx_ref, gain_ref, wo_ref, w1_ref, w2_ref,
    od_ref, ou_ref, d1_ref, u1_ref, d2_ref, u2_ref,
    la_ref, lb_ref, gm_ref, gctx_ref, g_od, g_ou, g_d1, g_u1, g_d2, g_u2,
    wo_s, w1_s, w2_s, mid_s, n_s, gf_s, feed_s, gn_s, lowo_s, low1_s, low2_s, b1_s, b2_s,
):
    half, depth = xa_ref.shape
    rows = 2 * half
    step, last = pl.program_id(0), pl.num_programs(0) - 1
    live = info[1].astype(F32)
    dp, tens, wop, wor, woc = wo_ref.shape
    fp, fr, fc = w1_ref.shape[2:]

    @pl.when(step == 0)
    def _():
        for a in range(dp):
            for t in range(tens):
                for k in range(wop):
                    row = (t * wop + k) * wor
                    wo_s[row : row + wor, a * woc : (a + 1) * woc] = wo_ref[a, t, k]
        ctx = ctx_ref[...]
        low = mm_nt(ctx, od_ref[0])
        lowo_s[...] = low
        attention = mm(ctx, wo_s[...]) + mm(low.astype(BF16), ou_ref[0])
        for part, ref in enumerate((xa_ref, xb_ref)):
            s = slice(part * half, (part + 1) * half)
            mid_s[s, :] = ref[...].astype(F32) + attention[s, :]
        for part, ref in enumerate((ca_ref, cb_ref)):
            s = slice(part * half, (part + 1) * half)
            gm_ref[s, :] = ref[...].astype(F32) * live
        gf_s[...] = gm_ref[...].astype(BF16)
        normed, _ = norm_parts(mid_s[...])
        n_s[...] = (normed * gain_ref[...]).astype(BF16)
        low1_s[...] = mm_nt(n_s[...], d1_ref[0])
        b2_s[...] = mm_nt(gf_s[...], u2_ref[0])
        feed_s[...] = jnp.zeros_like(feed_s)
        gn_s[...] = jnp.zeros_like(gn_s)
        low2_s[...] = jnp.zeros_like(low2_s)
        b1_s[...] = jnp.zeros_like(b1_s)

    for a in range(dp):
        for k in range(fp):
            w1_s[a * fr : (a + 1) * fr, k * fc : (k + 1) * fc] = w1_ref[a, 0, k]
        w2_s[:, a * woc : (a + 1) * woc] = w2_ref[a, 0].reshape(w2_s.shape[0], woc)
    w1, w2 = w1_s[...], w2_s[...]
    u1, d2 = u1_ref[0], d2_ref[0]
    n, gf = n_s[...], gf_s[...]
    low1, b2 = low1_s[...].astype(BF16), b2_s[...].astype(BF16)
    preact = mm(n, w1) + mm(low1, u1)
    ghid = mm_nt(gf, w2) + mm(b2, d2)
    hid, slope = gelu_both(preact)
    hid = hid.astype(BF16)
    gpre = (ghid * slope).astype(BF16)
    feed_s[...] += mm(hid, w2)
    gn_s[...] += mm_nt(gpre, w1)
    low2_s[...] += mm_nt(hid, d2)
    b1_s[...] += mm_nt(gpre, u1)
    g_d2[...] = mm_tn(b2, hid)
    g_u1[...] = mm_tn(low1, gpre)

    @pl.when(step == last)
    def _():
        low2, b1 = low2_s[...].astype(BF16), b1_s[...].astype(BF16)
        out = live * (mid_s[...] + feed_s[...] + mm(low2, u2_ref[0]))
        la_ref[...] = out[:half].astype(BF16)
        lb_ref[...] = out[half:].astype(BF16)
        g_u2[...] = mm_tn(low2, gf_s[...])
        gn = gn_s[...] + mm(b1, d1_ref[0])
        normed, scale = norm_parts(mid_s[...])
        g_d1[...] = mm_tn(b1, n_s[...])
        gm = gm_ref[...] + norm_back(normed, scale, gain_ref[...], gn)
        gm_ref[...] = gm
        ga = gm.astype(BF16)
        back = mm_nt(ga, ou_ref[0]).astype(BF16)
        gctx_ref[...] = (mm_nt(ga, wo_s[...]) + mm(back, od_ref[0])).astype(BF16)
        g_od[...] = mm_tn(back, ctx_ref[...])
        g_ou[...] = mm_tn(lowo_s[...].astype(BF16), ga)


def feed_forward(info, xa, xb, ca, cb, ctx, gain, wo, w1, w2, od, ou, d1, u1, d2, u2, cuts):
    half, depth = xa.shape
    rows = 2 * half
    rank = od.shape[1]
    dp, tens, wop, wor, woc = wo.shape
    fp, fr, fc = w1.shape[2:]
    rp, rr = w2.shape[2:4]
    hidden = fp * fc
    wide = hidden // cuts
    ff = hidden * tens
    once = lambda *shape: pl.BlockSpec(shape, lambda f, info: (0,) * len(shape), pipeline_mode=pl.Buffered(1))
    whole = lambda *shape: pl.BlockSpec(shape, lambda f, info: (0,) * len(shape))
    picked = pl.BlockSpec((1, rank, depth), lambda f, info: (info[0], 0, 0))
    picked_f = pl.BlockSpec((1, rank, wide), lambda f, info: (info[0], 0, f))
    unit = jax.ShapeDtypeStruct((rank, depth), F32)
    unit_f = jax.ShapeDtypeStruct((rank, ff), F32)
    block_f = pl.BlockSpec((rank, wide), lambda f, info: (0, f))
    return pl.pallas_call(
        feed_kernel,
        grid_spec=pltpu.PrefetchScalarGridSpec(
            num_scalar_prefetch=1,
            grid=(tens * cuts,),
            in_specs=[
                once(half, depth), once(half, depth), once(half, depth), once(half, depth),
                once(rows, depth),
                whole(1, depth),
                once(dp, tens, wop, wor, woc),
                pl.BlockSpec((dp, 1, fp // cuts, fr, fc), lambda f, info: (0, f // cuts, f % cuts, 0, 0)),
                pl.BlockSpec((dp, 1, rp // cuts, rr, woc), lambda f, info: (0, f // cuts, f % cuts, 0, 0)),
                picked, picked, picked, picked_f, picked_f, picked,
            ],
            out_specs=[
                whole(half, depth), whole(half, depth), whole(rows, depth), whole(rows, depth),
                whole(rank, depth), whole(rank, depth), whole(rank, depth), block_f, block_f, whole(rank, depth),
            ],
            scratch_shapes=[
                pltpu.VMEM((depth, depth), BF16),
                pltpu.VMEM((depth, wide), BF16),
                pltpu.VMEM((wide, depth), BF16),
                pltpu.VMEM((rows, depth), F32),
                pltpu.VMEM((rows, depth), BF16),
                pltpu.VMEM((rows, depth), BF16),
                pltpu.VMEM((rows, depth), F32),
                pltpu.VMEM((rows, depth), F32),
            ]
            + [pltpu.VMEM((rows, rank), F32)] * 5,
        ),
        out_shape=[
            jax.ShapeDtypeStruct((half, depth), BF16),
            jax.ShapeDtypeStruct((half, depth), BF16),
            jax.ShapeDtypeStruct((rows, depth), F32),
            jax.ShapeDtypeStruct((rows, depth), BF16),
            unit, unit, unit, unit_f, unit_f, unit,
        ],
        compiler_params=params(),
        name="feed_forward",
    )(info, xa, xb, ca, cb, ctx, gain, wo, w1, w2, od, ou, d1, u1, d2, u2)


def split3(x):
    hi = x.astype(BF16)
    rest = x - hi.astype(F32)
    mid = rest.astype(BF16)
    return hi, mid, (rest - mid.astype(F32)).astype(BF16)


def attend_back_kernel(
    q_ref, k_ref, v_ref, k2_ref, v2_ref, g_ref, o_ref, lse_ref, dq_ref, dk_ref, dv_ref, dk2_ref, dv2_ref, ks, vs, kd, acc
):
    rows = q_ref.shape[0]
    zero = BF16(0)
    lane = lax.broadcasted_iota(jnp.int32, (1, 128), 1)
    scale = BF16(HEAD_DIM ** -0.5)
    q2 = q_ref[...] * scale
    g2 = g_ref[...]
    hi, mid, lo = split3(pltpu.roll(lse_ref[...], HEAD_DIM, 1))
    prod = g2.astype(F32) * o_ref[...].astype(F32)
    qa, ga, qm, gm = [], [], [], []
    for h in range(2):
        mine, b = (lane // HEAD_DIM) == h, HEAD_DIM * (1 - h)
        qa.append(
            jnp.where(mine, q2, jnp.where(lane == b, -hi, jnp.where(lane == b + 1, -mid, jnp.where(lane == b + 2, -lo, zero))))
        )
        dh, dm, dl = split3(jnp.sum(jnp.where(mine, prod, 0.0), axis=1, keepdims=True))
        ga.append(
            jnp.where(mine, g2, jnp.where(lane == b, -dh, jnp.where(lane == b + 1, -dm, jnp.where(lane == b + 2, -dl, zero))))
        )
        qm.append(jnp.where(mine, q2, zero))
        gm.append(jnp.where(mine, g2, zero))
        ones = ((lane >= b) & (lane < b + 3)).astype(BF16)
        for i, (kr, vr) in enumerate(((k_ref, v_ref), (k2_ref, v2_ref))):
            s = slice(i * rows, (i + 1) * rows)
            ks[h, s, :] = jnp.where(mine, kr[0], ones)
            vs[h, s, :] = jnp.where(mine, vr[0], ones)
            kd[h, s, :] = jnp.where(mine, kr[0] * scale, zero)
    for i, (dk_out, dv_out) in enumerate(((dk_ref, dv_ref), (dk2_ref, dv2_ref))):
        s = slice(i * rows, (i + 1) * rows)
        dk = jnp.zeros((rows, 128), F32)
        dv = jnp.zeros((rows, 128), F32)
        dq = jnp.zeros((rows, 128), F32)
        for h in range(2):
            p = jnp.exp(mm_nt(ks[h, s, :], qa[h]))
            ds = (p * mm_nt(vs[h, s, :], ga[h])).astype(BF16)
            dv = dv + mm(p.astype(BF16), gm[h])
            dk = dk + mm(ds, qm[h])
            dq = dq + mm_tn(ds, kd[h, s, :])
        dk_out[0] = dk.astype(BF16)
        dv_out[0] = dv.astype(BF16)
        if i == 0:
            acc[...] = dq
        else:
            dq_ref[...] = (acc[...] + dq).astype(BF16)


def attend_back_body(*refs):
    *rest, dkv_ref, dkv2_ref, ks, vs, kd, acc = refs
    attend_back_kernel(
        *rest, dkv_ref.at[0:1], dkv_ref.at[1:2], dkv2_ref.at[0:1], dkv2_ref.at[1:2], ks, vs, kd, acc
    )


def attend_back(q, kv, kv2, g, ctx, lse):
    rows, depth = q.shape
    flat = pl.BlockSpec((rows, 128), lambda i: (0, i))
    part = lambda j: pl.BlockSpec((1, rows, 128), lambda i: (j, 0, i))
    both = pl.BlockSpec((2, rows, 128), lambda i: (0, 0, i))
    return pl.pallas_call(
        attend_back_body,
        grid=(depth // 128,),
        in_specs=[flat, part(0), part(1), part(0), part(1), flat, flat, flat],
        out_specs=[flat, both, both],
        out_shape=[jax.ShapeDtypeStruct((rows, depth), BF16)] + [jax.ShapeDtypeStruct((2, rows, depth), BF16)] * 2,
        scratch_shapes=[pltpu.VMEM((2, 2 * rows, 128), BF16)] * 3 + [pltpu.VMEM((rows, 128), F32)],
        compiler_params=params(),
        name="attend_back",
    )(q, kv, kv, kv2, kv2, g, ctx, lse)


def qkv_back_kernel(
    info, xa_ref, xb_ref, gain_ref, dq_ref, dkv_ref, dkv2_ref, gm_ref, low_ref, w_ref, down_ref, up_ref,
    ya_ref, yb_ref, g_down, g_up, gn_s, back_s,
):
    half, depth = xa_ref.shape
    parts, width = w_ref.shape[1], w_ref.shape[4]
    step, last = pl.program_id(0), pl.num_programs(0) - 1

    def go(g, first):
        back = mm_nt(g, up_ref[0, 0])
        total = back if first else back_s[...] + back
        back_s[...] = total
        acc = None if first else gn_s[...]
        for part in range(parts):
            cols = slice(part * width, (part + 1) * width)
            term = mm_nt(g[:, cols], w_ref[:, part, 0].reshape(depth, width))
            acc = term if acc is None else acc + term
        gn_s[...] = acc
        g_up[0] = mm_tn(low_ref[...].astype(BF16), g)

    @pl.when(step == 0)
    def _():
        go(dq_ref[...], True)

    @pl.when(step > 0)
    def _():
        go((dkv_ref[0].astype(F32) + dkv2_ref[0].astype(F32)).astype(BF16), False)

    @pl.when(step == last)
    def _():
        back = back_s[...].astype(BF16)
        gn_s[...] += mm(back, down_ref[0])
        total = jnp.zeros(g_down.shape, F32)
        for part, (x_ref, y_ref) in enumerate(((xa_ref, ya_ref), (xb_ref, yb_ref))):
            s = slice(part * half, (part + 1) * half)
            normed, scale = norm_parts(x_ref[...].astype(F32))
            total = total + mm_tn(back_s[s, :].astype(BF16), (normed * gain_ref[...]).astype(BF16))
            y_ref[...] = (gm_ref[s, :] + norm_back(normed, scale, gain_ref[...], gn_s[s, :])).astype(BF16)
        g_down[...] = total


def project_back(info, xa, xb, gain, dq, dkv, dkv2, gm, low, w, down, up):
    half, depth = xa.shape
    rows = 2 * half
    rank = down.shape[1]
    dp, tens, _, wr, wc = w.shape
    whole = lambda *shape: pl.BlockSpec(shape, lambda j, info: (0,) * len(shape))
    once = lambda *shape: pl.BlockSpec(shape, lambda j, info: (0,) * len(shape), pipeline_mode=pl.Buffered(1))
    pair = pl.BlockSpec((1, rows, depth), lambda j, info: (jnp.maximum(j - 1, 0), 0, 0))
    return pl.pallas_call(
        qkv_back_kernel,
        grid_spec=pltpu.PrefetchScalarGridSpec(
            num_scalar_prefetch=1,
            grid=(3,),
            in_specs=[
                once(half, depth), once(half, depth), whole(1, depth),
                once(rows, depth), pair, pair,
                once(rows, depth), once(rows, rank),
                pl.BlockSpec((dp, tens, 1, wr, wc), lambda j, info: (0, 0, j, 0, 0)),
                pl.BlockSpec((1, rank, depth), lambda j, info: (info[0], 0, 0)),
                pl.BlockSpec((1, 1, rank, depth), lambda j, info: (info[0], j, 0, 0)),
            ],
            out_specs=[
                whole(half, depth), whole(half, depth), whole(rank, depth),
                pl.BlockSpec((1, rank, depth), lambda j, info: (j, 0, 0)),
            ],
            scratch_shapes=[pltpu.VMEM((rows, depth), F32), pltpu.VMEM((rows, rank), F32)],
        ),
        out_shape=[
            jax.ShapeDtypeStruct((half, depth), BF16),
            jax.ShapeDtypeStruct((half, depth), BF16),
            jax.ShapeDtypeStruct((rank, depth), F32),
            jax.ShapeDtypeStruct((3, rank, depth), F32),
        ],
        compiler_params=params(),
        name="project_back",
    )(info, xa, xb, gain, dq, dkv, dkv2, gm, low, w, down, up)


def table_kernel(places, owner, g_ref, *outs):
    _, halves, tens, cuts, _, width = g_ref.shape
    pair = pl.program_id(0)

    @pl.when(pair == 0)
    def _():
        for out in outs:
            out[...] = jnp.zeros_like(out)

    for t in range(tens):
        e = owner[pair * tens + t]
        for out, (sub, start) in zip([outs[n] for n, _, _ in places], [(sub, start) for _, sub, start in places]):
            cols = out.shape[-1]
            step = min(cols, width)
            for c in range(0, cols, step):
                where = start + c
                half, where = where // (cuts * width), where % (cuts * width)
                cut, where = where // width, where % width
                piece = g_ref[0, half, t, cut, :, where : where + step].astype(F32)
                if sub is None:
                    out[e, :, c : c + step] += piece
                else:
                    out[e, sub, :, c : c + step] += piece


def tables(owner, gathered, outs, places):
    dps, tens = gathered.shape[:2]
    gathered = gathered.reshape((dps // 2, 2) + gathered.shape[1:])
    spots, start = [], 0
    for n, sub in places:
        spots.append((n, sub, start))
        start += outs[n][-1]
    block = (1,) + gathered.shape[1:]
    return pl.pallas_call(
        functools.partial(table_kernel, tuple(spots)),
        grid_spec=pltpu.PrefetchScalarGridSpec(
            num_scalar_prefetch=1,
            grid=(dps // 2,),
            in_specs=[pl.BlockSpec(block, lambda p, owner: (p, 0, 0, 0, 0, 0))],
            out_specs=[pl.BlockSpec(shape, lambda p, owner, n=len(shape): (0,) * n) for shape in outs],
        ),
        out_shape=[jax.ShapeDtypeStruct(shape, F32) for shape in outs],
        compiler_params=params(),
        name="tables",
    )(owner, gathered)


def per_device(
    tokens, cotangent, clip_live, adapter_index, gain_one, gain_two, weight_qkv, weight_out, weight_fc1, weight_fc2,
    qkv_down, qkv_up, out_down, out_up, fc1_down, fc1_up, fc2_down, fc2_up,
):
    dps, tens = lax.axis_size("dp"), lax.axis_size("tensor")
    slots = tokens.shape[0]
    axes = ("dp", "tensor")
    dp, t = lax.axis_index("dp"), lax.axis_index("tensor")
    assert slots == 2 and tens == 4 and dps % 2 == 0

    def route(flip):
        perm = []
        for a in range(dps):
            for b in range(tens):
                slot = (b % 2) ^ flip
                perm.append((a * tens + b, (a - a % 2 + b // 2) * tens + 2 * (a % 2) + slot))
        return perm

    routes = [route(0), route(1)]
    swap = [(a * tens + b, (a ^ 1) * tens + b) for a in range(dps) for b in range(tens)]
    back_routes = [[(d, s) for s, d in r] for r in routes]

    def spread(field):
        parts = []
        for flip in range(2):
            slot = (t % 2) ^ flip
            parts.append(lax.ppermute(lax.dynamic_index_in_dim(field, slot, 0, False), axes, routes[flip]))
        return parts

    def unspread(parts):
        got = [lax.ppermute(part, axes, r) for part, r in zip(parts, back_routes)]
        return jnp.where(t % 2 == 0, jnp.stack(got), jnp.stack(got[::-1]))

    codes = lax.all_gather(jnp.stack([adapter_index, clip_live]), "dp")
    owner, alive = codes[:, 0].reshape(-1), codes[:, 1].reshape(-1)
    clip = (dp // 2) * tens + t
    info = jnp.stack([owner[clip], alive[clip]])

    def fold(w, dim):
        k = max(1, 128 // w.shape[dim])
        if k == 1:
            return w
        w = jnp.moveaxis(w.reshape((dps // k, k) + w.shape[1:]), 1, dim)
        return w.reshape(w.shape[:dim] + (-1,) + w.shape[dim + 2 :])

    plan = Plan(dps, tens)
    fine = 8 if dps <= 8 else 2
    w_qkv = weight_qkv.reshape(-1, 16, weight_qkv.shape[2])
    w_qkv = gather(plan, dps, w_qkv, fine, 0).reshape((dps, tens) + weight_qkv.shape)
    w_qkv = fold(w_qkv, 3)
    xa, xb = spread(tokens)
    g1, g2 = gain_one.reshape(1, -1), gain_two.reshape(1, -1)
    q, kv, low = project(info, xa, xb, g1, w_qkv, qkv_down, qkv_up)
    kv2 = lax.ppermute(kv, axes, swap)
    ca, cb = spread(cotangent)
    in_rows = weight_fc1.shape[0]
    parts_1 = weight_fc1.reshape(in_rows, -1, 128).transpose(1, 0, 2)
    parts_2 = weight_fc2.reshape(parts_1.shape[0], -1, weight_fc2.shape[1])
    parts_o = weight_out.reshape(2, -1, weight_out.shape[1])
    ctx, lse, w_out, w_fc1, w_fc2 = attend_gather(plan, dps, q, kv, kv2, parts_o, parts_1, parts_2, fine, 1)
    w_out, w_fc1, w_fc2 = fold(w_out, 4), fold(w_fc1, 3), fold(w_fc2, 4)
    cuts = 2
    la, lb, gm, gctx, g_od, g_ou, g_d1, g_u1, g_d2, g_u2 = feed_forward(
        info, xa, xb, ca, cb, ctx, g2, w_out, w_fc1, w_fc2, out_down, out_up, fc1_down, fc1_up, fc2_down, fc2_up, cuts
    )
    layer_out = unspread([la, lb])

    def pool(pieces):
        flat = jnp.concatenate(pieces, axis=-1).astype(BF16)
        cols = flat.shape[-1] // 2
        mine = lax.dynamic_slice_in_dim(flat, dp % 2 * cols, cols, 1)
        other = lax.dynamic_slice_in_dim(flat, (1 - dp % 2) * cols, cols, 1)
        total = mine.astype(F32) + lax.ppermute(other, axes, swap).astype(F32)
        got = lax.all_gather(total.astype(BF16), axes)
        return got.reshape(dps, tens, 1, flat.shape[0], cols)

    early = pool([g_od, g_ou, g_u1, g_d1, g_u2, g_d2])
    dq, dkv, dkv_far = attend_back(q, kv, kv2, gctx, ctx, lse)
    dkv2 = lax.ppermute(dkv_far, axes, swap)
    dq, dkv2, early, layer_out = lax.optimization_barrier((dq, dkv2, early, layer_out))
    ya, yb, g_qd, g_qu = project_back(info, xa, xb, g1, dq, dkv, dkv2, gm, low, w_qkv, qkv_down, qkv_up)
    late = share(plan, dps, [g_qd, g_qu[0], g_qu[1], g_qu[2]], 2, 2)
    grad_tokens = unspread([ya, yb])
    t_od, t_ou, t_d1, t_u1, t_d2, t_u2 = tables(
        owner, early, [a.shape for a in (out_down, out_up, fc1_down, fc1_up, fc2_down, fc2_up)],
        [(0, None), (1, None), (3, None), (2, None), (5, None), (4, None)],
    )
    t_qd, t_qu = tables(owner, late, [qkv_down.shape, qkv_up.shape], [(0, None), (1, 0), (1, 1), (1, 2)])
    return layer_out, grad_tokens, t_qd, t_qu, t_od, t_ou, t_d1, t_u1, t_d2, t_u2


def solution(mesh):
    rows, whole = P("dp", "tensor", None), P()
    return jax.shard_map(
        per_device,
        mesh=mesh,
        in_specs=(rows, rows, P("dp"), P("dp"), whole, whole, P(None, "dp", "tensor"), P("tensor", "dp"),
                  P("dp", "tensor"), P("tensor", "dp")) + (whole,) * 8,
        out_specs=(rows, rows) + (whole,) * 8,
        check_vma=False,
    )
```

```python
import functools
import math

import jax
import jax.numpy as jnp
from jax import lax
from jax.experimental import pallas as pl
from jax.experimental.pallas import tpu as pltpu
from jax.sharding import PartitionSpec as P

HEAD_DIM = 64
EPS = 1e-06
F32 = jnp.float32
BF16 = jnp.bfloat16
NT = (((1,), (1,)), ((), ()))
TN = (((0,), (0,)), ((), ()))
VMEM_BYTES = 61 << 20
SAFE_SCORE = 60.0


def mm(a, b):
    return jnp.dot(a, b, preferred_element_type=F32)


def mm_nt(a, b):
    return lax.dot_general(a, b, NT, preferred_element_type=F32)


def mm_tn(a, b):
    return lax.dot_general(a, b, TN, preferred_element_type=F32)


def norm_parts(field):
    centered = field - jnp.mean(field, axis=-1, keepdims=True)
    scale = lax.rsqrt(jnp.mean(centered * centered, axis=-1, keepdims=True) + EPS)
    return centered * scale, scale


def norm_back(normed, scale, gain, incoming):
    weighted = incoming * gain
    return scale * (
        weighted
        - jnp.mean(weighted, axis=-1, keepdims=True)
        - normed * jnp.mean(weighted * normed, axis=-1, keepdims=True)
    )


def params(*semantics):
    return pltpu.CompilerParams(vmem_limit_bytes=VMEM_BYTES)


class Plan:
    def __init__(self, dps, tens):
        self.tens = tens
        bits = [1 << i for i in range(1, dps.bit_length() - 1)]
        self.orders = (bits + [1], bits[::-1] + [1])
        self.hops = dps - 1
        self.ways = []
        for order in self.orders:
            blocks = [0]
            for bit in order:
                blocks = blocks + [r | bit for r in blocks]
            tops = {r: max([j for j, bit in enumerate(order) if r & bit], default=-1) for r in blocks}
            sends = {r: range(tops[r] + 1, len(order)) for r in blocks}
            ids = {}
            for r in blocks:
                for j in sends[r]:
                    ids[(r, j)] = len(ids)
            blocks.sort(key=lambda r: bin(r).count("1"))
            self.ways.append((order, blocks, tops, sends, ids))

    def semaphores(self, items):
        dma = lambda *shape: pltpu.SemaphoreType.DMA(shape)
        near = self.tens - 1
        return [dma(items), dma(items, near), dma(items, near), dma(items, self.hops), dma(items, self.hops)]

    def greet(self, extra=()):
        me, t = lax.axis_index("dp"), lax.axis_index("tensor")
        peers = [(me, lax.rem(t + k, self.tens)) for k in range(1, self.tens)]
        peers += [(me ^ bit, t) for bit in self.orders[0]]
        peers += list(extra)
        barrier = pltpu.get_barrier_semaphore()
        for peer in peers:
            pl.semaphore_signal(barrier, inc=1, device_id=peer, device_id_type=pl.DeviceIdType.MESH)
        pl.semaphore_wait(barrier, len(peers))


class Item:
    def __init__(self, plan, sems, number, src, spot, order):
        self.plan, self.src, self.spot = plan, src, spot
        self.local, self.zs, self.zr, self.ss, self.rs = [s.at[number] for s in sems]
        self.order, self.blocks, self.tops, self.sends, self.ids = plan.ways[order]
        self.me, self.t = lax.axis_index("dp"), lax.axis_index("tensor")
        self.stages = [r for r in self.blocks if len(self.sends[r])]

    def keep(self):
        return pltpu.make_async_copy(self.src, self.spot(self.me, self.t), self.local)

    def along(self, d, arriving=False):
        n = self.plan.tens
        return pltpu.make_async_remote_copy(
            src_ref=self.src,
            dst_ref=self.spot(self.me, lax.rem(self.t + n - d, n) if arriving else self.t),
            send_sem=self.zs.at[d - 1],
            recv_sem=self.zr.at[d - 1],
            device_id=(self.me, lax.rem(self.t + d, n)),
            device_id_type=pl.DeviceIdType.MESH,
        )

    def across(self, r, j, arriving=False):
        bit, n = self.order[j], self.ids[(r, j)]
        block = self.me ^ r
        return pltpu.make_async_remote_copy(
            src_ref=self.spot(block, None),
            dst_ref=self.spot(block ^ bit if arriving else block, None),
            send_sem=self.ss.at[n],
            recv_sem=self.rs.at[n],
            device_id=(self.me ^ bit, self.t),
            device_id_type=pl.DeviceIdType.MESH,
        )

    def start(self):
        self.keep().start()
        for d in range(1, self.plan.tens):
            self.along(d).start()

    def arrived(self, r):
        if r == 0:
            self.keep().wait()
            for d in range(1, self.plan.tens):
                self.along(d, True).wait_recv()
        else:
            j = self.tops[r]
            self.across(r ^ self.order[j], j, True).wait_recv()

    def advance(self, stage):
        r = self.stages[stage]
        self.arrived(r)
        for j in self.sends[r]:
            self.across(r, j).start()

    def finish(self):
        for r in self.blocks:
            if not len(self.sends[r]):
                self.arrived(r)
        for d in range(1, self.plan.tens):
            self.along(d).wait_send()
        for r in self.blocks:
            for j in self.sends[r]:
                self.across(r, j).wait_send()


def schedule(items):
    pairs = [items[k : k + 2] for k in range(0, len(items), 2)]
    stages = len(items[0].stages)

    def step(s):
        for item in pairs[s : s + 1]:
            for one in item:
                one.start()
        for n, pair in enumerate(pairs):
            if 0 <= s - 1 - n < stages:
                for one in pair:
                    one.advance(s - 1 - n)

    def close():
        for item in items:
            item.finish()

    return [functools.partial(step, s) for s in range(len(pairs) + stages)] + [close]


class Route:
    def __init__(self, out, local, send, recv):
        self.out, self.local, self.send, self.recv = out, local, send, recv
        me, t = lax.axis_index("dp"), lax.axis_index("tensor")
        self.me, self.t = me, t
        core, high, low = lax.rem(me, 2), t // 2, lax.rem(t, 2)
        self.stays = core == high
        base = me - core
        self.peers = [(me ^ 1, t ^ 2), (base + high, 2 * core + 1 - low)]
        self.low = low

    def copy(self, f, src, out, arriving=False):
        if self.out:
            src, slot = src.at[self.low ^ f], f
        else:
            src, slot = src[f], self.low ^ f if arriving else self.low
        return pltpu.make_async_remote_copy(
            src_ref=src, dst_ref=out.at[slot], send_sem=self.send.at[f], recv_sem=self.recv.at[f],
            device_id=self.peers[f], device_id_type=pl.DeviceIdType.MESH,
        )

    def stay(self, blocks, out):
        if self.out:
            return pltpu.make_async_copy(blocks.at[self.low], out.at[0], self.local)
        return pltpu.make_async_copy(blocks[0], out.at[self.low], self.local)

    def start(self, blocks, out):
        self.copy(1, blocks, out).start()

        @pl.when(self.stays)
        def _():
            self.stay(blocks, out).start()

        @pl.when(jnp.logical_not(self.stays))
        def _():
            self.copy(0, blocks, out).start()

    def wait(self, blocks, out):
        @pl.when(self.stays)
        def _():
            self.stay(blocks, out).wait()

        @pl.when(jnp.logical_not(self.stays))
        def _():
            self.copy(0, blocks, out, True).wait_recv()
            self.copy(0, blocks, out).wait_send()

        self.copy(1, blocks, out, True).wait_recv()
        self.copy(1, blocks, out).wait_send()

    @staticmethod
    def semaphores():
        return [pltpu.SemaphoreType.DMA, pltpu.SemaphoreType.DMA((2,)), pltpu.SemaphoreType.DMA((2,))]


def at(ref, cut):
    return lambda a, t: ref.at[a, :, cut] if t is None else ref.at[a, t, cut]


class Pool:
    def __init__(self, plan, x_ref, o_ref, got, src, swap_send, swap_recv, *sems):
        me, t = lax.axis_index("dp"), lax.axis_index("tensor")
        self.mine = lax.rem(me, 2)
        self.x_ref, self.got, self.src = x_ref, got, src
        self.swap = pltpu.make_async_remote_copy(
            src_ref=x_ref.at[1 - self.mine], dst_ref=got, send_sem=swap_send, recv_sem=swap_recv,
            device_id=(me ^ 1, t), device_id_type=pl.DeviceIdType.MESH,
        )
        cuts = src.shape[0]
        self.items = [Item(plan, sems, k, src.at[pl.ds(k, 1)], at(o_ref, pl.ds(k, 1)), k % 2) for k in range(cuts)]
        steps = schedule(self.items)
        self.steps = [self.swap.start, functools.partial(self.add, steps[0])] + steps[1:]

    def add(self, then):
        self.swap.wait()
        self.src[...] = (self.x_ref[self.mine].astype(F32) + self.got[...].astype(F32)).astype(BF16)
        then()

    @staticmethod
    def scratch(plan, shape):
        return [pltpu.VMEM(shape, BF16), pltpu.VMEM(shape, BF16), pltpu.SemaphoreType.DMA, pltpu.SemaphoreType.DMA
                ] + plan.semaphores(shape[0])


def share_kernel(plan, x_ref, o_ref, *scratch):
    plan.greet()
    for step in Pool(plan, x_ref, o_ref, *scratch).steps:
        step()


def share(plan, dps, x, number):
    return pl.pallas_call(
        functools.partial(share_kernel, plan),
        in_specs=[pl.BlockSpec(memory_space=pltpu.VMEM)],
        out_specs=pl.BlockSpec(memory_space=pl.ANY),
        out_shape=jax.ShapeDtypeStruct((dps, plan.tens) + x.shape[1:], BF16),
        scratch_shapes=Pool.scratch(plan, x.shape[1:]),
        compiler_params=pltpu.CompilerParams(collective_id=number, has_side_effects=True),
        name="share",
    )(x)


def intro_kernel(
    plan, info, tok_ref, codes_ref, gain_ref, w_ref, wo_ref, w1_ref, w2_ref, down_ref, up_ref,
    x_ref, q_ref, kv_ref, kv2_ref, low_ref, codes_out, w_out, wo_out, w1_out, w2_out,
    x_s, w_s, n_s, kv_s, keep_sem, kv_send, kv_recv, r_local, r_send, r_recv, *sems,
):
    half, depth = x_ref.shape[1:]
    tens, width = plan.tens, w_ref.shape[2]
    me, t = lax.axis_index("dp"), lax.axis_index("tensor")
    sems_w, sems = sems[:5], sems[5:]
    cuts = sems_w[0].shape[0]
    size = w_ref.shape[0] // cuts
    first = [Item(plan, sems_w, k, w_ref.at[pl.ds(k * size, size)], at(w_s, pl.ds(k * size, size)), k % 2) for k in range(cuts)]
    rest = []
    for pairs in (((codes_ref, codes_out),), ((wo_ref, wo_out),), ((w1_ref, w1_out), (w2_ref, w2_out))):
        for k in range(pairs[0][0].shape[0]):
            for src, out in pairs:
                rest.append((src.at[pl.ds(k, 1)], at(out, pl.ds(k, 1))))
    rest = rest[1:] + rest[:1]
    rest = [Item(plan, sems, n, src, spot, n % 2) for n, (src, spot) in enumerate(rest)]
    later = schedule(rest)
    route = Route(True, r_local, r_send, r_recv)
    e = info[0]

    plan.greet(route.peers)
    for item in first:
        item.start()
    route.start(tok_ref, x_s)
    stages = len(first[0].stages)
    for s in range(cuts // 2 + stages - 1):
        for n in range(cuts // 2):
            if 0 <= s - n < stages:
                first[2 * n].advance(s - n)
                first[2 * n + 1].advance(s - n)
    route.wait(tok_ref, x_s)
    later[0]()
    x_ref[...] = x_s[...]
    for part in range(2):
        normed, _ = norm_parts(x_s[part].astype(F32))
        n_s[part * half : (part + 1) * half, :] = normed * gain_ref[...]
    n = n_s[...].astype(BF16)
    low = mm_nt(n, down_ref[e])
    low_ref[...] = low
    low = low.astype(BF16)
    for item in first:
        item.finish()
    keep = pltpu.make_async_copy(w_s, w_out, keep_sem)
    keep.start()
    swap = pltpu.make_async_remote_copy(
        src_ref=kv_s, dst_ref=kv2_ref, send_sem=kv_send, recv_sem=kv_recv,
        device_id=(me ^ 1, t), device_id_type=pl.DeviceIdType.MESH,
    )
    blocks = w_ref.shape[0] // 3
    for turn, j in enumerate((1, 2, 0)):
        later[turn + 1]()
        for c in range(tens):
            cols = slice(c * width, (c + 1) * width)
            w = w_s[:, c, j * blocks : (j + 1) * blocks].reshape(depth, width)
            res = (mm(n, w) + mm(low, up_ref[e, j, :, cols])).astype(BF16)
            if j == 0:
                q_ref[:, cols] = res
            else:
                kv_s[j - 1, :, cols] = res
        if j == 2:
            swap.start()
            kv_ref[...] = kv_s[...]
    for one in later[4:]:
        one()
    swap.wait()
    keep.wait()


def intro(plan, dps, info, tokens, codes, gain, w, wo, w1, w2, down, up, cuts, number):
    _, half, depth = tokens.shape
    rows, rank = 2 * half, down.shape[1]
    hbm, vm = pl.BlockSpec(memory_space=pl.ANY), pl.BlockSpec(memory_space=pltpu.VMEM)
    big = lambda x: jax.ShapeDtypeStruct((dps, plan.tens) + x.shape, x.dtype)
    items = codes.shape[0] + wo.shape[0] + 2 * w1.shape[0]
    return pl.pallas_call(
        functools.partial(intro_kernel, plan),
        in_specs=[pl.BlockSpec(memory_space=pltpu.SMEM), hbm, hbm, vm, hbm, hbm, hbm, hbm, vm, vm],
        out_specs=[vm, vm, vm, hbm, vm] + [hbm] * 5,
        out_shape=[
            jax.ShapeDtypeStruct(tokens.shape, BF16),
            jax.ShapeDtypeStruct((rows, depth), BF16),
            jax.ShapeDtypeStruct((2, rows, depth), BF16),
            jax.ShapeDtypeStruct((2, rows, depth), BF16),
            jax.ShapeDtypeStruct((rows, rank), F32),
            big(codes), big(w), big(wo), big(w1), big(w2),
        ],
        scratch_shapes=[
            pltpu.VMEM(tokens.shape, BF16), pltpu.VMEM((dps, plan.tens) + w.shape, BF16), pltpu.VMEM((rows, depth), F32),
            pltpu.VMEM((2, rows, depth), BF16),
        ]
        + [pltpu.SemaphoreType.DMA] * 3
        + Route.semaphores() + plan.semaphores(cuts) + plan.semaphores(items),
        compiler_params=pltpu.CompilerParams(
            vmem_limit_bytes=VMEM_BYTES, collective_id=number, has_side_effects=True
        ),
        name="intro",
    )(info, tokens, codes, gain, w, wo, w1, w2, down, up)


def attend_pair(q2, ks, vs, shifted):
    lane = lax.broadcasted_iota(jnp.int32, (1, 128), 1)
    outs, lses = [], []
    for h in range(2):
        mine = (lane // HEAD_DIM) == h
        s = mm_nt(jnp.where(mine, q2, BF16(0)), ks[...])
        if shifted:
            m = jnp.max(s, axis=1, keepdims=True)
            p = jnp.exp(s - m).astype(BF16)
        else:
            p = jnp.exp(s).astype(BF16)
        o = mm(p, vs[h])
        total = pltpu.roll(o, HEAD_DIM, 1)
        outs.append(o / total)
        lse = jnp.log(jnp.where(mine, total, o))
        lses.append(lse + m if shifted else lse)
    return (
        jnp.where(lane < HEAD_DIM, outs[0], outs[1]).astype(BF16),
        jnp.where(lane < HEAD_DIM, lses[0], lses[1]),
    )


def stage_keys(k_ref, v_ref, k2_ref, v2_ref, ks, vs):
    rows = k_ref.shape[1]
    lane = lax.broadcasted_iota(jnp.int32, (1, 128), 1)
    ks[0:rows, :] = k_ref[0]
    ks[rows:, :] = k2_ref[0]
    for h in range(2):
        mine = (lane // HEAD_DIM) == h
        vs[h, 0:rows, :] = jnp.where(mine, v_ref[0], BF16(1))
        vs[h, rows:, :] = jnp.where(mine, v2_ref[0], BF16(1))


def attend_kernel(q_ref, k_ref, v_ref, k2_ref, v2_ref, o_ref, lse_ref, ks, vs):
    stage_keys(k_ref, v_ref, k2_ref, v2_ref, ks, vs)
    q2 = q_ref[...] * BF16(HEAD_DIM ** -0.5)
    lane = lax.broadcasted_iota(jnp.int32, (1, 128), 1)
    qf, kf = q2.astype(F32), ks[...].astype(F32)
    safe = True
    for h in range(2):
        mine = (lane // HEAD_DIM) == h
        far = lambda x: jnp.max(jnp.sum(jnp.where(mine, x * x, 0.0), axis=1, keepdims=True))
        safe = jnp.logical_and(safe, far(qf) * far(kf) <= SAFE_SCORE * SAFE_SCORE)

    @pl.when(safe)
    def _():
        o_ref[...], lse_ref[...] = attend_pair(q2, ks, vs, False)

    @pl.when(jnp.logical_not(safe))
    def _():
        o_ref[...], lse_ref[...] = attend_pair(q2, ks, vs, True)


def attend(q, kv, kv2):
    rows, depth = q.shape
    flat = pl.BlockSpec((rows, 128), lambda i: (0, i))
    part = lambda j: pl.BlockSpec((1, rows, 128), lambda i: (j, 0, i))
    return pl.pallas_call(
        attend_kernel,
        grid=(depth // 128,),
        in_specs=[flat, part(0), part(1), part(0), part(1)],
        out_specs=[flat, flat],
        out_shape=[jax.ShapeDtypeStruct((rows, depth), BF16), jax.ShapeDtypeStruct((rows, depth), F32)],
        scratch_shapes=[pltpu.VMEM((2 * rows, 128), BF16), pltpu.VMEM((2, 2 * rows, 128), BF16)],
        compiler_params=params(),
        name="attend",
    )(q, kv, kv, kv2, kv2)


def gelu_both(x):
    cdf = 0.5 * (1.0 + lax.erf(x * (2.0 ** -0.5)))
    pdf = jnp.exp(-0.5 * x * x) * ((2.0 * math.pi) ** -0.5)
    return x * cdf, cdf + x * pdf


def feed_kernel(
    plan, info, xa_ref, xb_ref, ca_ref, cb_ref, ctx_ref, gain_ref, wo_ref, w1_ref, w2_ref, w1_src, w2_src,
    od_ref, ou_ref, d1_ref, u1_ref, d2_ref, u2_ref,
    la_ref, lb_ref, gm_ref, gctx_ref, grads_ref,
    wo_s, w1_s, w2_s, mid_s, n_s, gf_s, feed_s, gn_s, lowo_s, low1_s, low2_s, b1_s, b2_s, *late,
):
    half, depth = xa_ref.shape
    rows = 2 * half
    step, last = pl.program_id(0), pl.num_programs(0) - 1
    e, live = info[0], info[1].astype(F32)
    dp, tens, wop, wor, woc = wo_ref.shape
    fp, fr, fc = w1_ref.shape[2:]
    wide = fp * fc
    if late:
        w1_late, w2_late, *sems = late
        items = []
        for k in range(w1_src.shape[0]):
            for src, out in ((w1_src, w1_late), (w2_src, w2_late)):
                cut = pl.ds(k, 1)
                items.append(Item(plan, sems, len(items), src.at[cut], at(out, cut), len(items) % 2))
        steps = schedule(items)
        before = {0: 0, 2: 1, 3: 2, 4: 3, 5: 4, 6: 5, 7: 6}

    def put(unit, cols, value):
        per = grads_ref.shape[3] // depth
        cuts = grads_ref.shape[1]
        spot = (unit % per) * depth + cols
        if not isinstance(spot, int):
            spot = pl.multiple_of(spot, 128)
        grads_ref[unit // (per * cuts), unit // per % cuts, :, pl.ds(spot, value.shape[1])] = value.astype(BF16)

    if late:
        pl.when(step == 0)(plan.greet)
        for n, when in before.items():
            pl.when(step == when)(steps[n])
        for n in range(len(items) // 2):
            @pl.when(step == tens + n)
            def _():
                items[2 * n].finish()
                items[2 * n + 1].finish()

    @pl.when(step == 0)
    def _():
        for a in range(dp):
            for t in range(tens):
                for k in range(wop):
                    row = (t * wop + k) * wor
                    wo_s[row : row + wor, a * woc : (a + 1) * woc] = wo_ref[a, t, k]
        ctx = ctx_ref[...]
        low = mm_nt(ctx, od_ref[e])
        lowo_s[...] = low
        attention = mm(ctx, wo_s[...]) + mm(low.astype(BF16), ou_ref[e])
        for part, ref in enumerate((xa_ref, xb_ref)):
            s = slice(part * half, (part + 1) * half)
            mid_s[s, :] = ref[...].astype(F32) + attention[s, :]
        for part, ref in enumerate((ca_ref, cb_ref)):
            s = slice(part * half, (part + 1) * half)
            gm_ref[s, :] = ref[...].astype(F32) * live
        gf_s[...] = gm_ref[...].astype(BF16)
        normed, _ = norm_parts(mid_s[...])
        n_s[...] = (normed * gain_ref[...]).astype(BF16)
        low1_s[...] = mm_nt(n_s[...], d1_ref[e])
        b2_s[...] = mm_nt(gf_s[...], u2_ref[e])
        feed_s[...] = jnp.zeros_like(feed_s)
        gn_s[...] = jnp.zeros_like(gn_s)
        low2_s[...] = jnp.zeros_like(low2_s)
        b1_s[...] = jnp.zeros_like(b1_s)

    def stage(take_1, take_2):
        for a in range(dp):
            for k in range(fp):
                w1_s[a * fr : (a + 1) * fr, k * fc : (k + 1) * fc] = take_1(a, k)
                w2_s[k * fr : (k + 1) * fr, a * woc : (a + 1) * woc] = take_2(a, k)

    if late:
        @pl.when(step < tens)
        def _():
            stage(lambda a, k: w1_ref[a, 0, k], lambda a, k: w2_ref[a, 0, k])

        @pl.when(step >= tens)
        def _():
            part = step - tens
            stage(lambda a, k: w1_late[a, k, part], lambda a, k: w2_late[a, k, part])
    else:
        stage(lambda a, k: w1_ref[a, 0, k], lambda a, k: w2_ref[a, 0, k])

    w1, w2 = w1_s[...], w2_s[...]
    if late:
        early_step = step < tens
        runs = [
            pl.multiple_of(jnp.where(early_step, step * 2 * wide + k * fc, (2 * k + 1) * wide + (step - tens) * fc), fc)
            for k in range(fp)
        ]
        u1 = jnp.concatenate([u1_ref[e, :, pl.ds(run, fc)] for run in runs], axis=1)
        d2 = jnp.concatenate([d2_ref[e, :, pl.ds(run, fc)] for run in runs], axis=1)
    else:
        u1, d2 = u1_ref[e], d2_ref[e]
    n, gf = n_s[...], gf_s[...]
    low1, b2 = low1_s[...].astype(BF16), b2_s[...].astype(BF16)
    preact = mm(n, w1) + mm(low1, u1)
    ghid = mm_nt(gf, w2) + mm(b2, d2)
    if late:
        pl.when(step == 0)(steps[1])
    hid, slope = gelu_both(preact)
    hid = hid.astype(BF16)
    gpre = (ghid * slope).astype(BF16)
    feed_s[...] += mm(hid, w2)
    gn_s[...] += mm_nt(gpre, w1)
    low2_s[...] += mm_nt(hid, d2)
    b1_s[...] += mm_nt(gpre, u1)
    gu1, gd2 = mm_tn(low1, gpre), mm_tn(b2, hid)
    if late:
        for k, run in enumerate(runs):
            cols = slice(k * fc, (k + 1) * fc)
            put(4 + run // depth, lax.rem(run, depth), gu1[:, cols])
            put(4 + tens + run // depth, lax.rem(run, depth), gd2[:, cols])
    else:
        t, part = lax.rem(step, tens), step // tens
        put(4 + t, part * wide, gu1)
        put(4 + tens + t, part * wide, gd2)

    @pl.when(step == last)
    def _():
        low2, b1 = low2_s[...].astype(BF16), b1_s[...].astype(BF16)
        out = live * (mid_s[...] + feed_s[...] + mm(low2, u2_ref[e]))
        la_ref[...] = out[:half].astype(BF16)
        lb_ref[...] = out[half:].astype(BF16)
        put(3, 0, mm_tn(low2, gf_s[...]))
        gn = gn_s[...] + mm(b1, d1_ref[e])
        normed, scale = norm_parts(mid_s[...])
        put(2, 0, mm_tn(b1, n_s[...]))
        gm = gm_ref[...] + norm_back(normed, scale, gain_ref[...], gn)
        gm_ref[...] = gm
        ga = gm.astype(BF16)
        back = mm_nt(ga, ou_ref[e]).astype(BF16)
        gctx_ref[...] = (mm_nt(ga, wo_s[...]) + mm(back, od_ref[e])).astype(BF16)
        put(0, 0, mm_tn(back, ctx_ref[...]))
        put(1, 0, mm_tn(lowo_s[...].astype(BF16), ga))


def feed_forward(plan, info, xa, xb, ca, cb, ctx, gain, wo, w1, w2, late, od, ou, d1, u1, d2, u2, number):
    half, depth = xa.shape
    rows = 2 * half
    adapters, rank = od.shape[:2]
    dp, tens, wop, wor, woc = wo.shape
    fp, fr, fc = w1.shape[2:]
    fp = fp if late else fp // 2
    wide = fp * fc
    ff = 2 * wide * tens
    once = lambda *shape: pl.BlockSpec(shape, lambda f: (0,) * len(shape), pipeline_mode=pl.Buffered(1))
    whole = lambda *shape: pl.BlockSpec(shape, lambda f: (0,) * len(shape))
    table = once(adapters, rank, depth)
    if late:
        assert late[0].shape[0] == tens == fp
        table_f = once(adapters, rank, ff)
    else:
        table_f = pl.BlockSpec((adapters, rank, wide), lambda f: (0, 0, f % tens * 2 + f // tens))
    if late:
        place = lambda f: (0, jnp.minimum(f, tens - 1), 0, 0, 0)
    else:
        place = lambda f: (0, f % tens, f // tens, 0, 0)
    units = 4 + 2 * ff // depth
    cuts = 2
    hbm = pl.BlockSpec(memory_space=pl.ANY)
    scratch = [
        pltpu.VMEM((depth, depth), BF16),
        pltpu.VMEM((depth, wide), BF16),
        pltpu.VMEM((wide, depth), BF16),
        pltpu.VMEM((rows, depth), F32),
        pltpu.VMEM((rows, depth), BF16),
        pltpu.VMEM((rows, depth), BF16),
        pltpu.VMEM((rows, depth), F32),
        pltpu.VMEM((rows, depth), F32),
    ] + [pltpu.VMEM((rows, rank), F32)] * 5
    extra = {}
    if late:
        scratch += [pltpu.VMEM((dp, tens) + part.shape, BF16) for part in late]
        scratch += plan.semaphores(2 * late[0].shape[0])
        extra = dict(collective_id=number, has_side_effects=True)
    else:
        late = [jnp.zeros((16, 128), BF16)] * 2
    return pl.pallas_call(
        functools.partial(feed_kernel, plan),
        grid=(2 * tens,),
        in_specs=[
            pl.BlockSpec(memory_space=pltpu.SMEM),
            once(half, depth), once(half, depth), once(half, depth), once(half, depth),
            once(rows, depth),
            whole(1, depth),
            once(dp, tens, wop, wor, woc),
            pl.BlockSpec((dp, 1, fp, fr, fc), place),
            pl.BlockSpec((dp, 1, fp, fr, woc), place),
            hbm, hbm,
            table, table, table, table_f, table_f, table,
        ],
        out_specs=[
            whole(half, depth), whole(half, depth), whole(rows, depth), whole(rows, depth),
            whole(2, cuts, rank, units * depth // (2 * cuts)),
        ],
        scratch_shapes=scratch,
        out_shape=[
            jax.ShapeDtypeStruct((half, depth), BF16),
            jax.ShapeDtypeStruct((half, depth), BF16),
            jax.ShapeDtypeStruct((rows, depth), F32),
            jax.ShapeDtypeStruct((rows, depth), BF16),
            jax.ShapeDtypeStruct((2, cuts, rank, units * depth // (2 * cuts)), BF16),
        ],
        compiler_params=pltpu.CompilerParams(vmem_limit_bytes=VMEM_BYTES, **extra),
        name="feed_forward",
    )(info, xa, xb, ca, cb, ctx, gain, wo, w1, w2, late[0], late[1], od, ou, d1, u1, d2, u2)


def split3(x):
    hi = x.astype(BF16)
    rest = x - hi.astype(F32)
    mid = rest.astype(BF16)
    return hi, mid, (rest - mid.astype(F32)).astype(BF16)


def attend_back_kernel(
    plan, q_ref, k_ref, v_ref, k2_ref, v2_ref, g_ref, o_ref, lse_ref, la_ref, lb_ref, grads_ref,
    dq_ref, dkv_ref, far_ref, lo_ref, early_ref,
    ks, vs, kd, acc, far_s, far_send, far_recv, lo_local, lo_send, lo_recv, *pool,
):
    rows = q_ref.shape[0]
    step, steps = pl.program_id(0), pl.num_programs(0)
    me, t = lax.axis_index("dp"), lax.axis_index("tensor")
    route = Route(False, lo_local, lo_send, lo_recv)
    early = Pool(plan, grads_ref, early_ref, *pool).steps
    blocks = (la_ref, lb_ref)

    @pl.when(step == 0)
    def _():
        plan.greet(route.peers)

    for n, one in zip((0, 1, 3, 5, 6, 7), early[:-1]):
        @pl.when(step == n)
        def _():
            one()

    @pl.when(step == 3)
    def _():
        route.start(blocks, lo_ref)

    def far(n):
        return pltpu.make_async_remote_copy(
            src_ref=far_s.at[lax.rem(n, 2)],
            dst_ref=far_ref.at[:, :, pl.ds(pl.multiple_of(n * 128, 128), 128)],
            send_sem=far_send.at[n], recv_sem=far_recv.at[n],
            device_id=(me ^ 1, t), device_id_type=pl.DeviceIdType.MESH,
        )

    zero = BF16(0)
    lane = lax.broadcasted_iota(jnp.int32, (1, 128), 1)
    scale = BF16(HEAD_DIM ** -0.5)
    q2 = q_ref[...] * scale
    g2 = g_ref[...]
    hi, mid, lo = split3(pltpu.roll(lse_ref[...], HEAD_DIM, 1))
    prod = g2.astype(F32) * o_ref[...].astype(F32)
    qa, ga, qm, gm = [], [], [], []
    for h in range(2):
        mine, b = (lane // HEAD_DIM) == h, HEAD_DIM * (1 - h)
        qa.append(
            jnp.where(mine, q2, jnp.where(lane == b, -hi, jnp.where(lane == b + 1, -mid, jnp.where(lane == b + 2, -lo, zero))))
        )
        dh, dm, dl = split3(jnp.sum(jnp.where(mine, prod, 0.0), axis=1, keepdims=True))
        ga.append(
            jnp.where(mine, g2, jnp.where(lane == b, -dh, jnp.where(lane == b + 1, -dm, jnp.where(lane == b + 2, -dl, zero))))
        )
        qm.append(jnp.where(mine, q2, zero))
        gm.append(jnp.where(mine, g2, zero))
        ones = ((lane >= b) & (lane < b + 3)).astype(BF16)
        for i, (kr, vr) in enumerate(((k_ref, v_ref), (k2_ref, v2_ref))):
            s = slice(i * rows, (i + 1) * rows)
            ks[h, s, :] = jnp.where(mine, kr[0], ones)
            vs[h, s, :] = jnp.where(mine, vr[0], ones)
            kd[h, s, :] = jnp.where(mine, kr[0] * scale, zero)
    @pl.when(step >= 2)
    def _():
        far(step - 2).wait_send()

    slot = lax.rem(step, 2)
    for i in range(2):
        s = slice((1 - i) * rows, (2 - i) * rows)
        dk = jnp.zeros((rows, 128), F32)
        dv = jnp.zeros((rows, 128), F32)
        dq = jnp.zeros((rows, 128), F32)
        for h in range(2):
            p = jnp.exp(mm_nt(ks[h, s, :], qa[h]))
            ds = (p * mm_nt(vs[h, s, :], ga[h])).astype(BF16)
            dv = dv + mm(p.astype(BF16), gm[h])
            dk = dk + mm(ds, qm[h])
            dq = dq + mm_tn(ds, kd[h, s, :])
        if i == 0:
            far_s[slot, 0] = dk.astype(BF16)
            far_s[slot, 1] = dv.astype(BF16)
            far(step).start()
            acc[...] = dq
        else:
            dkv_ref[0] = dk.astype(BF16)
            dkv_ref[1] = dv.astype(BF16)
            dq_ref[...] = (acc[...] + dq).astype(BF16)

    @pl.when(step == steps - 1)
    def _():
        early[-1]()
        route.wait(blocks, lo_ref)
        far(step - 1).wait_send()
        far(step).wait_send()
        lax.fori_loop(0, steps, lambda n, c: (far(n).wait_recv(), c)[1], 0)


def attend_back(plan, dps, q, kv, kv2, g, ctx, lse, la, lb, grads, number):
    rows, depth = q.shape
    flat = pl.BlockSpec((rows, 128), lambda i: (0, i))
    part = lambda j: pl.BlockSpec((1, rows, 128), lambda i: (j, 0, i))
    both = pl.BlockSpec((2, rows, 128), lambda i: (0, 0, i))
    hbm = pl.BlockSpec(memory_space=pl.ANY)
    heads = depth // 128
    dma = lambda *shape: pltpu.SemaphoreType.DMA(shape)
    return pl.pallas_call(
        functools.partial(attend_back_kernel, plan),
        grid=(heads,),
        in_specs=[flat, part(0), part(1), part(0), part(1), flat, flat, flat, hbm, hbm,
                  pl.BlockSpec(grads.shape, lambda i: (0, 0, 0, 0), pipeline_mode=pl.Buffered(1))],
        out_specs=[flat, both, hbm, hbm, hbm],
        out_shape=[
            jax.ShapeDtypeStruct((rows, depth), BF16),
            jax.ShapeDtypeStruct((2, rows, depth), BF16),
            jax.ShapeDtypeStruct((2, rows, depth), BF16),
            jax.ShapeDtypeStruct((2,) + la.shape, BF16),
            jax.ShapeDtypeStruct((dps, plan.tens) + grads.shape[1:], BF16),
        ],
        scratch_shapes=[pltpu.VMEM((2, 2 * rows, 128), BF16)] * 3
        + [pltpu.VMEM((rows, 128), F32), pltpu.VMEM((2, 2, rows, 128), BF16), dma(heads), dma(heads),
           *Route.semaphores()]
        + Pool.scratch(plan, grads.shape[1:]),
        compiler_params=pltpu.CompilerParams(
            vmem_limit_bytes=VMEM_BYTES, collective_id=number, has_side_effects=True
        ),
        name="attend_back",
    )(q, kv, kv, kv2, kv2, g, ctx, lse, la, lb, grads)


def qkv_back_kernel(
    info, xa_ref, xb_ref, gain_ref, dq_ref, dkv_ref, dkv2_ref, gm_ref, low_ref, w_ref, down_ref, up_ref,
    ya_ref, yb_ref, g_down, g_up, gn_s, back_s,
):
    half, depth = xa_ref.shape
    parts, width = w_ref.shape[1], w_ref.shape[4]
    step, last = pl.program_id(0), pl.num_programs(0) - 1

    def go(g, first):
        back = mm_nt(g, up_ref[0, 0])
        total = back if first else back_s[...] + back
        back_s[...] = total
        acc = None if first else gn_s[...]
        for part in range(parts):
            cols = slice(part * width, (part + 1) * width)
            term = mm_nt(g[:, cols], w_ref[:, part, 0].reshape(depth, width))
            acc = term if acc is None else acc + term
        gn_s[...] = acc
        g_up[0] = mm_tn(low_ref[...].astype(BF16), g)

    @pl.when(step == 0)
    def _():
        go(dq_ref[...], True)

    @pl.when(step > 0)
    def _():
        go((dkv_ref[0].astype(F32) + dkv2_ref[0].astype(F32)).astype(BF16), False)

    @pl.when(step == last)
    def _():
        back = back_s[...].astype(BF16)
        gn_s[...] += mm(back, down_ref[0])
        total = jnp.zeros(g_down.shape, F32)
        for part, (x_ref, y_ref) in enumerate(((xa_ref, ya_ref), (xb_ref, yb_ref))):
            s = slice(part * half, (part + 1) * half)
            normed, scale = norm_parts(x_ref[...].astype(F32))
            total = total + mm_tn(back_s[s, :].astype(BF16), (normed * gain_ref[...]).astype(BF16))
            y_ref[...] = (gm_ref[s, :] + norm_back(normed, scale, gain_ref[...], gn_s[s, :])).astype(BF16)
        g_down[...] = total


def project_back(info, xa, xb, gain, dq, dkv, dkv2, gm, low, w, down, up):
    half, depth = xa.shape
    rows = 2 * half
    rank = down.shape[1]
    dp, tens, _, wr, wc = w.shape
    whole = lambda *shape: pl.BlockSpec(shape, lambda j, info: (0,) * len(shape))
    once = lambda *shape: pl.BlockSpec(shape, lambda j, info: (0,) * len(shape), pipeline_mode=pl.Buffered(1))
    pair = pl.BlockSpec((1, rows, depth), lambda j, info: (jnp.maximum(j - 1, 0), 0, 0))
    return pl.pallas_call(
        qkv_back_kernel,
        grid_spec=pltpu.PrefetchScalarGridSpec(
            num_scalar_prefetch=1,
            grid=(3,),
            in_specs=[
                once(half, depth), once(half, depth), whole(1, depth),
                once(rows, depth), pair, pair,
                once(rows, depth), once(rows, rank),
                pl.BlockSpec((dp, tens, 1, wr, wc), lambda j, info: (0, 0, j, 0, 0)),
                pl.BlockSpec((1, rank, depth), lambda j, info: (info[0], 0, 0)),
                pl.BlockSpec((1, 1, rank, depth), lambda j, info: (info[0], j, 0, 0)),
            ],
            out_specs=[
                whole(half, depth), whole(half, depth), whole(rank, depth),
                pl.BlockSpec((1, rank, depth), lambda j, info: (j, 0, 0)),
            ],
            scratch_shapes=[pltpu.VMEM((rows, depth), F32), pltpu.VMEM((rows, rank), F32)],
        ),
        out_shape=[
            jax.ShapeDtypeStruct((half, depth), BF16),
            jax.ShapeDtypeStruct((half, depth), BF16),
            jax.ShapeDtypeStruct((rank, depth), F32),
            jax.ShapeDtypeStruct((3, rank, depth), F32),
        ],
        compiler_params=params(),
        name="project_back",
    )(info, xa, xb, gain, dq, dkv, dkv2, gm, low, w, down, up)


def table_kernel(places, unit, owner, g_ref, *outs):
    _, _, tens, cuts, _, width = g_ref.shape
    pair, per = pl.program_id(0), width // unit

    @pl.when(pair == 0)
    def _():
        for out in outs:
            out[...] = jnp.zeros_like(out)

    for t in range(tens):
        e = owner[pair * tens + t]
        for n, (out, sub, start) in enumerate(places):
            col = n % per * unit
            piece = g_ref[0, n // (per * cuts), t, n // per % cuts, :, col : col + unit].astype(F32)
            if sub is None:
                outs[out][e, :, start : start + unit] += piece
            else:
                outs[out][e, sub, :, start : start + unit] += piece


def tables(owner, gathered, outs, places, unit):
    dps = gathered.shape[0]
    gathered = gathered.reshape((dps // 2, 2) + gathered.shape[1:])
    block = (1,) + gathered.shape[1:]
    return pl.pallas_call(
        functools.partial(table_kernel, places, unit),
        grid_spec=pltpu.PrefetchScalarGridSpec(
            num_scalar_prefetch=1,
            grid=(dps // 2,),
            in_specs=[pl.BlockSpec(block, lambda p, owner: (p, 0, 0, 0, 0, 0))],
            out_specs=[pl.BlockSpec(shape, lambda p, owner, n=len(shape): (0,) * n) for shape in outs],
        ),
        out_shape=[jax.ShapeDtypeStruct(shape, F32) for shape in outs],
        compiler_params=params(),
        name="tables",
    )(owner, gathered)


def per_device(
    tokens, cotangent, clip_live, adapter_index, gain_one, gain_two, weight_qkv, weight_out, weight_fc1, weight_fc2,
    qkv_down, qkv_up, out_down, out_up, fc1_down, fc1_up, fc2_down, fc2_up,
):
    dps, tens = lax.axis_size("dp"), lax.axis_size("tensor")
    slots = tokens.shape[0]
    axes = ("dp", "tensor")
    dp, t = lax.axis_index("dp"), lax.axis_index("tensor")
    assert slots == 2 and tens == 4 and dps % 2 == 0

    def route(flip):
        perm = []
        for a in range(dps):
            for b in range(tens):
                slot = (b % 2) ^ flip
                perm.append((a * tens + b, (a - a % 2 + b // 2) * tens + 2 * (a % 2) + slot))
        return perm

    routes = [route(0), route(1)]
    swap = [(a * tens + b, (a ^ 1) * tens + b) for a in range(dps) for b in range(tens)]
    back_routes = [[(d, s) for s, d in r] for r in routes]

    def spread(field):
        parts = []
        for flip in range(2):
            slot = (t % 2) ^ flip
            parts.append(lax.ppermute(lax.dynamic_index_in_dim(field, slot, 0, False), axes, routes[flip]))
        return parts

    def unspread(parts):
        got = [lax.ppermute(part, axes, r) for part, r in zip(parts, back_routes)]
        return jnp.where(t % 2 == 0, jnp.stack(got), jnp.stack(got[::-1]))

    both = jnp.stack([adapter_index, clip_live], axis=1)
    other = lax.ppermute(both, axes, swap)
    info = jnp.where(t // 2 == dp % 2, both, other)
    info = lax.dynamic_index_in_dim(info, t % 2, 0, False)
    codes = jnp.broadcast_to(adapter_index.reshape(1, 1, 2, 1), (1, 4, 2, 128)).reshape(1, 8, 128)

    def fold(w, dim):
        k = max(1, 128 // w.shape[dim])
        if k == 1:
            return w
        w = jnp.moveaxis(w.reshape((dps // k, k) + w.shape[1:]), 1, dim)
        return w.reshape(w.shape[:dim] + (-1,) + w.shape[dim + 2 :])

    plan = Plan(dps, tens)
    g1, g2 = gain_one.reshape(1, -1), gain_two.reshape(1, -1)
    parts_q = weight_qkv.reshape(-1, 16, weight_qkv.shape[2])
    in_rows = weight_fc1.shape[0]
    parts_1 = weight_fc1.reshape(in_rows, -1, 128).transpose(1, 0, 2)
    parts_2 = weight_fc2.reshape(parts_1.shape[0], -1, weight_fc2.shape[1])
    parts_o = weight_out.reshape(2, -1, weight_out.shape[1])
    late, fine = [], 2
    if dps <= 8:
        fine, n = 8, parts_1.shape[0] // 2
        late = [parts_1[n:], parts_2[n:]]
        parts_1, parts_2 = parts_1[:n], parts_2[:n]
    x, q, kv, kv2, low, codes, w_qkv, w_out, w_fc1, w_fc2 = intro(
        plan, dps, info, tokens, codes, g1, parts_q, parts_o, parts_1, parts_2, qkv_down, qkv_up, fine, 0
    )
    owner = codes[:, 0, 0, :2, 0].reshape(-1)
    xa, xb = x[0], x[1]
    w_qkv = fold(w_qkv.reshape((dps, tens) + weight_qkv.shape), 3)
    cotangent, q = lax.optimization_barrier((cotangent, q))
    ca, cb = spread(cotangent)
    ctx, lse = attend(q, kv, kv2)
    w_out, w_fc1, w_fc2 = fold(w_out, 4), fold(w_fc1, 3), fold(w_fc2, 4)
    la, lb, gm, gctx, grads = feed_forward(
        plan, info, xa, xb, ca, cb, ctx, g2, w_out, w_fc1, w_fc2, late,
        out_down, out_up, fc1_down, fc1_up, fc2_down, fc2_up, 2,
    )
    dq, dkv, dkv2, layer_out, early = attend_back(plan, dps, q, kv, kv2, gctx, ctx, lse, la, lb, grads, 3)
    depth, ff = out_down.shape[2], fc1_up.shape[2]
    t_od, t_ou, t_d1, t_u2, t_u1, t_d2 = tables(
        owner, early, [a.shape for a in (out_down, out_up, fc1_down, fc2_up, fc1_up, fc2_down)],
        [(n, None, 0) for n in range(4)] + [(n, None, c) for n in (4, 5) for c in range(0, ff, depth)], depth,
    )
    ya, yb, g_qd, g_qu = project_back(info, xa, xb, g1, dq, dkv, dkv2, gm, low, w_qkv, qkv_down, qkv_up)
    grads = jnp.concatenate([g_qd[None], g_qu]).astype(BF16)
    late_grads = share(plan, dps, grads.reshape((2, 2) + grads.shape[1:]), 4)
    grad_tokens = unspread([ya, yb])
    t_qd, t_qu = tables(
        owner, late_grads, [qkv_down.shape, qkv_up.shape], [(0, None, 0)] + [(1, j, 0) for j in range(3)], depth
    )
    return layer_out, grad_tokens, t_qd, t_qu, t_od, t_ou, t_d1, t_u1, t_d2, t_u2


def solution(mesh):
    rows, whole = P("dp", "tensor", None), P()
    return jax.shard_map(
        per_device,
        mesh=mesh,
        in_specs=(rows, rows, P("dp"), P("dp"), whole, whole, P(None, "dp", "tensor"), P("tensor", "dp"),
                  P("dp", "tensor"), P("tensor", "dp")) + (whole,) * 8,
        out_specs=(rows, rows) + (whole,) * 8,
        check_vma=False,
    )
```

```python
import functools
import math

import jax
import jax.numpy as jnp
from jax import lax
from jax.experimental import pallas as pl
from jax.experimental.pallas import tpu as pltpu
from jax.sharding import PartitionSpec as P

HEAD_DIM = 64
EPS = 1e-06
F32 = jnp.float32
BF16 = jnp.bfloat16
NT = (((1,), (1,)), ((), ()))
TN = (((0,), (0,)), ((), ()))
VMEM_BYTES = 61 << 20
SAFE_SCORE = 60.0
EARLY = 4


def mm(a, b):
    return jnp.dot(a, b, preferred_element_type=F32)


def mm_nt(a, b):
    return lax.dot_general(a, b, NT, preferred_element_type=F32)


def mm_tn(a, b):
    return lax.dot_general(a, b, TN, preferred_element_type=F32)


def norm_parts(field):
    centered = field - jnp.mean(field, axis=-1, keepdims=True)
    scale = lax.rsqrt(jnp.mean(centered * centered, axis=-1, keepdims=True) + EPS)
    return centered * scale, scale


def norm_back(normed, scale, gain, incoming):
    weighted = incoming * gain
    return scale * (
        weighted
        - jnp.mean(weighted, axis=-1, keepdims=True)
        - normed * jnp.mean(weighted * normed, axis=-1, keepdims=True)
    )


def params(*semantics):
    return pltpu.CompilerParams(vmem_limit_bytes=VMEM_BYTES)


class Plan:
    def __init__(self, dps, tens):
        self.tens = tens
        bits = [1 << i for i in range(1, dps.bit_length() - 1)]
        self.orders = (bits + [1], bits[::-1] + [1])
        self.hops = dps - 1
        self.ways = []
        for order in self.orders:
            blocks = [0]
            for bit in order:
                blocks = blocks + [r | bit for r in blocks]
            tops = {r: max([j for j, bit in enumerate(order) if r & bit], default=-1) for r in blocks}
            sends = {r: range(tops[r] + 1, len(order)) for r in blocks}
            ids = {}
            for r in blocks:
                for j in sends[r]:
                    ids[(r, j)] = len(ids)
            blocks.sort(key=lambda r: bin(r).count("1"))
            self.ways.append((order, blocks, tops, sends, ids))

    def semaphores(self, items):
        dma = lambda *shape: pltpu.SemaphoreType.DMA(shape)
        near = self.tens - 1
        return [dma(items), dma(items, near), dma(items, near), dma(items, self.hops), dma(items, self.hops)]

    def greet(self, extra=()):
        me, t = lax.axis_index("dp"), lax.axis_index("tensor")
        peers = [(me, lax.rem(t + k, self.tens)) for k in range(1, self.tens)]
        peers += [(me ^ bit, t) for bit in self.orders[0]]
        peers += list(extra)
        barrier = pltpu.get_barrier_semaphore()
        for peer in peers:
            pl.semaphore_signal(barrier, inc=1, device_id=peer, device_id_type=pl.DeviceIdType.MESH)
        pl.semaphore_wait(barrier, len(peers))


class Item:
    def __init__(self, plan, sems, number, src, spot, order):
        self.plan, self.src, self.spot = plan, src, spot
        self.local, self.zs, self.zr, self.ss, self.rs = [s.at[number] for s in sems]
        self.order, self.blocks, self.tops, self.sends, self.ids = plan.ways[order]
        self.me, self.t = lax.axis_index("dp"), lax.axis_index("tensor")
        self.stages = [r for r in self.blocks if len(self.sends[r])]

    def keep(self):
        return pltpu.make_async_copy(self.src, self.spot(self.me, self.t), self.local)

    def along(self, d, arriving=False):
        n = self.plan.tens
        return pltpu.make_async_remote_copy(
            src_ref=self.src,
            dst_ref=self.spot(self.me, lax.rem(self.t + n - d, n) if arriving else self.t),
            send_sem=self.zs.at[d - 1],
            recv_sem=self.zr.at[d - 1],
            device_id=(self.me, lax.rem(self.t + d, n)),
            device_id_type=pl.DeviceIdType.MESH,
        )

    def across(self, r, j, arriving=False):
        bit, n = self.order[j], self.ids[(r, j)]
        block = self.me ^ r
        return pltpu.make_async_remote_copy(
            src_ref=self.spot(block, None),
            dst_ref=self.spot(block ^ bit if arriving else block, None),
            send_sem=self.ss.at[n],
            recv_sem=self.rs.at[n],
            device_id=(self.me ^ bit, self.t),
            device_id_type=pl.DeviceIdType.MESH,
        )

    def start(self):
        self.keep().start()
        for d in range(1, self.plan.tens):
            self.along(d).start()

    def arrived(self, r):
        if r == 0:
            self.keep().wait()
            for d in range(1, self.plan.tens):
                self.along(d, True).wait_recv()
        else:
            j = self.tops[r]
            self.across(r ^ self.order[j], j, True).wait_recv()

    def advance(self, stage):
        r = self.stages[stage]
        self.arrived(r)
        for j in self.sends[r]:
            self.across(r, j).start()

    def finish(self):
        for r in self.blocks:
            if not len(self.sends[r]):
                self.arrived(r)
        for d in range(1, self.plan.tens):
            self.along(d).wait_send()
        for r in self.blocks:
            for j in self.sends[r]:
                self.across(r, j).wait_send()


def schedule(items):
    pairs = [items[k : k + 2] for k in range(0, len(items), 2)]
    stages = len(items[0].stages)

    def step(s):
        for item in pairs[0:2] if s == 0 else pairs[s + 1 : s + 2]:
            for one in item:
                one.start()
        for n, pair in enumerate(pairs):
            if 0 <= s - 1 - n < stages:
                for one in pair:
                    one.advance(s - 1 - n)

    def close():
        for item in items:
            item.finish()

    return [functools.partial(step, s) for s in range(len(pairs) + stages)] + [close]


class Route:
    def __init__(self, out, local, send, recv):
        self.out, self.local, self.send, self.recv = out, local, send, recv
        me, t = lax.axis_index("dp"), lax.axis_index("tensor")
        self.me, self.t = me, t
        core, high, low = lax.rem(me, 2), t // 2, lax.rem(t, 2)
        self.stays = core == high
        base = me - core
        self.peers = [(me ^ 1, t ^ 2), (base + high, 2 * core + 1 - low)]
        self.low = low

    def copy(self, f, src, out, arriving=False):
        if self.out:
            src, slot = src.at[self.low ^ f], f
        else:
            src, slot = src[f], self.low ^ f if arriving else self.low
        return pltpu.make_async_remote_copy(
            src_ref=src, dst_ref=out.at[slot], send_sem=self.send.at[f], recv_sem=self.recv.at[f],
            device_id=self.peers[f], device_id_type=pl.DeviceIdType.MESH,
        )

    def stay(self, blocks, out):
        if self.out:
            return pltpu.make_async_copy(blocks.at[self.low], out.at[0], self.local)
        return pltpu.make_async_copy(blocks[0], out.at[self.low], self.local)

    def start(self, blocks, out):
        self.copy(1, blocks, out).start()

        @pl.when(self.stays)
        def _():
            self.stay(blocks, out).start()

        @pl.when(jnp.logical_not(self.stays))
        def _():
            self.copy(0, blocks, out).start()

    def wait(self, blocks, out):
        @pl.when(self.stays)
        def _():
            self.stay(blocks, out).wait()

        @pl.when(jnp.logical_not(self.stays))
        def _():
            self.copy(0, blocks, out, True).wait_recv()
            self.copy(0, blocks, out).wait_send()

        self.copy(1, blocks, out, True).wait_recv()
        self.copy(1, blocks, out).wait_send()

    @staticmethod
    def semaphores():
        return [pltpu.SemaphoreType.DMA, pltpu.SemaphoreType.DMA((2,)), pltpu.SemaphoreType.DMA((2,))]


def at(ref, cut):
    return lambda a, t: ref.at[a, :, cut] if t is None else ref.at[a, t, cut]


class Pool:
    def __init__(self, plan, x_ref, o_ref, got, src, swap_send, swap_recv, *sems):
        me, t = lax.axis_index("dp"), lax.axis_index("tensor")
        self.mine = lax.rem(me, 2)
        self.x_ref, self.got, self.src = x_ref, got, src
        self.swap = pltpu.make_async_remote_copy(
            src_ref=x_ref.at[1 - self.mine], dst_ref=got, send_sem=swap_send, recv_sem=swap_recv,
            device_id=(me ^ 1, t), device_id_type=pl.DeviceIdType.MESH,
        )
        cuts = src.shape[0]
        self.items = [Item(plan, sems, k, src.at[pl.ds(k, 1)], at(o_ref, pl.ds(k, 1)), k % 2) for k in range(cuts)]
        steps = schedule(self.items)
        self.steps = [self.swap.start, functools.partial(self.add, steps[0])] + steps[1:]

    def add(self, then):
        self.swap.wait()
        self.src[...] = (self.x_ref[self.mine].astype(F32) + self.got[...].astype(F32)).astype(BF16)
        then()

    @staticmethod
    def scratch(plan, shape):
        return [pltpu.VMEM(shape, BF16), pltpu.VMEM(shape, BF16), pltpu.SemaphoreType.DMA, pltpu.SemaphoreType.DMA
                ] + plan.semaphores(shape[0])


def intro_kernel(
    plan, info, tok_ref, codes_ref, gain_ref, w_ref, wo_ref, w1_ref, w2_ref, down_ref, up_ref,
    x_ref, q_ref, kv_ref, kv2_ref, low_ref, reach_ref, codes_out, w_out, wo_out, w1_out, w2_out,
    x_s, w_s, n_s, kv_s, far_s, far_got, keep_sem, kv_send, kv_recv, far_send, far_recv, r_local, r_send, r_recv, *sems,
):
    half, depth = x_ref.shape[1:]
    tens, width = plan.tens, w_ref.shape[2]
    me, t = lax.axis_index("dp"), lax.axis_index("tensor")
    sems_w, sems = sems[:5], sems[5:]
    cuts = sems_w[0].shape[0]
    size = w_ref.shape[0] // cuts
    first = [Item(plan, sems_w, k, w_ref.at[pl.ds(k * size, size)], at(w_s, pl.ds(k * size, size)), k % 2) for k in range(cuts)]
    rest = []
    for pairs in (((codes_ref, codes_out),), ((wo_ref, wo_out),), ((w1_ref, w1_out), (w2_ref, w2_out))):
        for k in range(pairs[0][0].shape[0]):
            for src, out in pairs:
                rest.append((src.at[pl.ds(k, 1)], at(out, pl.ds(k, 1))))
    rest = rest[1:] + rest[:1]
    rest = [Item(plan, sems, n, src, spot, n % 2) for n, (src, spot) in enumerate(rest)]
    later = schedule(rest)
    route = Route(True, r_local, r_send, r_recv)
    e = info[0]

    plan.greet(route.peers)
    for item in first:
        item.start()
    stages = len(first[0].stages)
    for s in range(cuts // 2 + stages - 1):
        for n in range(cuts // 2):
            if 0 <= s - n < stages:
                first[2 * n].advance(s - n)
                first[2 * n + 1].advance(s - n)
        if s == cuts // 2 - 1:
            later[0]()
            route.start(tok_ref, x_s)
    later[1]()
    later[2]()
    route.wait(tok_ref, x_s)
    x_ref[...] = x_s[...]
    for part in range(2):
        normed, _ = norm_parts(x_s[part].astype(F32))
        n_s[part * half : (part + 1) * half, :] = normed * gain_ref[...]
    n = n_s[...].astype(BF16)
    low = mm_nt(n, down_ref[e])
    low_ref[...] = low
    low = low.astype(BF16)
    for item in first:
        item.finish()
    keep = pltpu.make_async_copy(w_s, w_out, keep_sem)
    keep.start()
    swap = pltpu.make_async_remote_copy(
        src_ref=kv_s, dst_ref=kv2_ref, send_sem=kv_send, recv_sem=kv_recv,
        device_id=(me ^ 1, t), device_id_type=pl.DeviceIdType.MESH,
    )
    far_swap = pltpu.make_async_remote_copy(
        src_ref=far_s, dst_ref=far_got, send_sem=far_send, recv_sem=far_recv,
        device_id=(me ^ 1, t), device_id_type=pl.DeviceIdType.MESH,
    )
    blocks = w_ref.shape[0] // 3
    for turn, j in enumerate((1, 2, 0)):
        later[turn + 3]()
        for c in range(tens):
            cols = slice(c * width, (c + 1) * width)
            w = w_s[:, c, j * blocks : (j + 1) * blocks].reshape(depth, width)
            res = (mm(n, w) + mm(low, up_ref[e, j, :, cols])).astype(BF16)
            if j == 0:
                q_ref[:, cols] = res
            else:
                kv_s[j - 1, :, cols] = res
            if j != 2:
                spread = lax.broadcasted_iota(jnp.int32, (width, 128), 0) // HEAD_DIM + c * (width // HEAD_DIM)
                spread = (spread == lax.broadcasted_iota(jnp.int32, (width, 128), 1)).astype(BF16)
                norms = mm(res * res, spread)
                reach = norms if c == 0 else reach + norms
        if j != 2:
            reach = 1.02 * jnp.max(reach, axis=0, keepdims=True)
        if j == 1:
            far_s[...] = jnp.broadcast_to(reach, far_s.shape)
            far_swap.start()
        if j == 0:
            far_swap.wait()
            reach_ref[...] = reach * jnp.maximum(far_s[...], far_got[...]) * (1.0 / HEAD_DIM)
        if j == 2:
            swap.start()
            kv_ref[...] = kv_s[...]
    for one in later[6:]:
        one()
    swap.wait()
    keep.wait()


def intro(plan, dps, info, tokens, codes, gain, w, wo, w1, w2, down, up, cuts, number):
    _, half, depth = tokens.shape
    rows, rank = 2 * half, down.shape[1]
    hbm, vm = pl.BlockSpec(memory_space=pl.ANY), pl.BlockSpec(memory_space=pltpu.VMEM)
    big = lambda x: jax.ShapeDtypeStruct((dps, plan.tens) + x.shape, x.dtype)
    items = codes.shape[0] + wo.shape[0] + 2 * w1.shape[0]
    return pl.pallas_call(
        functools.partial(intro_kernel, plan),
        in_specs=[pl.BlockSpec(memory_space=pltpu.SMEM), hbm, hbm, vm, hbm, hbm, hbm, hbm, vm, vm],
        out_specs=[vm, vm, vm, hbm, vm, vm] + [hbm] * 5,
        out_shape=[
            jax.ShapeDtypeStruct(tokens.shape, BF16),
            jax.ShapeDtypeStruct((rows, depth), BF16),
            jax.ShapeDtypeStruct((2, rows, depth), BF16),
            jax.ShapeDtypeStruct((2, rows, depth), BF16),
            jax.ShapeDtypeStruct((rows, rank), F32),
            jax.ShapeDtypeStruct((8, 128), F32),
            big(codes), big(w), big(wo), big(w1), big(w2),
        ],
        scratch_shapes=[
            pltpu.VMEM(tokens.shape, BF16), pltpu.VMEM((dps, plan.tens) + w.shape, BF16), pltpu.VMEM((rows, depth), F32),
            pltpu.VMEM((2, rows, depth), BF16), pltpu.VMEM((8, 128), F32), pltpu.VMEM((8, 128), F32),
        ]
        + [pltpu.SemaphoreType.DMA] * 5
        + Route.semaphores() + plan.semaphores(cuts) + plan.semaphores(items),
        compiler_params=pltpu.CompilerParams(
            vmem_limit_bytes=VMEM_BYTES, collective_id=number, has_side_effects=True
        ),
        name="intro",
    )(info, tokens, codes, gain, w, wo, w1, w2, down, up)


def attend_pair(q2, ks, vs, shifted):
    lane = lax.broadcasted_iota(jnp.int32, (1, 128), 1)
    outs, lses = [], []
    for h in range(2):
        mine = (lane // HEAD_DIM) == h
        s = mm_nt(jnp.where(mine, q2, BF16(0)), ks[...])
        if shifted:
            m = jnp.max(s, axis=1, keepdims=True)
            p = jnp.exp(s - m).astype(BF16)
        else:
            p = jnp.exp(s).astype(BF16)
        o = mm(p, vs[h])
        total = pltpu.roll(o, HEAD_DIM, 1)
        outs.append(o / total)
        lse = jnp.log(jnp.where(mine, total, o))
        lses.append(lse + m if shifted else lse)
    return (
        jnp.where(lane < HEAD_DIM, outs[0], outs[1]).astype(BF16),
        jnp.where(lane < HEAD_DIM, lses[0], lses[1]),
    )


def stage_keys(k_ref, v_ref, k2_ref, v2_ref, ks, vs):
    rows = k_ref.shape[1]
    lane = lax.broadcasted_iota(jnp.int32, (1, 128), 1)
    ks[0:rows, :] = k_ref[0]
    ks[rows:, :] = k2_ref[0]
    for h in range(2):
        mine = (lane // HEAD_DIM) == h
        vs[h, 0:rows, :] = jnp.where(mine, v_ref[0], BF16(1))
        vs[h, rows:, :] = jnp.where(mine, v2_ref[0], BF16(1))


def attend_kernel(safe, q_ref, k_ref, v_ref, k2_ref, v2_ref, o_ref, lse_ref, ks, vs):
    stage_keys(k_ref, v_ref, k2_ref, v2_ref, ks, vs)
    q2 = q_ref[...] * BF16(HEAD_DIM ** -0.5)
    pair = safe[pl.program_id(0)]

    @pl.when(pair == 1)
    def _():
        o_ref[...], lse_ref[...] = attend_pair(q2, ks, vs, False)

    @pl.when(pair != 1)
    def _():
        o_ref[...], lse_ref[...] = attend_pair(q2, ks, vs, True)


def attend(reach, q, kv, kv2):
    rows, depth = q.shape
    heads = depth // 128
    safe = (jnp.max(reach[0, : 2 * heads].reshape(heads, 2), axis=1) <= SAFE_SCORE * SAFE_SCORE).astype(jnp.int32)
    flat = pl.BlockSpec((rows, 128), lambda i, safe: (0, i))
    part = lambda j: pl.BlockSpec((1, rows, 128), lambda i, safe: (j, 0, i))
    return pl.pallas_call(
        attend_kernel,
        grid_spec=pltpu.PrefetchScalarGridSpec(
            num_scalar_prefetch=1,
            grid=(heads,),
            in_specs=[flat, part(0), part(1), part(0), part(1)],
            out_specs=[flat, flat],
            scratch_shapes=[pltpu.VMEM((2 * rows, 128), BF16), pltpu.VMEM((2, 2 * rows, 128), BF16)],
        ),
        out_shape=[jax.ShapeDtypeStruct((rows, depth), BF16), jax.ShapeDtypeStruct((rows, depth), F32)],
        compiler_params=params(),
        name="attend",
    )(safe, q, kv, kv, kv2, kv2)


def gelu_both(x):
    cdf = 0.5 * (1.0 + lax.erf(x * (2.0 ** -0.5)))
    pdf = jnp.exp(-0.5 * x * x) * ((2.0 * math.pi) ** -0.5)
    return x * cdf, cdf + x * pdf


def feed_kernel(
    plan, info, xa_ref, xb_ref, ca_ref, cb_ref, ctx_ref, gain_ref, wo_ref, w1_ref, w2_ref, w1_src, w2_src,
    od_ref, ou_ref, d1_ref, u1_ref, d2_ref, u2_ref,
    la_ref, lb_ref, gm_ref, gctx_ref, grads_ref,
    wo_s, w1_s, w2_s, mid_s, n_s, gf_s, feed_s, gn_s, lowo_s, low1_s, low2_s, b1_s, b2_s, *late,
):
    half, depth = xa_ref.shape
    rows = 2 * half
    step, last = pl.program_id(0), pl.num_programs(0) - 1
    e, live = info[0], info[1].astype(F32)
    dp, tens, wop, wor, woc = wo_ref.shape
    fr, fc = w1_ref.shape[3:]
    wide = tens * fc
    ff = u1_ref.shape[2]
    parts = ff // wide
    if late:
        w1_late, w2_late, *sems = late
        items = []
        for k in range(w1_src.shape[0]):
            for src, out in ((w1_src, w1_late), (w2_src, w2_late)):
                cut = pl.ds(k, 1)
                items.append(Item(plan, sems, len(items), src.at[cut], at(out, cut), len(items) % 2))
        steps = schedule(items)
        known = parts - len(items) // 2
    else:
        known = parts

    def put(unit, cols, value):
        per = grads_ref.shape[3] // depth
        cuts = grads_ref.shape[1]
        spot = (unit % per) * depth + cols
        if not isinstance(spot, int):
            spot = pl.multiple_of(spot, 128)
        grads_ref[unit // (per * cuts), unit // per % cuts, :, pl.ds(spot, value.shape[1])] = value.astype(BF16)

    if late:
        pl.when(step == 0)(plan.greet)
        pl.when(step == 0)(steps[0])
        for n in range(3, len(steps) - 1):
            pl.when(step == n - 2)(steps[n])
        for n in range(parts - known):
            @pl.when(step == known + n)
            def _():
                items[2 * n].finish()
                items[2 * n + 1].finish()

    @pl.when(step == 0)
    def _():
        for a in range(dp):
            for t in range(tens):
                for k in range(wop):
                    row = (t * wop + k) * wor
                    wo_s[row : row + wor, a * woc : (a + 1) * woc] = wo_ref[a, t, k]
        ctx = ctx_ref[...]
        low = mm_nt(ctx, od_ref[e])
        lowo_s[...] = low
        attention = mm(ctx, wo_s[...]) + mm(low.astype(BF16), ou_ref[e])
        for part, ref in enumerate((xa_ref, xb_ref)):
            s = slice(part * half, (part + 1) * half)
            mid_s[s, :] = ref[...].astype(F32) + attention[s, :]
        if late:
            steps[1]()
        for part, ref in enumerate((ca_ref, cb_ref)):
            s = slice(part * half, (part + 1) * half)
            gm_ref[s, :] = ref[...].astype(F32) * live
        gf_s[...] = gm_ref[...].astype(BF16)
        normed, _ = norm_parts(mid_s[...])
        n_s[...] = (normed * gain_ref[...]).astype(BF16)
        low1_s[...] = mm_nt(n_s[...], d1_ref[e])
        b2_s[...] = mm_nt(gf_s[...], u2_ref[e])
        feed_s[...] = jnp.zeros_like(feed_s)
        gn_s[...] = jnp.zeros_like(gn_s)
        low2_s[...] = jnp.zeros_like(low2_s)
        b1_s[...] = jnp.zeros_like(b1_s)

    def stage(ref_1, ref_2, part):
        for a in range(dp):
            for t in range(tens):
                w1_s[a * fr : (a + 1) * fr, t * fc : (t + 1) * fc] = ref_1[a, t, part]
                w2_s[t * fr : (t + 1) * fr, a * woc : (a + 1) * woc] = ref_2[a, t, part]

    if late:
        @pl.when(step < known)
        def _():
            stage(w1_ref, w2_ref, 0)

        @pl.when(step >= known)
        def _():
            stage(w1_late, w2_late, step - known)
    else:
        stage(w1_ref, w2_ref, 0)

    w1, w2 = w1_s[...], w2_s[...]
    runs = [pl.multiple_of((t * parts + step) * fc, fc) for t in range(tens)]
    u1 = jnp.concatenate([u1_ref[e, :, pl.ds(run, fc)] for run in runs], axis=1)
    d2 = jnp.concatenate([d2_ref[e, :, pl.ds(run, fc)] for run in runs], axis=1)
    n, gf = n_s[...], gf_s[...]
    low1, b2 = low1_s[...].astype(BF16), b2_s[...].astype(BF16)
    preact = mm(n, w1) + mm(low1, u1)
    ghid = mm_nt(gf, w2) + mm(b2, d2)
    if late:
        pl.when(step == 0)(steps[2])
    hid, slope = gelu_both(preact)
    hid = hid.astype(BF16)
    gpre = (ghid * slope).astype(BF16)
    feed_s[...] += mm(hid, w2)
    gn_s[...] += mm_nt(gpre, w1)
    low2_s[...] += mm_nt(hid, d2)
    b1_s[...] += mm_nt(gpre, u1)
    gu1, gd2 = mm_tn(low1, gpre), mm_tn(b2, hid)
    for t, run in enumerate(runs):
        cols = slice(t * fc, (t + 1) * fc)
        put(4 + run // depth, lax.rem(run, depth), gu1[:, cols])
        put(4 + ff // depth + run // depth, lax.rem(run, depth), gd2[:, cols])

    @pl.when(step == last)
    def _():
        low2, b1 = low2_s[...].astype(BF16), b1_s[...].astype(BF16)
        out = live * (mid_s[...] + feed_s[...] + mm(low2, u2_ref[e]))
        la_ref[...] = out[:half].astype(BF16)
        lb_ref[...] = out[half:].astype(BF16)
        put(3, 0, mm_tn(low2, gf_s[...]))
        gn = gn_s[...] + mm(b1, d1_ref[e])
        normed, scale = norm_parts(mid_s[...])
        put(2, 0, mm_tn(b1, n_s[...]))
        gm = gm_ref[...] + norm_back(normed, scale, gain_ref[...], gn)
        gm_ref[...] = gm
        ga = gm.astype(BF16)
        back = mm_nt(ga, ou_ref[e]).astype(BF16)
        gctx_ref[...] = (mm_nt(ga, wo_s[...]) + mm(back, od_ref[e])).astype(BF16)
        put(0, 0, mm_tn(back, ctx_ref[...]))
        put(1, 0, mm_tn(lowo_s[...].astype(BF16), ga))


def feed_forward(plan, info, xa, xb, ca, cb, ctx, gain, wo, w1, w2, late, od, ou, d1, u1, d2, u2, number):
    half, depth = xa.shape
    rows = 2 * half
    adapters, rank = od.shape[:2]
    dp, tens, wop, wor, woc = wo.shape
    fr, fc = w1.shape[3:]
    wide = tens * fc
    ff = u1.shape[2]
    known = w1.shape[2]
    once = lambda *shape: pl.BlockSpec(shape, lambda f: (0,) * len(shape), pipeline_mode=pl.Buffered(1))
    whole = lambda *shape: pl.BlockSpec(shape, lambda f: (0,) * len(shape))
    table, table_f = once(adapters, rank, depth), once(adapters, rank, ff)
    place = lambda f: (0, 0, jnp.minimum(f, known - 1), 0, 0)
    units = 4 + 2 * ff // depth
    cuts = 2
    hbm = pl.BlockSpec(memory_space=pl.ANY)
    scratch = [
        pltpu.VMEM((depth, depth), BF16),
        pltpu.VMEM((depth, wide), BF16),
        pltpu.VMEM((wide, depth), BF16),
        pltpu.VMEM((rows, depth), F32),
        pltpu.VMEM((rows, depth), BF16),
        pltpu.VMEM((rows, depth), BF16),
        pltpu.VMEM((rows, depth), F32),
        pltpu.VMEM((rows, depth), F32),
    ] + [pltpu.VMEM((rows, rank), F32)] * 5
    extra = {}
    if late:
        scratch += [pltpu.VMEM((dp, tens) + part.shape, BF16) for part in late]
        scratch += plan.semaphores(2 * late[0].shape[0])
        extra = dict(collective_id=number, has_side_effects=True)
    else:
        late = [jnp.zeros((16, 128), BF16)] * 2
    return pl.pallas_call(
        functools.partial(feed_kernel, plan),
        grid=(ff // wide,),
        in_specs=[
            pl.BlockSpec(memory_space=pltpu.SMEM),
            once(half, depth), once(half, depth), once(half, depth), once(half, depth),
            once(rows, depth),
            whole(1, depth),
            once(dp, tens, wop, wor, woc),
            pl.BlockSpec((dp, tens, 1, fr, fc), place),
            pl.BlockSpec((dp, tens, 1, fr, woc), place),
            hbm, hbm,
            table, table, table, table_f, table_f, table,
        ],
        out_specs=[
            whole(half, depth), whole(half, depth), whole(rows, depth), whole(rows, depth),
            whole(2, cuts, rank, units * depth // (2 * cuts)),
        ],
        scratch_shapes=scratch,
        out_shape=[
            jax.ShapeDtypeStruct((half, depth), BF16),
            jax.ShapeDtypeStruct((half, depth), BF16),
            jax.ShapeDtypeStruct((rows, depth), F32),
            jax.ShapeDtypeStruct((rows, depth), BF16),
            jax.ShapeDtypeStruct((2, cuts, rank, units * depth // (2 * cuts)), BF16),
        ],
        compiler_params=pltpu.CompilerParams(vmem_limit_bytes=VMEM_BYTES, **extra),
        name="feed_forward",
    )(info, xa, xb, ca, cb, ctx, gain, wo, w1, w2, late[0], late[1], od, ou, d1, u1, d2, u2)


def split3(x):
    hi = x.astype(BF16)
    rest = x - hi.astype(F32)
    mid = rest.astype(BF16)
    return hi, mid, (rest - mid.astype(F32)).astype(BF16)


def attend_back_kernel(
    plan, q_ref, k_ref, v_ref, k2_ref, v2_ref, g_ref, o_ref, lse_ref, la_ref, lb_ref, grads_ref,
    dq_ref, dkv_ref, far_ref, lo_ref, early_ref,
    ks, vs, qs, gs, acc, far_s, far_send, far_recv, lo_local, lo_send, lo_recv, *pool,
):
    rows = q_ref.shape[0]
    step, steps = pl.program_id(0), pl.num_programs(0)
    me, t = lax.axis_index("dp"), lax.axis_index("tensor")
    route = Route(False, lo_local, lo_send, lo_recv)
    early = Pool(plan, grads_ref, early_ref, *pool).steps
    blocks = (la_ref, lb_ref)

    @pl.when(step == 0)
    def _():
        plan.greet(route.peers)

    for n, one in zip((0, 1, 3, 5, 6, 7), early[:-1]):
        @pl.when(step == n)
        def _():
            one()

    @pl.when(step == 3)
    def _():
        route.start(blocks, lo_ref)

    def far(n):
        return pltpu.make_async_remote_copy(
            src_ref=far_s.at[lax.rem(n, 2)],
            dst_ref=far_ref.at[:, :, pl.ds(pl.multiple_of(n * 128, 128), 128)],
            send_sem=far_send.at[n], recv_sem=far_recv.at[n],
            device_id=(me ^ 1, t), device_id_type=pl.DeviceIdType.MESH,
        )

    zero = BF16(0)
    lane = lax.broadcasted_iota(jnp.int32, (1, 128), 1)
    scale = BF16(HEAD_DIM ** -0.5)
    q2, g2 = q_ref[...] * scale, g_ref[...]
    prod = g2.astype(F32) * o_ref[...].astype(F32)

    def less(parts, b):
        return jnp.where(lane == b, -parts[0], jnp.where(lane == b + 1, -parts[1], jnp.where(lane == b + 2, -parts[2], zero)))

    totals = split3(lse_ref[...])
    for h in range(2):
        mine, b = (lane // HEAD_DIM) == h, HEAD_DIM * h
        s = slice(h * rows, (h + 1) * rows)
        qs[s, 0:128] = jnp.where(mine, q2, zero)
        qs[s, 128:256] = less(totals, b)
        gs[s, 0:128] = jnp.where(mine, g2, zero)
        gs[s, 128:256] = less(split3(jnp.sum(jnp.where(mine, prod, 0.0), axis=1, keepdims=True)), b)
    ones = jnp.broadcast_to((lax.rem(lane, HEAD_DIM) < 3).astype(BF16), (rows, 128))

    @pl.when(step >= 2)
    def _():
        far(step - 2).wait_send()

    slot = lax.rem(step, 2)
    for i, (kr, vr) in enumerate(((k2_ref, v2_ref), (k_ref, v_ref))):
        s = slice(i * rows, (i + 1) * rows)
        ks[s, 0:128] = kr[0]
        vs[s, 0:128] = vr[0]
        ks[s, 128:256] = ones
        vs[s, 128:256] = ones
        p = jnp.exp(mm_nt(ks[s, :], qs[...]))
        ds = (p * mm_nt(vs[s, :], gs[...])).astype(BF16)
        dv = mm(p.astype(BF16), gs[:, 0:128]).astype(BF16)
        dk = mm(ds, qs[:, 0:128]).astype(BF16)
        dq = mm_tn(ds, ks[s, 0:128])
        dq = jnp.where(lane < HEAD_DIM, dq[:rows], dq[rows:])
        if i == 0:
            far_s[slot, 0] = dk
            far_s[slot, 1] = dv
            far(step).start()
            acc[...] = dq
        else:
            dkv_ref[0] = dk
            dkv_ref[1] = dv
            dq_ref[...] = ((acc[...] + dq) * (HEAD_DIM ** -0.5)).astype(BF16)

    @pl.when(step == steps - 1)
    def _():
        early[-1]()
        route.wait(blocks, lo_ref)
        far(step - 1).wait_send()
        far(step).wait_send()
        lax.fori_loop(0, steps, lambda n, c: (far(n).wait_recv(), c)[1], 0)


def attend_back(plan, dps, q, kv, kv2, g, ctx, lse, la, lb, grads, number):
    rows, depth = q.shape
    flat = pl.BlockSpec((rows, 128), lambda i: (0, i))
    part = lambda j: pl.BlockSpec((1, rows, 128), lambda i: (j, 0, i))
    both = pl.BlockSpec((2, rows, 128), lambda i: (0, 0, i))
    hbm = pl.BlockSpec(memory_space=pl.ANY)
    heads = depth // 128
    dma = lambda *shape: pltpu.SemaphoreType.DMA(shape)
    return pl.pallas_call(
        functools.partial(attend_back_kernel, plan),
        grid=(heads,),
        in_specs=[flat, part(0), part(1), part(0), part(1), flat, flat, flat, hbm, hbm,
                  pl.BlockSpec(grads.shape, lambda i: (0, 0, 0, 0), pipeline_mode=pl.Buffered(1))],
        out_specs=[flat, both, hbm, hbm, hbm],
        out_shape=[
            jax.ShapeDtypeStruct((rows, depth), BF16),
            jax.ShapeDtypeStruct((2, rows, depth), BF16),
            jax.ShapeDtypeStruct((2, rows, depth), BF16),
            jax.ShapeDtypeStruct((2,) + la.shape, BF16),
            jax.ShapeDtypeStruct((dps, plan.tens) + grads.shape[1:], BF16),
        ],
        scratch_shapes=[pltpu.VMEM((2 * rows, 256), BF16)] * 4
        + [pltpu.VMEM((rows, 128), F32), pltpu.VMEM((2, 2, rows, 128), BF16), dma(heads), dma(heads),
           *Route.semaphores()]
        + Pool.scratch(plan, grads.shape[1:]),
        compiler_params=pltpu.CompilerParams(
            vmem_limit_bytes=VMEM_BYTES, collective_id=number, has_side_effects=True
        ),
        name="attend_back",
    )(q, kv, kv, kv2, kv2, g, ctx, lse, la, lb, grads)


def low_back_kernel(info, x_ref, gain_ref, dq_ref, dkv_ref, dkv2_ref, low_ref, up_ref, gkv_ref, back_ref, grads_ref):
    half = x_ref.shape[1]
    step, last = pl.program_id(0), pl.num_programs(0) - 1
    cuts = grads_ref.shape[1]

    def go(g, first):
        back = mm_nt(g, up_ref[0, 0])
        back_ref[...] = back if first else back_ref[...] + back
        grads_ref[(step + 1) // cuts, lax.rem(step + 1, cuts)] = mm_tn(low_ref[...].astype(BF16), g).astype(BF16)

    @pl.when(step == 0)
    def _():
        go(dq_ref[...], True)

    @pl.when(step > 0)
    def _():
        g = (dkv_ref[0].astype(F32) + dkv2_ref[0].astype(F32)).astype(BF16)
        gkv_ref[0] = g
        go(g, False)

    @pl.when(step == last)
    def _():
        total = None
        for part in range(2):
            normed, _ = norm_parts(x_ref[part].astype(F32))
            back = back_ref[part * half : (part + 1) * half, :].astype(BF16)
            term = mm_tn(back, (normed * gain_ref[...]).astype(BF16))
            total = term if total is None else total + term
        grads_ref[0, 0] = total.astype(BF16)


def low_back(info, x, gain, dq, dkv, dkv2, low, up):
    _, half, depth = x.shape
    rows, rank = 2 * half, low.shape[1]
    once = lambda *shape: pl.BlockSpec(shape, lambda j, info: (0,) * len(shape), pipeline_mode=pl.Buffered(1))
    pair = pl.BlockSpec((1, rows, depth), lambda j, info: (jnp.maximum(j - 1, 0), 0, 0))
    return pl.pallas_call(
        low_back_kernel,
        grid_spec=pltpu.PrefetchScalarGridSpec(
            num_scalar_prefetch=1,
            grid=(3,),
            in_specs=[
                once(2, half, depth), once(1, depth), once(rows, depth), pair, pair, once(rows, rank),
                pl.BlockSpec((1, 1, rank, depth), lambda j, info: (info[0], j, 0, 0)),
            ],
            out_specs=[
                pair, pl.BlockSpec((rows, rank), lambda j, info: (0, 0)),
                pl.BlockSpec((2, 2, rank, depth), lambda j, info: (0, 0, 0, 0)),
            ],
        ),
        out_shape=[
            jax.ShapeDtypeStruct((2, rows, depth), BF16),
            jax.ShapeDtypeStruct((rows, rank), F32),
            jax.ShapeDtypeStruct((2, 2, rank, depth), BF16),
        ],
        compiler_params=params(),
        name="low_back",
    )(info, x, gain, dq, dkv, dkv2, low, up)


def outro_kernel(
    plan, info, x_ref, gain_ref, dq_ref, gkv_ref, back_ref, gm_ref, w_ref, down_ref, grads_ref,
    ya_ref, yb_ref, late_ref, gn_s, *pool,
):
    half, depth = x_ref.shape[1:]
    parts, width = w_ref.shape[1], w_ref.shape[4]
    step, last = pl.program_id(0), pl.num_programs(0) - 1
    late = Pool(plan, grads_ref, late_ref, *pool).steps

    @pl.when(step == 0)
    def _():
        plan.greet()
        late[0]()

    def go(g, first):
        acc = mm(back_ref[...].astype(BF16), down_ref[info[0]]) if first else gn_s[...]
        for part in range(parts):
            cols = slice(part * width, (part + 1) * width)
            acc = acc + mm_nt(g[:, cols], w_ref[:, part, 0].reshape(depth, width))
        gn_s[...] = acc

    @pl.when(step == 0)
    def _():
        go(dq_ref[...], True)
        late[1]()

    @pl.when(step > 0)
    def _():
        go(gkv_ref[0], False)

    @pl.when(step == 1)
    def _():
        late[2]()

    @pl.when(step == last)
    def _():
        late[3]()
        for part, y_ref in enumerate((ya_ref, yb_ref)):
            s = slice(part * half, (part + 1) * half)
            normed, scale = norm_parts(x_ref[part].astype(F32))
            y_ref[...] = (gm_ref[s, :] + norm_back(normed, scale, gain_ref[...], gn_s[s, :])).astype(BF16)
        for one in late[4:]:
            one()


def outro(plan, dps, info, x, gain, dq, gkv, back, gm, w, down, grads, number):
    _, half, depth = x.shape
    rows = 2 * half
    dp, tens, _, wr, wc = w.shape
    whole = lambda *shape: pl.BlockSpec(shape, lambda j: (0,) * len(shape))
    once = lambda *shape: pl.BlockSpec(shape, lambda j: (0,) * len(shape), pipeline_mode=pl.Buffered(1))
    return pl.pallas_call(
        functools.partial(outro_kernel, plan),
        grid=(3,),
        in_specs=[
            pl.BlockSpec(memory_space=pltpu.SMEM),
            once(2, half, depth), once(1, depth), once(rows, depth),
            pl.BlockSpec((1, rows, depth), lambda j: (jnp.maximum(j - 1, 0), 0, 0)),
            once(*back.shape), once(rows, depth),
            pl.BlockSpec((dp, tens, 1, wr, wc), lambda j: (0, 0, j, 0, 0)),
            once(*down.shape), once(*grads.shape),
        ],
        out_specs=[whole(half, depth), whole(half, depth), pl.BlockSpec(memory_space=pl.ANY)],
        out_shape=[
            jax.ShapeDtypeStruct((half, depth), BF16),
            jax.ShapeDtypeStruct((half, depth), BF16),
            jax.ShapeDtypeStruct((dps, plan.tens) + grads.shape[1:], BF16),
        ],
        scratch_shapes=[pltpu.VMEM((rows, depth), F32)] + Pool.scratch(plan, grads.shape[1:]),
        compiler_params=pltpu.CompilerParams(
            vmem_limit_bytes=VMEM_BYTES, collective_id=number, has_side_effects=True
        ),
        name="outro",
    )(info, x, gain, dq, gkv, back, gm, w, down, grads)


def table_kernel(places, unit, owner, g_ref, *outs):
    _, _, tens, cuts, _, width = g_ref.shape
    pair, per = pl.program_id(0), width // unit

    @pl.when(pair == 0)
    def _():
        for out in outs:
            out[...] = jnp.zeros_like(out)

    for t in range(tens):
        e = owner[pair * tens + t]
        for n, (out, sub, start) in enumerate(places):
            col = n % per * unit
            piece = g_ref[0, n // (per * cuts), t, n // per % cuts, :, col : col + unit].astype(F32)
            if sub is None:
                outs[out][e, :, start : start + unit] += piece
            else:
                outs[out][e, sub, :, start : start + unit] += piece


def tables(owner, gathered, outs, places, unit):
    dps = gathered.shape[0]
    gathered = gathered.reshape((dps // 2, 2) + gathered.shape[1:])
    block = (1,) + gathered.shape[1:]
    return pl.pallas_call(
        functools.partial(table_kernel, places, unit),
        grid_spec=pltpu.PrefetchScalarGridSpec(
            num_scalar_prefetch=1,
            grid=(dps // 2,),
            in_specs=[pl.BlockSpec(block, lambda p, owner: (p, 0, 0, 0, 0, 0))],
            out_specs=[pl.BlockSpec(shape, lambda p, owner, n=len(shape): (0,) * n) for shape in outs],
        ),
        out_shape=[jax.ShapeDtypeStruct(shape, F32) for shape in outs],
        compiler_params=params(),
        name="tables",
    )(owner, gathered)


def per_device(
    tokens, cotangent, clip_live, adapter_index, gain_one, gain_two, weight_qkv, weight_out, weight_fc1, weight_fc2,
    qkv_down, qkv_up, out_down, out_up, fc1_down, fc1_up, fc2_down, fc2_up,
):
    dps, tens = lax.axis_size("dp"), lax.axis_size("tensor")
    slots = tokens.shape[0]
    axes = ("dp", "tensor")
    dp, t = lax.axis_index("dp"), lax.axis_index("tensor")
    assert slots == 2 and tens == 4 and dps % 2 == 0

    def route(flip):
        perm = []
        for a in range(dps):
            for b in range(tens):
                slot = (b % 2) ^ flip
                perm.append((a * tens + b, (a - a % 2 + b // 2) * tens + 2 * (a % 2) + slot))
        return perm

    routes = [route(0), route(1)]
    swap = [(a * tens + b, (a ^ 1) * tens + b) for a in range(dps) for b in range(tens)]
    back_routes = [[(d, s) for s, d in r] for r in routes]

    def spread(field):
        parts = []
        for flip in range(2):
            slot = (t % 2) ^ flip
            parts.append(lax.ppermute(lax.dynamic_index_in_dim(field, slot, 0, False), axes, routes[flip]))
        return parts

    def unspread(parts):
        got = [lax.ppermute(part, axes, r) for part, r in zip(parts, back_routes)]
        return jnp.where(t % 2 == 0, jnp.stack(got), jnp.stack(got[::-1]))

    both = jnp.stack([adapter_index, clip_live], axis=1)
    other = lax.ppermute(both, axes, swap)
    info = jnp.where(t // 2 == dp % 2, both, other)
    info = lax.dynamic_index_in_dim(info, t % 2, 0, False)
    codes = jnp.broadcast_to(adapter_index.reshape(1, 1, 2, 1), (1, 4, 2, 128)).reshape(1, 8, 128)

    def fold(w, dim):
        k = max(1, 128 // w.shape[dim])
        if k == 1:
            return w
        w = jnp.moveaxis(w.reshape((dps // k, k) + w.shape[1:]), 1, dim)
        return w.reshape(w.shape[:dim] + (-1,) + w.shape[dim + 2 :])

    plan = Plan(dps, tens)
    g1, g2 = gain_one.reshape(1, -1), gain_two.reshape(1, -1)
    parts_q = weight_qkv.reshape(-1, 16, weight_qkv.shape[2])
    in_rows = weight_fc1.shape[0]
    parts_1 = weight_fc1.reshape(in_rows, -1, 128).transpose(1, 0, 2)
    parts_2 = weight_fc2.reshape(parts_1.shape[0], -1, weight_fc2.shape[1])
    parts_o = weight_out.reshape(2, -1, weight_out.shape[1])
    late, fine = [], 2
    if dps <= 8:
        fine, n = 8, parts_1.shape[0] * EARLY // 8
        late = [parts_1[n:], parts_2[n:]]
        parts_1, parts_2 = parts_1[:n], parts_2[:n]
    x, q, kv, kv2, low, reach, codes, w_qkv, w_out, w_fc1, w_fc2 = intro(
        plan, dps, info, tokens, codes, g1, parts_q, parts_o, parts_1, parts_2, qkv_down, qkv_up, fine, 0
    )
    owner = codes[:, 0, 0, :2, 0].reshape(-1)
    xa, xb = x[0], x[1]
    w_qkv = fold(w_qkv.reshape((dps, tens) + weight_qkv.shape), 3)
    cotangent, q = lax.optimization_barrier((cotangent, q))
    ca, cb = spread(cotangent)
    ctx, lse = attend(reach, q, kv, kv2)
    w_out, w_fc1, w_fc2 = fold(w_out, 4), fold(w_fc1, 3), fold(w_fc2, 4)
    la, lb, gm, gctx, grads = feed_forward(
        plan, info, xa, xb, ca, cb, ctx, g2, w_out, w_fc1, w_fc2, late,
        out_down, out_up, fc1_down, fc1_up, fc2_down, fc2_up, 2,
    )
    dq, dkv, dkv2, layer_out, early = attend_back(plan, dps, q, kv, kv2, gctx, ctx, lse, la, lb, grads, 3)
    depth, ff = out_down.shape[2], fc1_up.shape[2]
    gkv, back, grads = low_back(info, x, g1, dq, dkv, dkv2, low, qkv_up)
    ya, yb, late_grads = outro(plan, dps, info, x, g1, dq, gkv, back, gm, w_qkv, qkv_down, grads, 4)
    grad_tokens = unspread([ya, yb])
    late_grads, early, owner, ya = lax.optimization_barrier((late_grads, early, owner, ya))
    t_od, t_ou, t_d1, t_u2, t_u1, t_d2 = tables(
        owner, early, [a.shape for a in (out_down, out_up, fc1_down, fc2_up, fc1_up, fc2_down)],
        [(n, None, 0) for n in range(4)] + [(n, None, c) for n in (4, 5) for c in range(0, ff, depth)], depth,
    )
    t_qd, t_qu = tables(
        owner, late_grads, [qkv_down.shape, qkv_up.shape], [(0, None, 0)] + [(1, j, 0) for j in range(3)], depth
    )
    return layer_out, grad_tokens, t_qd, t_qu, t_od, t_ou, t_d1, t_u1, t_d2, t_u2


def solution(mesh):
    rows, whole = P("dp", "tensor", None), P()
    return jax.shard_map(
        per_device,
        mesh=mesh,
        in_specs=(rows, rows, P("dp"), P("dp"), whole, whole, P(None, "dp", "tensor"), P("tensor", "dp"),
                  P("dp", "tensor"), P("tensor", "dp")) + (whole,) * 8,
        out_specs=(rows, rows) + (whole,) * 8,
        check_vma=False,
    )
```

```python
import functools
import math

import jax
import jax.numpy as jnp
from jax import lax
from jax.experimental import pallas as pl
from jax.experimental.pallas import tpu as pltpu
from jax.sharding import PartitionSpec as P

HEAD_DIM = 64
EPS = 1e-06
F32 = jnp.float32
BF16 = jnp.bfloat16
NT = (((1,), (1,)), ((), ()))
TN = (((0,), (0,)), ((), ()))
VMEM_BYTES = 61 << 20
SAFE_SCORE = 60.0
EARLY = 4


def mm(a, b):
    return jnp.dot(a, b, preferred_element_type=F32)


def mm_nt(a, b):
    return lax.dot_general(a, b, NT, preferred_element_type=F32)


def mm_tn(a, b):
    return lax.dot_general(a, b, TN, preferred_element_type=F32)


def norm_parts(field):
    centered = field - jnp.mean(field, axis=-1, keepdims=True)
    scale = lax.rsqrt(jnp.mean(centered * centered, axis=-1, keepdims=True) + EPS)
    return centered * scale, scale


def norm_back(normed, scale, gain, incoming):
    weighted = incoming * gain
    return scale * (
        weighted
        - jnp.mean(weighted, axis=-1, keepdims=True)
        - normed * jnp.mean(weighted * normed, axis=-1, keepdims=True)
    )


def params(*semantics):
    return pltpu.CompilerParams(vmem_limit_bytes=VMEM_BYTES)


class Plan:
    def __init__(self, dps, tens):
        self.tens = tens
        bits = [1 << i for i in range(1, dps.bit_length() - 1)]
        self.orders = (bits + [1], bits[::-1] + [1])
        self.hops = dps - 1
        self.ways = []
        for order in self.orders:
            blocks = [0]
            for bit in order:
                blocks = blocks + [r | bit for r in blocks]
            tops = {r: max([j for j, bit in enumerate(order) if r & bit], default=-1) for r in blocks}
            sends = {r: range(tops[r] + 1, len(order)) for r in blocks}
            ids = {}
            for r in blocks:
                for j in sends[r]:
                    ids[(r, j)] = len(ids)
            blocks.sort(key=lambda r: bin(r).count("1"))
            self.ways.append((order, blocks, tops, sends, ids))

    def semaphores(self, items):
        dma = lambda *shape: pltpu.SemaphoreType.DMA(shape)
        near = self.tens - 1
        return [dma(items), dma(items, near), dma(items, near), dma(items, self.hops), dma(items, self.hops)]

    def greet(self, extra=()):
        me, t = lax.axis_index("dp"), lax.axis_index("tensor")
        peers = [(me, lax.rem(t + k, self.tens)) for k in range(1, self.tens)]
        peers += [(me ^ bit, t) for bit in self.orders[0]]
        peers += list(extra)
        barrier = pltpu.get_barrier_semaphore()
        for peer in peers:
            pl.semaphore_signal(barrier, inc=1, device_id=peer, device_id_type=pl.DeviceIdType.MESH)
        pl.semaphore_wait(barrier, len(peers))


class Item:
    def __init__(self, plan, sems, number, src, spot, order):
        self.plan, self.src, self.spot = plan, src, spot
        self.local, self.zs, self.zr, self.ss, self.rs = [s.at[number] for s in sems]
        self.order, self.blocks, self.tops, self.sends, self.ids = plan.ways[order]
        self.me, self.t = lax.axis_index("dp"), lax.axis_index("tensor")
        passed = [r for r in self.blocks if len(self.sends[r])]
        far = sorted({bin(r).count("1") for r in passed})
        self.stages = [[r for r in passed if bin(r).count("1") == n] for n in far]

    def keep(self):
        return pltpu.make_async_copy(self.src, self.spot(self.me, self.t), self.local)

    def along(self, d, arriving=False):
        n = self.plan.tens
        return pltpu.make_async_remote_copy(
            src_ref=self.src,
            dst_ref=self.spot(self.me, lax.rem(self.t + n - d, n) if arriving else self.t),
            send_sem=self.zs.at[d - 1],
            recv_sem=self.zr.at[d - 1],
            device_id=(self.me, lax.rem(self.t + d, n)),
            device_id_type=pl.DeviceIdType.MESH,
        )

    def across(self, r, j, arriving=False):
        bit, n = self.order[j], self.ids[(r, j)]
        block = self.me ^ r
        return pltpu.make_async_remote_copy(
            src_ref=self.spot(block, None),
            dst_ref=self.spot(block ^ bit if arriving else block, None),
            send_sem=self.ss.at[n],
            recv_sem=self.rs.at[n],
            device_id=(self.me ^ bit, self.t),
            device_id_type=pl.DeviceIdType.MESH,
        )

    def start(self):
        self.keep().start()
        for d in range(1, self.plan.tens):
            self.along(d).start()

    def arrived(self, r):
        if r == 0:
            self.keep().wait()
            for d in range(1, self.plan.tens):
                self.along(d, True).wait_recv()
        else:
            j = self.tops[r]
            self.across(r ^ self.order[j], j, True).wait_recv()

    def advance(self, stage):
        for r in self.stages[stage]:
            self.arrived(r)
            for j in self.sends[r]:
                self.across(r, j).start()

    def finish(self):
        for r in self.blocks:
            if not len(self.sends[r]):
                self.arrived(r)
        for d in range(1, self.plan.tens):
            self.along(d).wait_send()
        for r in self.blocks:
            for j in self.sends[r]:
                self.across(r, j).wait_send()


def schedule(items):
    pairs = [items[k : k + 2] for k in range(0, len(items), 2)]
    stages = len(items[0].stages)

    def step(s):
        for item in pairs[0:2] if s == 0 else pairs[s + 1 : s + 2]:
            for one in item:
                one.start()
        for n, pair in enumerate(pairs):
            if 0 <= s - 1 - n < stages:
                for one in pair:
                    one.advance(s - 1 - n)

    def close():
        for item in items:
            item.finish()

    return [functools.partial(step, s) for s in range(len(pairs) + stages)] + [close]


class Route:
    def __init__(self, out, local, send, recv):
        self.out, self.local, self.send, self.recv = out, local, send, recv
        me, t = lax.axis_index("dp"), lax.axis_index("tensor")
        self.me, self.t = me, t
        core, high, low = lax.rem(me, 2), t // 2, lax.rem(t, 2)
        self.stays = core == high
        base = me - core
        self.peers = [(me ^ 1, t ^ 2), (base + high, 2 * core + 1 - low)]
        self.low = low

    def copy(self, f, src, out, arriving=False):
        if self.out:
            src, slot = src.at[self.low ^ f], f
        else:
            src, slot = src[f], self.low ^ f if arriving else self.low
        return pltpu.make_async_remote_copy(
            src_ref=src, dst_ref=out.at[slot], send_sem=self.send.at[f], recv_sem=self.recv.at[f],
            device_id=self.peers[f], device_id_type=pl.DeviceIdType.MESH,
        )

    def stay(self, blocks, out):
        if self.out:
            return pltpu.make_async_copy(blocks.at[self.low], out.at[0], self.local)
        return pltpu.make_async_copy(blocks[0], out.at[self.low], self.local)

    def start(self, blocks, out):
        self.copy(1, blocks, out).start()

        @pl.when(self.stays)
        def _():
            self.stay(blocks, out).start()

        @pl.when(jnp.logical_not(self.stays))
        def _():
            self.copy(0, blocks, out).start()

    def wait(self, blocks, out):
        @pl.when(self.stays)
        def _():
            self.stay(blocks, out).wait()

        @pl.when(jnp.logical_not(self.stays))
        def _():
            self.copy(0, blocks, out, True).wait_recv()
            self.copy(0, blocks, out).wait_send()

        self.copy(1, blocks, out, True).wait_recv()
        self.copy(1, blocks, out).wait_send()

    @staticmethod
    def semaphores():
        return [pltpu.SemaphoreType.DMA, pltpu.SemaphoreType.DMA((2,)), pltpu.SemaphoreType.DMA((2,))]


def at(ref, cut):
    return lambda a, t: ref.at[a, :, cut] if t is None else ref.at[a, t, cut]


class Pool:
    def __init__(self, plan, x_ref, o_ref, got, src, swap_send, swap_recv, *sems):
        me, t = lax.axis_index("dp"), lax.axis_index("tensor")
        self.mine = lax.rem(me, 2)
        self.x_ref, self.got, self.src = x_ref, got, src
        self.swap = pltpu.make_async_remote_copy(
            src_ref=x_ref.at[1 - self.mine], dst_ref=got, send_sem=swap_send, recv_sem=swap_recv,
            device_id=(me ^ 1, t), device_id_type=pl.DeviceIdType.MESH,
        )
        cuts = src.shape[0]
        self.items = [Item(plan, sems, k, src.at[pl.ds(k, 1)], at(o_ref, pl.ds(k, 1)), k % 2) for k in range(cuts)]
        steps = schedule(self.items)
        self.steps = [self.swap.start, functools.partial(self.add, steps[0])] + steps[1:]

    def add(self, then):
        self.swap.wait()
        self.src[...] = (self.x_ref[self.mine].astype(F32) + self.got[...].astype(F32)).astype(BF16)
        then()

    @staticmethod
    def scratch(plan, shape):
        return [pltpu.VMEM(shape, BF16), pltpu.VMEM(shape, BF16), pltpu.SemaphoreType.DMA, pltpu.SemaphoreType.DMA
                ] + plan.semaphores(shape[0])


def intro_kernel(
    plan, info, tok_ref, codes_ref, gain_ref, w_ref, wo_ref, w1_ref, w2_ref, down_ref, up_ref,
    x_ref, q_ref, kv_ref, kv2_ref, low_ref, reach_ref, codes_out, w_out, wo_out, w1_out, w2_out,
    x_s, w_s, n_s, kv_s, far_s, far_got, keep_sem, kv_send, kv_recv, far_send, far_recv, r_local, r_send, r_recv, *sems,
):
    half, depth = x_ref.shape[1:]
    tens, width = plan.tens, w_ref.shape[2]
    me, t = lax.axis_index("dp"), lax.axis_index("tensor")
    sems_w, sems = sems[:5], sems[5:]
    cuts = sems_w[0].shape[0]
    size = w_ref.shape[0] // cuts
    first = [Item(plan, sems_w, k, w_ref.at[pl.ds(k * size, size)], at(w_s, pl.ds(k * size, size)), k % 2) for k in range(cuts)]
    rest = []
    for pairs in (((codes_ref, codes_out),), ((wo_ref, wo_out),), ((w1_ref, w1_out), (w2_ref, w2_out))):
        for k in range(pairs[0][0].shape[0]):
            for src, out in pairs:
                rest.append((src.at[pl.ds(k, 1)], at(out, pl.ds(k, 1))))
    rest = rest[1:] + rest[:1]
    rest = [Item(plan, sems, n, src, spot, n % 2) for n, (src, spot) in enumerate(rest)]
    later = schedule(rest)
    route = Route(True, r_local, r_send, r_recv)
    e = info[0]

    plan.greet(route.peers)
    for item in first:
        item.start()
    stages = len(first[0].stages)
    for s in range(cuts // 2 + stages - 1):
        for n in range(cuts // 2):
            if 0 <= s - n < stages:
                first[2 * n].advance(s - n)
                first[2 * n + 1].advance(s - n)
        if s == cuts // 2 - 1:
            later[0]()
            route.start(tok_ref, x_s)
    later[1]()
    later[2]()
    route.wait(tok_ref, x_s)
    x_ref[...] = x_s[...]
    for part in range(2):
        normed, _ = norm_parts(x_s[part].astype(F32))
        n_s[part * half : (part + 1) * half, :] = normed * gain_ref[...]
    n = n_s[...].astype(BF16)
    low = mm_nt(n, down_ref[e])
    low_ref[...] = low
    low = low.astype(BF16)
    for item in first:
        item.finish()
    keep = pltpu.make_async_copy(w_s, w_out, keep_sem)
    keep.start()
    swap = pltpu.make_async_remote_copy(
        src_ref=kv_s, dst_ref=kv2_ref, send_sem=kv_send, recv_sem=kv_recv,
        device_id=(me ^ 1, t), device_id_type=pl.DeviceIdType.MESH,
    )
    far_swap = pltpu.make_async_remote_copy(
        src_ref=far_s, dst_ref=far_got, send_sem=far_send, recv_sem=far_recv,
        device_id=(me ^ 1, t), device_id_type=pl.DeviceIdType.MESH,
    )
    blocks = w_ref.shape[0] // 3
    for turn, j in enumerate((1, 2, 0)):
        later[turn + 3]()
        for c in range(tens):
            cols = slice(c * width, (c + 1) * width)
            w = w_s[:, c, j * blocks : (j + 1) * blocks].reshape(depth, width)
            res = (mm(n, w) + mm(low, up_ref[e, j, :, cols])).astype(BF16)
            if j == 0:
                q_ref[:, cols] = res
            else:
                kv_s[j - 1, :, cols] = res
            if j != 2:
                spread = lax.broadcasted_iota(jnp.int32, (width, 128), 0) // HEAD_DIM + c * (width // HEAD_DIM)
                spread = (spread == lax.broadcasted_iota(jnp.int32, (width, 128), 1)).astype(BF16)
                norms = mm(res * res, spread)
                reach = norms if c == 0 else reach + norms
        if j != 2:
            reach = 1.02 * jnp.max(reach, axis=0, keepdims=True)
        if j == 1:
            far_s[...] = jnp.broadcast_to(reach, far_s.shape)
            far_swap.start()
        if j == 0:
            far_swap.wait()
            reach_ref[...] = reach * jnp.maximum(far_s[...], far_got[...]) * (1.0 / HEAD_DIM)
        if j == 2:
            swap.start()
            kv_ref[...] = kv_s[...]
    for one in later[6:]:
        one()
    swap.wait()
    keep.wait()


def intro(plan, dps, info, tokens, codes, gain, w, wo, w1, w2, down, up, cuts, number):
    _, half, depth = tokens.shape
    rows, rank = 2 * half, down.shape[1]
    hbm, vm = pl.BlockSpec(memory_space=pl.ANY), pl.BlockSpec(memory_space=pltpu.VMEM)
    big = lambda x: jax.ShapeDtypeStruct((dps, plan.tens) + x.shape, x.dtype)
    items = codes.shape[0] + wo.shape[0] + 2 * w1.shape[0]
    return pl.pallas_call(
        functools.partial(intro_kernel, plan),
        in_specs=[pl.BlockSpec(memory_space=pltpu.SMEM), hbm, hbm, vm, hbm, hbm, hbm, hbm, vm, vm],
        out_specs=[vm, vm, vm, hbm, vm, vm] + [hbm] * 5,
        out_shape=[
            jax.ShapeDtypeStruct(tokens.shape, BF16),
            jax.ShapeDtypeStruct((rows, depth), BF16),
            jax.ShapeDtypeStruct((2, rows, depth), BF16),
            jax.ShapeDtypeStruct((2, rows, depth), BF16),
            jax.ShapeDtypeStruct((rows, rank), F32),
            jax.ShapeDtypeStruct((8, 128), F32),
            big(codes), big(w), big(wo), big(w1), big(w2),
        ],
        scratch_shapes=[
            pltpu.VMEM(tokens.shape, BF16), pltpu.VMEM((dps, plan.tens) + w.shape, BF16), pltpu.VMEM((rows, depth), F32),
            pltpu.VMEM((2, rows, depth), BF16), pltpu.VMEM((8, 128), F32), pltpu.VMEM((8, 128), F32),
        ]
        + [pltpu.SemaphoreType.DMA] * 5
        + Route.semaphores() + plan.semaphores(cuts) + plan.semaphores(items),
        compiler_params=pltpu.CompilerParams(
            vmem_limit_bytes=VMEM_BYTES, collective_id=number, has_side_effects=True
        ),
        name="intro",
    )(info, tokens, codes, gain, w, wo, w1, w2, down, up)


def attend_pair(q2, ks, vs, shifted):
    lane = lax.broadcasted_iota(jnp.int32, (1, 128), 1)
    outs, lses = [], []
    for h in range(2):
        mine = (lane // HEAD_DIM) == h
        s = mm_nt(jnp.where(mine, q2, BF16(0)), ks[...])
        if shifted:
            m = jnp.max(s, axis=1, keepdims=True)
            p = jnp.exp(s - m).astype(BF16)
        else:
            p = jnp.exp(s).astype(BF16)
        o = mm(p, vs[h])
        total = pltpu.roll(o, HEAD_DIM, 1)
        outs.append(o / total)
        lse = jnp.log(jnp.where(mine, total, o))
        lses.append(lse + m if shifted else lse)
    return (
        jnp.where(lane < HEAD_DIM, outs[0], outs[1]).astype(BF16),
        jnp.where(lane < HEAD_DIM, lses[0], lses[1]),
    )


def stage_keys(k_ref, v_ref, k2_ref, v2_ref, ks, vs):
    rows = k_ref.shape[1]
    lane = lax.broadcasted_iota(jnp.int32, (1, 128), 1)
    ks[0:rows, :] = k_ref[0]
    ks[rows:, :] = k2_ref[0]
    for h in range(2):
        mine = (lane // HEAD_DIM) == h
        vs[h, 0:rows, :] = jnp.where(mine, v_ref[0], BF16(1))
        vs[h, rows:, :] = jnp.where(mine, v2_ref[0], BF16(1))


def attend_kernel(safe, q_ref, k_ref, v_ref, k2_ref, v2_ref, o_ref, lse_ref, ks, vs):
    stage_keys(k_ref, v_ref, k2_ref, v2_ref, ks, vs)
    q2 = q_ref[...] * BF16(HEAD_DIM ** -0.5)
    pair = safe[pl.program_id(0)]

    @pl.when(pair == 1)
    def _():
        o_ref[...], lse_ref[...] = attend_pair(q2, ks, vs, False)

    @pl.when(pair != 1)
    def _():
        o_ref[...], lse_ref[...] = attend_pair(q2, ks, vs, True)


def attend(reach, q, kv, kv2):
    rows, depth = q.shape
    heads = depth // 128
    safe = (jnp.max(reach[0, : 2 * heads].reshape(heads, 2), axis=1) <= SAFE_SCORE * SAFE_SCORE).astype(jnp.int32)
    flat = pl.BlockSpec((rows, 128), lambda i, safe: (0, i))
    part = lambda j: pl.BlockSpec((1, rows, 128), lambda i, safe: (j, 0, i))
    return pl.pallas_call(
        attend_kernel,
        grid_spec=pltpu.PrefetchScalarGridSpec(
            num_scalar_prefetch=1,
            grid=(heads,),
            in_specs=[flat, part(0), part(1), part(0), part(1)],
            out_specs=[flat, flat],
            scratch_shapes=[pltpu.VMEM((2 * rows, 128), BF16), pltpu.VMEM((2, 2 * rows, 128), BF16)],
        ),
        out_shape=[jax.ShapeDtypeStruct((rows, depth), BF16), jax.ShapeDtypeStruct((rows, depth), F32)],
        compiler_params=params(),
        name="attend",
    )(safe, q, kv, kv, kv2, kv2)


def gelu_both(x):
    cdf = 0.5 * (1.0 + lax.erf(x * (2.0 ** -0.5)))
    pdf = jnp.exp(-0.5 * x * x) * ((2.0 * math.pi) ** -0.5)
    return x * cdf, cdf + x * pdf


def feed_kernel(
    plan, info, xa_ref, xb_ref, ca_ref, cb_ref, ctx_ref, gain_ref, wo_ref, w1_ref, w2_ref, w1_src, w2_src,
    od_ref, ou_ref, d1_ref, u1_ref, d2_ref, u2_ref,
    la_ref, lb_ref, gm_ref, gctx_ref, grads_ref,
    wo_s, w1_s, w2_s, mid_s, n_s, gf_s, feed_s, gn_s, lowo_s, low1_s, low2_s, b1_s, b2_s, *late,
):
    half, depth = xa_ref.shape
    rows = 2 * half
    step, last = pl.program_id(0), pl.num_programs(0) - 1
    e, live = info[0], info[1].astype(F32)
    dp, tens, wop, wor, woc = wo_ref.shape
    fr, fc = w1_ref.shape[3:]
    wide = tens * fc
    ff = u1_ref.shape[2]
    parts = ff // wide
    if late:
        w1_late, w2_late, *sems = late
        items = []
        for k in range(w1_src.shape[0]):
            for src, out in ((w1_src, w1_late), (w2_src, w2_late)):
                cut = pl.ds(k, 1)
                items.append(Item(plan, sems, len(items), src.at[cut], at(out, cut), len(items) % 2))
        steps = schedule(items)
        known = parts - len(items) // 2
    else:
        known = parts

    def put(unit, cols, value):
        per = grads_ref.shape[3] // depth
        cuts = grads_ref.shape[1]
        spot = (unit % per) * depth + cols
        if not isinstance(spot, int):
            spot = pl.multiple_of(spot, 128)
        grads_ref[unit // (per * cuts), unit // per % cuts, :, pl.ds(spot, value.shape[1])] = value.astype(BF16)

    if late:
        pl.when(step == 0)(plan.greet)
        pl.when(step == 0)(steps[0])
        delay = known - len(items[0].stages) - 1
        for n in range(1 if delay else 2, len(steps) - 1):
            pl.when(step == n + delay)(steps[n])
        for n in range(parts - known):
            @pl.when(step == known + n)
            def _():
                items[2 * n].finish()
                items[2 * n + 1].finish()

    @pl.when(step == 0)
    def _():
        for a in range(dp):
            for t in range(tens):
                for k in range(wop):
                    row = (t * wop + k) * wor
                    wo_s[row : row + wor, a * woc : (a + 1) * woc] = wo_ref[a, t, k]
        ctx = ctx_ref[...]
        low = mm_nt(ctx, od_ref[e])
        lowo_s[...] = low
        attention = mm(ctx, wo_s[...]) + mm(low.astype(BF16), ou_ref[e])
        for part, ref in enumerate((xa_ref, xb_ref)):
            s = slice(part * half, (part + 1) * half)
            mid_s[s, :] = ref[...].astype(F32) + attention[s, :]
        for part, ref in enumerate((ca_ref, cb_ref)):
            s = slice(part * half, (part + 1) * half)
            gm_ref[s, :] = ref[...].astype(F32) * live
        gf_s[...] = gm_ref[...].astype(BF16)
        normed, _ = norm_parts(mid_s[...])
        n_s[...] = (normed * gain_ref[...]).astype(BF16)
        low1_s[...] = mm_nt(n_s[...], d1_ref[e])
        b2_s[...] = mm_nt(gf_s[...], u2_ref[e])
        feed_s[...] = jnp.zeros_like(feed_s)
        gn_s[...] = jnp.zeros_like(gn_s)
        low2_s[...] = jnp.zeros_like(low2_s)
        b1_s[...] = jnp.zeros_like(b1_s)

    def stage(ref_1, ref_2, part):
        for a in range(dp):
            for t in range(tens):
                w1_s[a * fr : (a + 1) * fr, t * fc : (t + 1) * fc] = ref_1[a, t, part]
                w2_s[t * fr : (t + 1) * fr, a * woc : (a + 1) * woc] = ref_2[a, t, part]

    if late:
        @pl.when(step < known)
        def _():
            stage(w1_ref, w2_ref, 0)

        @pl.when(step >= known)
        def _():
            stage(w1_late, w2_late, step - known)
    else:
        stage(w1_ref, w2_ref, 0)

    w1, w2 = w1_s[...], w2_s[...]
    runs = [pl.multiple_of((t * parts + step) * fc, fc) for t in range(tens)]
    u1 = jnp.concatenate([u1_ref[e, :, pl.ds(run, fc)] for run in runs], axis=1)
    d2 = jnp.concatenate([d2_ref[e, :, pl.ds(run, fc)] for run in runs], axis=1)
    n, gf = n_s[...], gf_s[...]
    low1, b2 = low1_s[...].astype(BF16), b2_s[...].astype(BF16)
    preact = mm(n, w1) + mm(low1, u1)
    ghid = mm_nt(gf, w2) + mm(b2, d2)
    if late and not delay:
        pl.when(step == 0)(steps[1])
    hid, slope = gelu_both(preact)
    hid = hid.astype(BF16)
    gpre = (ghid * slope).astype(BF16)
    feed_s[...] += mm(hid, w2)
    gn_s[...] += mm_nt(gpre, w1)
    low2_s[...] += mm_nt(hid, d2)
    b1_s[...] += mm_nt(gpre, u1)
    gu1, gd2 = mm_tn(low1, gpre), mm_tn(b2, hid)
    for t, run in enumerate(runs):
        cols = slice(t * fc, (t + 1) * fc)
        put(4 + run // depth, lax.rem(run, depth), gu1[:, cols])
        put(4 + ff // depth + run // depth, lax.rem(run, depth), gd2[:, cols])

    @pl.when(step == last)
    def _():
        low2, b1 = low2_s[...].astype(BF16), b1_s[...].astype(BF16)
        out = live * (mid_s[...] + feed_s[...] + mm(low2, u2_ref[e]))
        la_ref[...] = out[:half].astype(BF16)
        lb_ref[...] = out[half:].astype(BF16)
        put(3, 0, mm_tn(low2, gf_s[...]))
        gn = gn_s[...] + mm(b1, d1_ref[e])
        normed, scale = norm_parts(mid_s[...])
        put(2, 0, mm_tn(b1, n_s[...]))
        gm = gm_ref[...] + norm_back(normed, scale, gain_ref[...], gn)
        gm_ref[...] = gm
        ga = gm.astype(BF16)
        back = mm_nt(ga, ou_ref[e]).astype(BF16)
        gctx_ref[...] = (mm_nt(ga, wo_s[...]) + mm(back, od_ref[e])).astype(BF16)
        put(0, 0, mm_tn(back, ctx_ref[...]))
        put(1, 0, mm_tn(lowo_s[...].astype(BF16), ga))


def feed_forward(plan, info, xa, xb, ca, cb, ctx, gain, wo, w1, w2, late, od, ou, d1, u1, d2, u2, number):
    half, depth = xa.shape
    rows = 2 * half
    adapters, rank = od.shape[:2]
    dp, tens, wop, wor, woc = wo.shape
    fr, fc = w1.shape[3:]
    wide = tens * fc
    ff = u1.shape[2]
    known = w1.shape[2]
    once = lambda *shape: pl.BlockSpec(shape, lambda f: (0,) * len(shape), pipeline_mode=pl.Buffered(1))
    whole = lambda *shape: pl.BlockSpec(shape, lambda f: (0,) * len(shape))
    table, table_f = once(adapters, rank, depth), once(adapters, rank, ff)
    place = lambda f: (0, 0, jnp.minimum(f, known - 1), 0, 0)
    units = 4 + 2 * ff // depth
    cuts = 2
    hbm = pl.BlockSpec(memory_space=pl.ANY)
    scratch = [
        pltpu.VMEM((depth, depth), BF16),
        pltpu.VMEM((depth, wide), BF16),
        pltpu.VMEM((wide, depth), BF16),
        pltpu.VMEM((rows, depth), F32),
        pltpu.VMEM((rows, depth), BF16),
        pltpu.VMEM((rows, depth), BF16),
        pltpu.VMEM((rows, depth), F32),
        pltpu.VMEM((rows, depth), F32),
    ] + [pltpu.VMEM((rows, rank), F32)] * 5
    extra = {}
    if late:
        scratch += [pltpu.VMEM((dp, tens) + part.shape, BF16) for part in late]
        scratch += plan.semaphores(2 * late[0].shape[0])
        extra = dict(collective_id=number, has_side_effects=True)
    else:
        late = [jnp.zeros((16, 128), BF16)] * 2
    return pl.pallas_call(
        functools.partial(feed_kernel, plan),
        grid=(ff // wide,),
        in_specs=[
            pl.BlockSpec(memory_space=pltpu.SMEM),
            once(half, depth), once(half, depth), once(half, depth), once(half, depth),
            once(rows, depth),
            whole(1, depth),
            once(dp, tens, wop, wor, woc),
            pl.BlockSpec((dp, tens, 1, fr, fc), place),
            pl.BlockSpec((dp, tens, 1, fr, woc), place),
            hbm, hbm,
            table, table, table, table_f, table_f, table,
        ],
        out_specs=[
            whole(half, depth), whole(half, depth), whole(rows, depth), whole(rows, depth),
            whole(2, cuts, rank, units * depth // (2 * cuts)),
        ],
        scratch_shapes=scratch,
        out_shape=[
            jax.ShapeDtypeStruct((half, depth), BF16),
            jax.ShapeDtypeStruct((half, depth), BF16),
            jax.ShapeDtypeStruct((rows, depth), F32),
            jax.ShapeDtypeStruct((rows, depth), BF16),
            jax.ShapeDtypeStruct((2, cuts, rank, units * depth // (2 * cuts)), BF16),
        ],
        compiler_params=pltpu.CompilerParams(vmem_limit_bytes=VMEM_BYTES, **extra),
        name="feed_forward",
    )(info, xa, xb, ca, cb, ctx, gain, wo, w1, w2, late[0], late[1], od, ou, d1, u1, d2, u2)


def split3(x):
    hi = x.astype(BF16)
    rest = x - hi.astype(F32)
    mid = rest.astype(BF16)
    return hi, mid, (rest - mid.astype(F32)).astype(BF16)


def attend_back_kernel(
    plan, q_ref, k_ref, v_ref, k2_ref, v2_ref, g_ref, o_ref, lse_ref, la_ref, lb_ref, grads_ref,
    dq_ref, dkv_ref, far_ref, lo_ref, early_ref,
    ks, vs, qs, gs, acc, far_s, far_send, far_recv, lo_local, lo_send, lo_recv, *pool,
):
    rows = q_ref.shape[0]
    step, steps = pl.program_id(0), pl.num_programs(0)
    me, t = lax.axis_index("dp"), lax.axis_index("tensor")
    route = Route(False, lo_local, lo_send, lo_recv)
    early = Pool(plan, grads_ref, early_ref, *pool).steps
    blocks = (la_ref, lb_ref)

    @pl.when(step == 0)
    def _():
        plan.greet(route.peers)

    for n, one in zip((0, 1, 3, 5, 7), early[:-1]):
        @pl.when(step == n)
        def _():
            one()

    @pl.when(step == 3)
    def _():
        route.start(blocks, lo_ref)

    def far(n):
        return pltpu.make_async_remote_copy(
            src_ref=far_s.at[lax.rem(n, 2)],
            dst_ref=far_ref.at[:, :, pl.ds(pl.multiple_of(n * 128, 128), 128)],
            send_sem=far_send.at[n], recv_sem=far_recv.at[n],
            device_id=(me ^ 1, t), device_id_type=pl.DeviceIdType.MESH,
        )

    zero = BF16(0)
    lane = lax.broadcasted_iota(jnp.int32, (1, 128), 1)
    scale = BF16(HEAD_DIM ** -0.5)
    q2, g2 = q_ref[...] * scale, g_ref[...]
    prod = g2.astype(F32) * o_ref[...].astype(F32)

    def less(parts, b):
        return jnp.where(lane == b, -parts[0], jnp.where(lane == b + 1, -parts[1], jnp.where(lane == b + 2, -parts[2], zero)))

    totals = split3(lse_ref[...])
    for h in range(2):
        mine, b = (lane // HEAD_DIM) == h, HEAD_DIM * h
        s = slice(h * rows, (h + 1) * rows)
        qs[s, 0:128] = jnp.where(mine, q2, zero)
        qs[s, 128:256] = less(totals, b)
        gs[s, 0:128] = jnp.where(mine, g2, zero)
        gs[s, 128:256] = less(split3(jnp.sum(jnp.where(mine, prod, 0.0), axis=1, keepdims=True)), b)
    ones = jnp.broadcast_to((lax.rem(lane, HEAD_DIM) < 3).astype(BF16), (rows, 128))

    @pl.when(step >= 2)
    def _():
        far(step - 2).wait_send()

    slot = lax.rem(step, 2)
    for i, (kr, vr) in enumerate(((k2_ref, v2_ref), (k_ref, v_ref))):
        s = slice(i * rows, (i + 1) * rows)
        ks[s, 0:128] = kr[0]
        vs[s, 0:128] = vr[0]
        ks[s, 128:256] = ones
        vs[s, 128:256] = ones
        p = jnp.exp(mm_nt(ks[s, :], qs[...]))
        ds = (p * mm_nt(vs[s, :], gs[...])).astype(BF16)
        dv = mm(p.astype(BF16), gs[:, 0:128]).astype(BF16)
        dk = mm(ds, qs[:, 0:128]).astype(BF16)
        dq = mm_tn(ds, ks[s, 0:128])
        dq = jnp.where(lane < HEAD_DIM, dq[:rows], dq[rows:])
        if i == 0:
            far_s[slot, 0] = dk
            far_s[slot, 1] = dv
            far(step).start()
            acc[...] = dq
        else:
            dkv_ref[0] = dk
            dkv_ref[1] = dv
            dq_ref[...] = ((acc[...] + dq) * (HEAD_DIM ** -0.5)).astype(BF16)

    @pl.when(step == steps - 1)
    def _():
        early[-1]()
        route.wait(blocks, lo_ref)
        far(step - 1).wait_send()
        far(step).wait_send()
        lax.fori_loop(0, steps, lambda n, c: (far(n).wait_recv(), c)[1], 0)


def attend_back(plan, dps, q, kv, kv2, g, ctx, lse, la, lb, grads, number):
    rows, depth = q.shape
    flat = pl.BlockSpec((rows, 128), lambda i: (0, i))
    part = lambda j: pl.BlockSpec((1, rows, 128), lambda i: (j, 0, i))
    both = pl.BlockSpec((2, rows, 128), lambda i: (0, 0, i))
    hbm = pl.BlockSpec(memory_space=pl.ANY)
    heads = depth // 128
    dma = lambda *shape: pltpu.SemaphoreType.DMA(shape)
    return pl.pallas_call(
        functools.partial(attend_back_kernel, plan),
        grid=(heads,),
        in_specs=[flat, part(0), part(1), part(0), part(1), flat, flat, flat, hbm, hbm,
                  pl.BlockSpec(grads.shape, lambda i: (0, 0, 0, 0), pipeline_mode=pl.Buffered(1))],
        out_specs=[flat, both, hbm, hbm, hbm],
        out_shape=[
            jax.ShapeDtypeStruct((rows, depth), BF16),
            jax.ShapeDtypeStruct((2, rows, depth), BF16),
            jax.ShapeDtypeStruct((2, rows, depth), BF16),
            jax.ShapeDtypeStruct((2,) + la.shape, BF16),
            jax.ShapeDtypeStruct((dps, plan.tens) + grads.shape[1:], BF16),
        ],
        scratch_shapes=[pltpu.VMEM((2 * rows, 256), BF16)] * 4
        + [pltpu.VMEM((rows, 128), F32), pltpu.VMEM((2, 2, rows, 128), BF16), dma(heads), dma(heads),
           *Route.semaphores()]
        + Pool.scratch(plan, grads.shape[1:]),
        compiler_params=pltpu.CompilerParams(
            vmem_limit_bytes=VMEM_BYTES, collective_id=number, has_side_effects=True
        ),
        name="attend_back",
    )(q, kv, kv, kv2, kv2, g, ctx, lse, la, lb, grads)


def low_back_kernel(info, x_ref, gain_ref, dq_ref, dkv_ref, dkv2_ref, low_ref, up_ref, gkv_ref, back_ref, grads_ref):
    half = x_ref.shape[1]
    step, last = pl.program_id(0), pl.num_programs(0) - 1
    cuts = grads_ref.shape[1]

    def go(g, first):
        back = mm_nt(g, up_ref[0, 0])
        back_ref[...] = back if first else back_ref[...] + back
        grads_ref[(step + 1) // cuts, lax.rem(step + 1, cuts)] = mm_tn(low_ref[...].astype(BF16), g).astype(BF16)

    @pl.when(step == 0)
    def _():
        go(dq_ref[...], True)

    @pl.when(step > 0)
    def _():
        g = (dkv_ref[0].astype(F32) + dkv2_ref[0].astype(F32)).astype(BF16)
        gkv_ref[0] = g
        go(g, False)

    @pl.when(step == last)
    def _():
        total = None
        for part in range(2):
            normed, _ = norm_parts(x_ref[part].astype(F32))
            back = back_ref[part * half : (part + 1) * half, :].astype(BF16)
            term = mm_tn(back, (normed * gain_ref[...]).astype(BF16))
            total = term if total is None else total + term
        grads_ref[0, 0] = total.astype(BF16)


def low_back(info, x, gain, dq, dkv, dkv2, low, up):
    _, half, depth = x.shape
    rows, rank = 2 * half, low.shape[1]
    once = lambda *shape: pl.BlockSpec(shape, lambda j, info: (0,) * len(shape), pipeline_mode=pl.Buffered(1))
    pair = pl.BlockSpec((1, rows, depth), lambda j, info: (jnp.maximum(j - 1, 0), 0, 0))
    return pl.pallas_call(
        low_back_kernel,
        grid_spec=pltpu.PrefetchScalarGridSpec(
            num_scalar_prefetch=1,
            grid=(3,),
            in_specs=[
                once(2, half, depth), once(1, depth), once(rows, depth), pair, pair, once(rows, rank),
                pl.BlockSpec((1, 1, rank, depth), lambda j, info: (info[0], j, 0, 0)),
            ],
            out_specs=[
                pair, pl.BlockSpec((rows, rank), lambda j, info: (0, 0)),
                pl.BlockSpec((2, 2, rank, depth), lambda j, info: (0, 0, 0, 0)),
            ],
        ),
        out_shape=[
            jax.ShapeDtypeStruct((2, rows, depth), BF16),
            jax.ShapeDtypeStruct((rows, rank), F32),
            jax.ShapeDtypeStruct((2, 2, rank, depth), BF16),
        ],
        compiler_params=params(),
        name="low_back",
    )(info, x, gain, dq, dkv, dkv2, low, up)


def outro_kernel(
    plan, info, x_ref, gain_ref, dq_ref, gkv_ref, back_ref, gm_ref, w_ref, down_ref, grads_ref,
    ya_ref, yb_ref, late_ref, gn_s, *pool,
):
    half, depth = x_ref.shape[1:]
    parts, width = w_ref.shape[1], w_ref.shape[4]
    step, last = pl.program_id(0), pl.num_programs(0) - 1
    late = Pool(plan, grads_ref, late_ref, *pool).steps

    @pl.when(step == 0)
    def _():
        plan.greet()
        late[0]()

    def go(g, first):
        acc = mm(back_ref[...].astype(BF16), down_ref[info[0]]) if first else gn_s[...]
        for part in range(parts):
            cols = slice(part * width, (part + 1) * width)
            acc = acc + mm_nt(g[:, cols], w_ref[:, part, 0].reshape(depth, width))
        gn_s[...] = acc

    @pl.when(step == 0)
    def _():
        go(dq_ref[...], True)
        late[1]()

    @pl.when(step > 0)
    def _():
        go(gkv_ref[0], False)

    @pl.when(step == 1)
    def _():
        late[2]()

    @pl.when(step == last)
    def _():
        late[3]()
        for part, y_ref in enumerate((ya_ref, yb_ref)):
            s = slice(part * half, (part + 1) * half)
            normed, scale = norm_parts(x_ref[part].astype(F32))
            y_ref[...] = (gm_ref[s, :] + norm_back(normed, scale, gain_ref[...], gn_s[s, :])).astype(BF16)
        for one in late[4:]:
            one()


def outro(plan, dps, info, x, gain, dq, gkv, back, gm, w, down, grads, number):
    _, half, depth = x.shape
    rows = 2 * half
    dp, tens, _, wr, wc = w.shape
    whole = lambda *shape: pl.BlockSpec(shape, lambda j: (0,) * len(shape))
    once = lambda *shape: pl.BlockSpec(shape, lambda j: (0,) * len(shape), pipeline_mode=pl.Buffered(1))
    return pl.pallas_call(
        functools.partial(outro_kernel, plan),
        grid=(3,),
        in_specs=[
            pl.BlockSpec(memory_space=pltpu.SMEM),
            once(2, half, depth), once(1, depth), once(rows, depth),
            pl.BlockSpec((1, rows, depth), lambda j: (jnp.maximum(j - 1, 0), 0, 0)),
            once(*back.shape), once(rows, depth),
            pl.BlockSpec((dp, tens, 1, wr, wc), lambda j: (0, 0, j, 0, 0)),
            once(*down.shape), once(*grads.shape),
        ],
        out_specs=[whole(half, depth), whole(half, depth), pl.BlockSpec(memory_space=pl.ANY)],
        out_shape=[
            jax.ShapeDtypeStruct((half, depth), BF16),
            jax.ShapeDtypeStruct((half, depth), BF16),
            jax.ShapeDtypeStruct((dps, plan.tens) + grads.shape[1:], BF16),
        ],
        scratch_shapes=[pltpu.VMEM((rows, depth), F32)] + Pool.scratch(plan, grads.shape[1:]),
        compiler_params=pltpu.CompilerParams(
            vmem_limit_bytes=VMEM_BYTES, collective_id=number, has_side_effects=True
        ),
        name="outro",
    )(info, x, gain, dq, gkv, back, gm, w, down, grads)


def table_kernel(places, unit, owner, g_ref, *outs):
    _, _, tens, cuts, _, width = g_ref.shape
    pair, per = pl.program_id(0), width // unit

    @pl.when(pair == 0)
    def _():
        for out in outs:
            out[...] = jnp.zeros_like(out)

    for t in range(tens):
        e = owner[pair * tens + t]
        for n, (out, sub, start) in enumerate(places):
            col = n % per * unit
            piece = g_ref[0, n // (per * cuts), t, n // per % cuts, :, col : col + unit].astype(F32)
            if sub is None:
                outs[out][e, :, start : start + unit] += piece
            else:
                outs[out][e, sub, :, start : start + unit] += piece


def tables(owner, gathered, outs, places, unit):
    dps = gathered.shape[0]
    gathered = gathered.reshape((dps // 2, 2) + gathered.shape[1:])
    block = (1,) + gathered.shape[1:]
    return pl.pallas_call(
        functools.partial(table_kernel, places, unit),
        grid_spec=pltpu.PrefetchScalarGridSpec(
            num_scalar_prefetch=1,
            grid=(dps // 2,),
            in_specs=[pl.BlockSpec(block, lambda p, owner: (p, 0, 0, 0, 0, 0))],
            out_specs=[pl.BlockSpec(shape, lambda p, owner, n=len(shape): (0,) * n) for shape in outs],
        ),
        out_shape=[jax.ShapeDtypeStruct(shape, F32) for shape in outs],
        compiler_params=params(),
        name="tables",
    )(owner, gathered)


def per_device(
    tokens, cotangent, clip_live, adapter_index, gain_one, gain_two, weight_qkv, weight_out, weight_fc1, weight_fc2,
    qkv_down, qkv_up, out_down, out_up, fc1_down, fc1_up, fc2_down, fc2_up,
):
    dps, tens = lax.axis_size("dp"), lax.axis_size("tensor")
    slots = tokens.shape[0]
    axes = ("dp", "tensor")
    dp, t = lax.axis_index("dp"), lax.axis_index("tensor")
    assert slots == 2 and tens == 4 and dps % 2 == 0

    def route(flip):
        perm = []
        for a in range(dps):
            for b in range(tens):
                slot = (b % 2) ^ flip
                perm.append((a * tens + b, (a - a % 2 + b // 2) * tens + 2 * (a % 2) + slot))
        return perm

    routes = [route(0), route(1)]
    swap = [(a * tens + b, (a ^ 1) * tens + b) for a in range(dps) for b in range(tens)]
    back_routes = [[(d, s) for s, d in r] for r in routes]

    def spread(field):
        parts = []
        for flip in range(2):
            slot = (t % 2) ^ flip
            parts.append(lax.ppermute(lax.dynamic_index_in_dim(field, slot, 0, False), axes, routes[flip]))
        return parts

    def unspread(parts):
        got = [lax.ppermute(part, axes, r) for part, r in zip(parts, back_routes)]
        return jnp.where(t % 2 == 0, jnp.stack(got), jnp.stack(got[::-1]))

    both = jnp.stack([adapter_index, clip_live], axis=1)
    other = lax.ppermute(both, axes, swap)
    info = jnp.where(t // 2 == dp % 2, both, other)
    info = lax.dynamic_index_in_dim(info, t % 2, 0, False)
    codes = jnp.broadcast_to(adapter_index.reshape(1, 1, 2, 1), (1, 4, 2, 128)).reshape(1, 8, 128)

    def fold(w, dim):
        k = max(1, 128 // w.shape[dim])
        if k == 1:
            return w
        w = jnp.moveaxis(w.reshape((dps // k, k) + w.shape[1:]), 1, dim)
        return w.reshape(w.shape[:dim] + (-1,) + w.shape[dim + 2 :])

    plan = Plan(dps, tens)
    g1, g2 = gain_one.reshape(1, -1), gain_two.reshape(1, -1)
    parts_q = weight_qkv.reshape(-1, 16, weight_qkv.shape[2])
    in_rows = weight_fc1.shape[0]
    parts_1 = weight_fc1.reshape(in_rows, -1, 128).transpose(1, 0, 2)
    parts_2 = weight_fc2.reshape(parts_1.shape[0], -1, weight_fc2.shape[1])
    parts_o = weight_out.reshape(2, -1, weight_out.shape[1])
    late, fine = [], 2
    if dps <= 8:
        fine, n = 8, parts_1.shape[0] * EARLY // 8
        late = [parts_1[n:], parts_2[n:]]
        parts_1, parts_2 = parts_1[:n], parts_2[:n]
    x, q, kv, kv2, low, reach, codes, w_qkv, w_out, w_fc1, w_fc2 = intro(
        plan, dps, info, tokens, codes, g1, parts_q, parts_o, parts_1, parts_2, qkv_down, qkv_up, fine, 0
    )
    owner = codes[:, 0, 0, :2, 0].reshape(-1)
    xa, xb = x[0], x[1]
    w_qkv = fold(w_qkv.reshape((dps, tens) + weight_qkv.shape), 3)
    cotangent, q = lax.optimization_barrier((cotangent, q))
    ca, cb = spread(cotangent)
    ctx, lse = attend(reach, q, kv, kv2)
    w_out, w_fc1, w_fc2 = fold(w_out, 4), fold(w_fc1, 3), fold(w_fc2, 4)
    la, lb, gm, gctx, grads = feed_forward(
        plan, info, xa, xb, ca, cb, ctx, g2, w_out, w_fc1, w_fc2, late,
        out_down, out_up, fc1_down, fc1_up, fc2_down, fc2_up, 2,
    )
    dq, dkv, dkv2, layer_out, early = attend_back(plan, dps, q, kv, kv2, gctx, ctx, lse, la, lb, grads, 3)
    depth, ff = out_down.shape[2], fc1_up.shape[2]
    gkv, back, grads = low_back(info, x, g1, dq, dkv, dkv2, low, qkv_up)
    ya, yb, late_grads = outro(plan, dps, info, x, g1, dq, gkv, back, gm, w_qkv, qkv_down, grads, 4)
    grad_tokens = unspread([ya, yb])
    late_grads, early, owner, ya = lax.optimization_barrier((late_grads, early, owner, ya))
    t_od, t_ou, t_d1, t_u2, t_u1, t_d2 = tables(
        owner, early, [a.shape for a in (out_down, out_up, fc1_down, fc2_up, fc1_up, fc2_down)],
        [(n, None, 0) for n in range(4)] + [(n, None, c) for n in (4, 5) for c in range(0, ff, depth)], depth,
    )
    t_qd, t_qu = tables(
        owner, late_grads, [qkv_down.shape, qkv_up.shape], [(0, None, 0)] + [(1, j, 0) for j in range(3)], depth
    )
    return layer_out, grad_tokens, t_qd, t_qu, t_od, t_ou, t_d1, t_u1, t_d2, t_u2


def solution(mesh):
    rows, whole = P("dp", "tensor", None), P()
    return jax.shard_map(
        per_device,
        mesh=mesh,
        in_specs=(rows, rows, P("dp"), P("dp"), whole, whole, P(None, "dp", "tensor"), P("tensor", "dp"),
                  P("dp", "tensor"), P("tensor", "dp")) + (whole,) * 8,
        out_specs=(rows, rows) + (whole,) * 8,
        check_vma=False,
    )
```

```python
import functools
import math

import jax
import jax.numpy as jnp
from jax import lax
from jax.experimental import pallas as pl
from jax.experimental.pallas import tpu as pltpu
from jax.sharding import PartitionSpec as P

HEAD_DIM = 64
EPS = 1e-06
F32 = jnp.float32
BF16 = jnp.bfloat16
NT = (((1,), (1,)), ((), ()))
TN = (((0,), (0,)), ((), ()))
VMEM_BYTES = 61 << 20
SAFE_SCORE = 60.0
EARLY = 4


def mm(a, b):
    return jnp.dot(a, b, preferred_element_type=F32)


def mm_nt(a, b):
    return lax.dot_general(a, b, NT, preferred_element_type=F32)


def mm_tn(a, b):
    return lax.dot_general(a, b, TN, preferred_element_type=F32)


def norm_parts(field):
    centered = field - jnp.mean(field, axis=-1, keepdims=True)
    scale = lax.rsqrt(jnp.mean(centered * centered, axis=-1, keepdims=True) + EPS)
    return centered * scale, scale


def norm_back(normed, scale, gain, incoming):
    weighted = incoming * gain
    return scale * (
        weighted
        - jnp.mean(weighted, axis=-1, keepdims=True)
        - normed * jnp.mean(weighted * normed, axis=-1, keepdims=True)
    )


def params(*semantics):
    return pltpu.CompilerParams(vmem_limit_bytes=VMEM_BYTES)


class Plan:
    def __init__(self, dps, tens):
        self.tens = tens
        bits = [1 << i for i in range(1, dps.bit_length() - 1)]
        self.orders = (bits + [1], bits[::-1] + [1])
        self.hops = dps - 1
        self.ways = []
        for order in self.orders:
            blocks = [0]
            for bit in order:
                blocks = blocks + [r | bit for r in blocks]
            tops = {r: max([j for j, bit in enumerate(order) if r & bit], default=-1) for r in blocks}
            sends = {r: range(tops[r] + 1, len(order)) for r in blocks}
            ids = {}
            for r in blocks:
                for j in sends[r]:
                    ids[(r, j)] = len(ids)
            blocks.sort(key=lambda r: bin(r).count("1"))
            self.ways.append((order, blocks, tops, sends, ids))

    def semaphores(self, items):
        dma = lambda *shape: pltpu.SemaphoreType.DMA(shape)
        near = self.tens - 1
        return [dma(items), dma(items, near), dma(items, near), dma(items, self.hops), dma(items, self.hops)]

    def greet(self, extra=()):
        me, t = lax.axis_index("dp"), lax.axis_index("tensor")
        peers = [(me, lax.rem(t + k, self.tens)) for k in range(1, self.tens)]
        peers += [(me ^ bit, t) for bit in self.orders[0]]
        peers += list(extra)
        barrier = pltpu.get_barrier_semaphore()
        for peer in peers:
            pl.semaphore_signal(barrier, inc=1, device_id=peer, device_id_type=pl.DeviceIdType.MESH)
        pl.semaphore_wait(barrier, len(peers))


class Item:
    def __init__(self, plan, sems, number, src, spot, order):
        self.plan, self.src, self.spot = plan, src, spot
        self.local, self.zs, self.zr, self.ss, self.rs = [s.at[number] for s in sems]
        self.order, self.blocks, self.tops, self.sends, self.ids = plan.ways[order]
        self.me, self.t = lax.axis_index("dp"), lax.axis_index("tensor")
        passed = [r for r in self.blocks if len(self.sends[r])]
        far = sorted({bin(r).count("1") for r in passed})
        self.stages = [[r for r in passed if bin(r).count("1") == n] for n in far]

    def keep(self):
        return pltpu.make_async_copy(self.src, self.spot(self.me, self.t), self.local)

    def along(self, d, arriving=False):
        n = self.plan.tens
        return pltpu.make_async_remote_copy(
            src_ref=self.src,
            dst_ref=self.spot(self.me, lax.rem(self.t + n - d, n) if arriving else self.t),
            send_sem=self.zs.at[d - 1],
            recv_sem=self.zr.at[d - 1],
            device_id=(self.me, lax.rem(self.t + d, n)),
            device_id_type=pl.DeviceIdType.MESH,
        )

    def across(self, r, j, arriving=False):
        bit, n = self.order[j], self.ids[(r, j)]
        block = self.me ^ r
        return pltpu.make_async_remote_copy(
            src_ref=self.spot(block, None),
            dst_ref=self.spot(block ^ bit if arriving else block, None),
            send_sem=self.ss.at[n],
            recv_sem=self.rs.at[n],
            device_id=(self.me ^ bit, self.t),
            device_id_type=pl.DeviceIdType.MESH,
        )

    def start(self):
        self.keep().start()
        for d in range(1, self.plan.tens):
            self.along(d).start()

    def arrived(self, r):
        if r == 0:
            self.keep().wait()
            for d in range(1, self.plan.tens):
                self.along(d, True).wait_recv()
        else:
            j = self.tops[r]
            self.across(r ^ self.order[j], j, True).wait_recv()

    def advance(self, stage):
        for r in self.stages[stage]:
            self.arrived(r)
            for j in self.sends[r]:
                self.across(r, j).start()

    def finish(self):
        for r in self.blocks:
            if not len(self.sends[r]):
                self.arrived(r)
        for d in range(1, self.plan.tens):
            self.along(d).wait_send()
        for r in self.blocks:
            for j in self.sends[r]:
                self.across(r, j).wait_send()


def schedule(items):
    pairs = [items[k : k + 2] for k in range(0, len(items), 2)]
    stages = len(items[0].stages)

    def step(s):
        for item in pairs[0:2] if s == 0 else pairs[s + 1 : s + 2]:
            for one in item:
                one.start()
        for n, pair in enumerate(pairs):
            if 0 <= s - 1 - n < stages:
                for one in pair:
                    one.advance(s - 1 - n)

    def close():
        for item in items:
            item.finish()

    return [functools.partial(step, s) for s in range(len(pairs) + stages)] + [close]


class Route:
    def __init__(self, out, local, send, recv):
        self.out, self.local, self.send, self.recv = out, local, send, recv
        me, t = lax.axis_index("dp"), lax.axis_index("tensor")
        self.me, self.t = me, t
        core, high, low = lax.rem(me, 2), t // 2, lax.rem(t, 2)
        self.stays = core == high
        base = me - core
        self.peers = [(me ^ 1, t ^ 2), (base + high, 2 * core + 1 - low)]
        self.low = low

    def copy(self, f, src, out, arriving=False):
        if self.out:
            src, slot = src.at[self.low ^ f], f
        else:
            src, slot = src[f], self.low ^ f if arriving else self.low
        return pltpu.make_async_remote_copy(
            src_ref=src, dst_ref=out.at[slot], send_sem=self.send.at[f], recv_sem=self.recv.at[f],
            device_id=self.peers[f], device_id_type=pl.DeviceIdType.MESH,
        )

    def stay(self, blocks, out):
        if self.out:
            return pltpu.make_async_copy(blocks.at[self.low], out.at[0], self.local)
        return pltpu.make_async_copy(blocks[0], out.at[self.low], self.local)

    def start(self, blocks, out):
        self.copy(1, blocks, out).start()

        @pl.when(self.stays)
        def _():
            self.stay(blocks, out).start()

        @pl.when(jnp.logical_not(self.stays))
        def _():
            self.copy(0, blocks, out).start()

    def wait(self, blocks, out):
        @pl.when(self.stays)
        def _():
            self.stay(blocks, out).wait()

        @pl.when(jnp.logical_not(self.stays))
        def _():
            self.copy(0, blocks, out, True).wait_recv()
            self.copy(0, blocks, out).wait_send()

        self.copy(1, blocks, out, True).wait_recv()
        self.copy(1, blocks, out).wait_send()

    @staticmethod
    def semaphores():
        return [pltpu.SemaphoreType.DMA, pltpu.SemaphoreType.DMA((2,)), pltpu.SemaphoreType.DMA((2,))]


def at(ref, cut):
    return lambda a, t: ref.at[a, :, cut] if t is None else ref.at[a, t, cut]


class Pool:
    def __init__(self, plan, x_ref, o_ref, got, src, swap_send, swap_recv, *sems):
        me, t = lax.axis_index("dp"), lax.axis_index("tensor")
        self.mine = lax.rem(me, 2)
        self.x_ref, self.got, self.src = x_ref, got, src
        self.swap = pltpu.make_async_remote_copy(
            src_ref=x_ref.at[1 - self.mine], dst_ref=got, send_sem=swap_send, recv_sem=swap_recv,
            device_id=(me ^ 1, t), device_id_type=pl.DeviceIdType.MESH,
        )
        cuts = src.shape[0]
        self.items = [Item(plan, sems, k, src.at[pl.ds(k, 1)], at(o_ref, pl.ds(k, 1)), k % 2) for k in range(cuts)]
        steps = schedule(self.items)
        self.steps = [self.swap.start, functools.partial(self.add, steps[0])] + steps[1:]

    def add(self, then):
        self.swap.wait()
        self.src[...] = (self.x_ref[self.mine].astype(F32) + self.got[...].astype(F32)).astype(BF16)
        then()

    @staticmethod
    def scratch(plan, shape):
        return [pltpu.VMEM(shape, BF16), pltpu.VMEM(shape, BF16), pltpu.SemaphoreType.DMA, pltpu.SemaphoreType.DMA
                ] + plan.semaphores(shape[0])


def intro_kernel(
    plan, info, tok_ref, codes_ref, gain_ref, w_ref, wo_ref, w1_ref, w2_ref, down_ref, up_ref,
    x_ref, q_ref, kv_ref, kv2_ref, low_ref, reach_ref, codes_out, w_out, wo_out, w1_out, w2_out,
    x_s, w_s, n_s, kv_s, far_s, far_got, keep_sem, kv_send, kv_recv, far_send, far_recv, r_local, r_send, r_recv, *sems,
):
    half, depth = x_ref.shape[1:]
    tens, width = plan.tens, w_ref.shape[2]
    me, t = lax.axis_index("dp"), lax.axis_index("tensor")
    sems_w, sems = sems[:5], sems[5:]
    cuts = sems_w[0].shape[0]
    size = w_ref.shape[0] // cuts
    first = [Item(plan, sems_w, k, w_ref.at[pl.ds(k * size, size)], at(w_s, pl.ds(k * size, size)), k % 2) for k in range(cuts)]
    rest = []
    for pairs in (((codes_ref, codes_out),), ((wo_ref, wo_out),), ((w1_ref, w1_out), (w2_ref, w2_out))):
        for k in range(pairs[0][0].shape[0]):
            for src, out in pairs:
                rest.append((src.at[pl.ds(k, 1)], at(out, pl.ds(k, 1))))
    rest = rest[1:] + rest[:1]
    rest = [Item(plan, sems, n, src, spot, n % 2) for n, (src, spot) in enumerate(rest)]
    later = schedule(rest)
    route = Route(True, r_local, r_send, r_recv)
    e = info[0]

    plan.greet(route.peers)
    for item in first:
        item.start()
    stages = len(first[0].stages)
    for s in range(cuts // 2 + stages - 1):
        for n in range(cuts // 2):
            if 0 <= s - n < stages:
                first[2 * n].advance(s - n)
                first[2 * n + 1].advance(s - n)
        if s == cuts // 2 - 1:
            later[0]()
            route.start(tok_ref, x_s)
    later[1]()
    later[2]()
    later[3]()
    later[4]()
    route.wait(tok_ref, x_s)
    x_ref[...] = x_s[...]
    for part in range(2):
        normed, _ = norm_parts(x_s[part].astype(F32))
        n_s[part * half : (part + 1) * half, :] = normed * gain_ref[...]
    n = n_s[...].astype(BF16)
    low = mm_nt(n, down_ref[e])
    low_ref[...] = low
    low = low.astype(BF16)
    for item in first:
        item.finish()
    keep = pltpu.make_async_copy(w_s, w_out, keep_sem)
    keep.start()
    swap = pltpu.make_async_remote_copy(
        src_ref=kv_s, dst_ref=kv2_ref, send_sem=kv_send, recv_sem=kv_recv,
        device_id=(me ^ 1, t), device_id_type=pl.DeviceIdType.MESH,
    )
    far_swap = pltpu.make_async_remote_copy(
        src_ref=far_s, dst_ref=far_got, send_sem=far_send, recv_sem=far_recv,
        device_id=(me ^ 1, t), device_id_type=pl.DeviceIdType.MESH,
    )
    blocks = w_ref.shape[0] // 3
    for turn, j in enumerate((1, 2, 0)):
        if turn == 1:
            later[5]()
        for c in range(tens):
            cols = slice(c * width, (c + 1) * width)
            w = w_s[:, c, j * blocks : (j + 1) * blocks].reshape(depth, width)
            res = (mm(n, w) + mm(low, up_ref[e, j, :, cols])).astype(BF16)
            if j == 0:
                q_ref[:, cols] = res
            else:
                kv_s[j - 1, :, cols] = res
            if j != 2:
                spread = lax.broadcasted_iota(jnp.int32, (width, 128), 0) // HEAD_DIM + c * (width // HEAD_DIM)
                spread = (spread == lax.broadcasted_iota(jnp.int32, (width, 128), 1)).astype(BF16)
                norms = mm(res * res, spread)
                reach = norms if c == 0 else reach + norms
        if j != 2:
            reach = 1.02 * jnp.max(reach, axis=0, keepdims=True)
        if j == 1:
            far_s[...] = jnp.broadcast_to(reach, far_s.shape)
            far_swap.start()
        if j == 0:
            far_swap.wait()
            reach_ref[...] = reach * jnp.maximum(far_s[...], far_got[...]) * (1.0 / HEAD_DIM)
        if j == 2:
            swap.start()
            kv_ref[...] = kv_s[...]
    for one in later[6:]:
        one()
    swap.wait()
    keep.wait()


def intro(plan, dps, info, tokens, codes, gain, w, wo, w1, w2, down, up, cuts, number):
    _, half, depth = tokens.shape
    rows, rank = 2 * half, down.shape[1]
    hbm, vm = pl.BlockSpec(memory_space=pl.ANY), pl.BlockSpec(memory_space=pltpu.VMEM)
    big = lambda x: jax.ShapeDtypeStruct((dps, plan.tens) + x.shape, x.dtype)
    items = codes.shape[0] + wo.shape[0] + 2 * w1.shape[0]
    return pl.pallas_call(
        functools.partial(intro_kernel, plan),
        in_specs=[pl.BlockSpec(memory_space=pltpu.SMEM), hbm, hbm, vm, hbm, hbm, hbm, hbm, vm, vm],
        out_specs=[vm, vm, vm, hbm, vm, vm] + [hbm] * 5,
        out_shape=[
            jax.ShapeDtypeStruct(tokens.shape, BF16),
            jax.ShapeDtypeStruct((rows, depth), BF16),
            jax.ShapeDtypeStruct((2, rows, depth), BF16),
            jax.ShapeDtypeStruct((2, rows, depth), BF16),
            jax.ShapeDtypeStruct((rows, rank), F32),
            jax.ShapeDtypeStruct((8, 128), F32),
            big(codes), big(w), big(wo), big(w1), big(w2),
        ],
        scratch_shapes=[
            pltpu.VMEM(tokens.shape, BF16), pltpu.VMEM((dps, plan.tens) + w.shape, BF16), pltpu.VMEM((rows, depth), F32),
            pltpu.VMEM((2, rows, depth), BF16), pltpu.VMEM((8, 128), F32), pltpu.VMEM((8, 128), F32),
        ]
        + [pltpu.SemaphoreType.DMA] * 5
        + Route.semaphores() + plan.semaphores(cuts) + plan.semaphores(items),
        compiler_params=pltpu.CompilerParams(
            vmem_limit_bytes=VMEM_BYTES, collective_id=number, has_side_effects=True
        ),
        name="intro",
    )(info, tokens, codes, gain, w, wo, w1, w2, down, up)


def attend_pair(q2, ks, vs, shifted):
    lane = lax.broadcasted_iota(jnp.int32, (1, 128), 1)
    outs, lses = [], []
    for h in range(2):
        mine = (lane // HEAD_DIM) == h
        s = mm_nt(jnp.where(mine, q2, BF16(0)), ks[...])
        if shifted:
            m = jnp.max(s, axis=1, keepdims=True)
            p = jnp.exp(s - m).astype(BF16)
        else:
            p = jnp.exp(s).astype(BF16)
        o = mm(p, vs[h])
        total = pltpu.roll(o, HEAD_DIM, 1)
        outs.append(o / total)
        lse = jnp.log(jnp.where(mine, total, o))
        lses.append(lse + m if shifted else lse)
    return (
        jnp.where(lane < HEAD_DIM, outs[0], outs[1]).astype(BF16),
        jnp.where(lane < HEAD_DIM, lses[0], lses[1]),
    )


def stage_keys(k_ref, v_ref, k2_ref, v2_ref, ks, vs):
    rows = k_ref.shape[1]
    lane = lax.broadcasted_iota(jnp.int32, (1, 128), 1)
    ks[0:rows, :] = k_ref[0]
    ks[rows:, :] = k2_ref[0]
    for h in range(2):
        mine = (lane // HEAD_DIM) == h
        vs[h, 0:rows, :] = jnp.where(mine, v_ref[0], BF16(1))
        vs[h, rows:, :] = jnp.where(mine, v2_ref[0], BF16(1))


def attend_kernel(safe, q_ref, k_ref, v_ref, k2_ref, v2_ref, o_ref, lse_ref, ks, vs):
    stage_keys(k_ref, v_ref, k2_ref, v2_ref, ks, vs)
    q2 = q_ref[...] * BF16(HEAD_DIM ** -0.5)
    pair = safe[pl.program_id(0)]

    @pl.when(pair == 1)
    def _():
        o_ref[...], lse_ref[...] = attend_pair(q2, ks, vs, False)

    @pl.when(pair != 1)
    def _():
        o_ref[...], lse_ref[...] = attend_pair(q2, ks, vs, True)


def attend(reach, q, kv, kv2):
    rows, depth = q.shape
    heads = depth // 128
    safe = (jnp.max(reach[0, : 2 * heads].reshape(heads, 2), axis=1) <= SAFE_SCORE * SAFE_SCORE).astype(jnp.int32)
    flat = pl.BlockSpec((rows, 128), lambda i, safe: (0, i))
    part = lambda j: pl.BlockSpec((1, rows, 128), lambda i, safe: (j, 0, i))
    return pl.pallas_call(
        attend_kernel,
        grid_spec=pltpu.PrefetchScalarGridSpec(
            num_scalar_prefetch=1,
            grid=(heads,),
            in_specs=[flat, part(0), part(1), part(0), part(1)],
            out_specs=[flat, flat],
            scratch_shapes=[pltpu.VMEM((2 * rows, 128), BF16), pltpu.VMEM((2, 2 * rows, 128), BF16)],
        ),
        out_shape=[jax.ShapeDtypeStruct((rows, depth), BF16), jax.ShapeDtypeStruct((rows, depth), F32)],
        compiler_params=params(),
        name="attend",
    )(safe, q, kv, kv, kv2, kv2)


def gelu_both(x):
    cdf = 0.5 * (1.0 + lax.erf(x * (2.0 ** -0.5)))
    pdf = jnp.exp(-0.5 * x * x) * ((2.0 * math.pi) ** -0.5)
    return x * cdf, cdf + x * pdf


def feed_kernel(
    plan, info, xa_ref, xb_ref, ca_ref, cb_ref, ctx_ref, gain_ref, wo_ref, w1_ref, w2_ref, w1_src, w2_src,
    od_ref, ou_ref, d1_ref, u1_ref, d2_ref, u2_ref,
    la_ref, lb_ref, gm_ref, gctx_ref, grads_ref,
    wo_s, w1_s, w2_s, mid_s, n_s, gf_s, feed_s, gn_s, lowo_s, low1_s, low2_s, b1_s, b2_s, *late,
):
    half, depth = xa_ref.shape
    rows = 2 * half
    step, last = pl.program_id(0), pl.num_programs(0) - 1
    e, live = info[0], info[1].astype(F32)
    dp, tens, wop, wor, woc = wo_ref.shape
    fr, fc = w1_ref.shape[3:]
    wide = tens * fc
    ff = u1_ref.shape[2]
    parts = ff // wide
    if late:
        w1_late, w2_late, *sems = late
        items = []
        for k in range(w1_src.shape[0]):
            for src, out in ((w1_src, w1_late), (w2_src, w2_late)):
                cut = pl.ds(k, 1)
                items.append(Item(plan, sems, len(items), src.at[cut], at(out, cut), len(items) % 2))
        steps = schedule(items)
        known = parts - len(items) // 2
    else:
        known = parts

    def put(unit, cols, value):
        per = grads_ref.shape[3] // depth
        cuts = grads_ref.shape[1]
        spot = (unit % per) * depth + cols
        if not isinstance(spot, int):
            spot = pl.multiple_of(spot, 128)
        grads_ref[unit // (per * cuts), unit // per % cuts, :, pl.ds(spot, value.shape[1])] = value.astype(BF16)

    if late:
        pl.when(step == 0)(plan.greet)
        pl.when(step == 0)(steps[0])
        delay = known - len(items[0].stages) - 1
        for n in range(1 if delay else 2, len(steps) - 1):
            pl.when(step == n + delay)(steps[n])
        for n in range(parts - known):
            @pl.when(step == known + n)
            def _():
                items[2 * n].finish()
                items[2 * n + 1].finish()

    @pl.when(step == 0)
    def _():
        for a in range(dp):
            for t in range(tens):
                for k in range(wop):
                    row = (t * wop + k) * wor
                    wo_s[row : row + wor, a * woc : (a + 1) * woc] = wo_ref[a, t, k]
        ctx = ctx_ref[...]
        low = mm_nt(ctx, od_ref[e])
        lowo_s[...] = low
        attention = mm(ctx, wo_s[...]) + mm(low.astype(BF16), ou_ref[e])
        for part, ref in enumerate((xa_ref, xb_ref)):
            s = slice(part * half, (part + 1) * half)
            mid_s[s, :] = ref[...].astype(F32) + attention[s, :]
        for part, ref in enumerate((ca_ref, cb_ref)):
            s = slice(part * half, (part + 1) * half)
            gm_ref[s, :] = ref[...].astype(F32) * live
        gf_s[...] = gm_ref[...].astype(BF16)
        normed, _ = norm_parts(mid_s[...])
        n_s[...] = (normed * gain_ref[...]).astype(BF16)
        low1_s[...] = mm_nt(n_s[...], d1_ref[e])
        b2_s[...] = mm_nt(gf_s[...], u2_ref[e])
        feed_s[...] = jnp.zeros_like(feed_s)
        gn_s[...] = jnp.zeros_like(gn_s)
        low2_s[...] = jnp.zeros_like(low2_s)
        b1_s[...] = jnp.zeros_like(b1_s)

    def stage(ref_1, ref_2, part):
        for a in range(dp):
            for t in range(tens):
                w1_s[a * fr : (a + 1) * fr, t * fc : (t + 1) * fc] = ref_1[a, t, part]
                w2_s[t * fr : (t + 1) * fr, a * woc : (a + 1) * woc] = ref_2[a, t, part]

    if late:
        @pl.when(step < known)
        def _():
            stage(w1_ref, w2_ref, 0)

        @pl.when(step >= known)
        def _():
            stage(w1_late, w2_late, step - known)
    else:
        stage(w1_ref, w2_ref, 0)

    w1, w2 = w1_s[...], w2_s[...]
    runs = [pl.multiple_of((t * parts + step) * fc, fc) for t in range(tens)]
    u1 = jnp.concatenate([u1_ref[e, :, pl.ds(run, fc)] for run in runs], axis=1)
    d2 = jnp.concatenate([d2_ref[e, :, pl.ds(run, fc)] for run in runs], axis=1)
    n, gf = n_s[...], gf_s[...]
    low1, b2 = low1_s[...].astype(BF16), b2_s[...].astype(BF16)
    preact = mm(n, w1) + mm(low1, u1)
    ghid = mm_nt(gf, w2) + mm(b2, d2)
    if late and not delay:
        pl.when(step == 0)(steps[1])
    hid, slope = gelu_both(preact)
    hid = hid.astype(BF16)
    gpre = (ghid * slope).astype(BF16)
    feed_s[...] += mm(hid, w2)
    gn_s[...] += mm_nt(gpre, w1)
    low2_s[...] += mm_nt(hid, d2)
    b1_s[...] += mm_nt(gpre, u1)
    gu1, gd2 = mm_tn(low1, gpre), mm_tn(b2, hid)
    for t, run in enumerate(runs):
        cols = slice(t * fc, (t + 1) * fc)
        put(4 + run // depth, lax.rem(run, depth), gu1[:, cols])
        put(4 + ff // depth + run // depth, lax.rem(run, depth), gd2[:, cols])

    @pl.when(step == last)
    def _():
        low2, b1 = low2_s[...].astype(BF16), b1_s[...].astype(BF16)
        out = live * (mid_s[...] + feed_s[...] + mm(low2, u2_ref[e]))
        la_ref[...] = out[:half].astype(BF16)
        lb_ref[...] = out[half:].astype(BF16)
        put(3, 0, mm_tn(low2, gf_s[...]))
        gn = gn_s[...] + mm(b1, d1_ref[e])
        normed, scale = norm_parts(mid_s[...])
        put(2, 0, mm_tn(b1, n_s[...]))
        gm = gm_ref[...] + norm_back(normed, scale, gain_ref[...], gn)
        gm_ref[...] = gm
        ga = gm.astype(BF16)
        back = mm_nt(ga, ou_ref[e]).astype(BF16)
        gctx_ref[...] = (mm_nt(ga, wo_s[...]) + mm(back, od_ref[e])).astype(BF16)
        put(0, 0, mm_tn(back, ctx_ref[...]))
        put(1, 0, mm_tn(lowo_s[...].astype(BF16), ga))


def feed_forward(plan, info, xa, xb, ca, cb, ctx, gain, wo, w1, w2, late, od, ou, d1, u1, d2, u2, number):
    half, depth = xa.shape
    rows = 2 * half
    adapters, rank = od.shape[:2]
    dp, tens, wop, wor, woc = wo.shape
    fr, fc = w1.shape[3:]
    wide = tens * fc
    ff = u1.shape[2]
    known = w1.shape[2]
    once = lambda *shape: pl.BlockSpec(shape, lambda f: (0,) * len(shape), pipeline_mode=pl.Buffered(1))
    whole = lambda *shape: pl.BlockSpec(shape, lambda f: (0,) * len(shape))
    table, table_f = once(adapters, rank, depth), once(adapters, rank, ff)
    place = lambda f: (0, 0, jnp.minimum(f, known - 1), 0, 0)
    units = 4 + 2 * ff // depth
    cuts = 2
    hbm = pl.BlockSpec(memory_space=pl.ANY)
    scratch = [
        pltpu.VMEM((depth, depth), BF16),
        pltpu.VMEM((depth, wide), BF16),
        pltpu.VMEM((wide, depth), BF16),
        pltpu.VMEM((rows, depth), F32),
        pltpu.VMEM((rows, depth), BF16),
        pltpu.VMEM((rows, depth), BF16),
        pltpu.VMEM((rows, depth), F32),
        pltpu.VMEM((rows, depth), F32),
    ] + [pltpu.VMEM((rows, rank), F32)] * 5
    extra = {}
    if late:
        scratch += [pltpu.VMEM((dp, tens) + part.shape, BF16) for part in late]
        scratch += plan.semaphores(2 * late[0].shape[0])
        extra = dict(collective_id=number, has_side_effects=True)
    else:
        late = [jnp.zeros((16, 128), BF16)] * 2
    return pl.pallas_call(
        functools.partial(feed_kernel, plan),
        grid=(ff // wide,),
        in_specs=[
            pl.BlockSpec(memory_space=pltpu.SMEM),
            once(half, depth), once(half, depth), once(half, depth), once(half, depth),
            once(rows, depth),
            whole(1, depth),
            once(dp, tens, wop, wor, woc),
            pl.BlockSpec((dp, tens, 1, fr, fc), place),
            pl.BlockSpec((dp, tens, 1, fr, woc), place),
            hbm, hbm,
            table, table, table, table_f, table_f, table,
        ],
        out_specs=[
            whole(half, depth), whole(half, depth), whole(rows, depth), whole(rows, depth),
            whole(2, cuts, rank, units * depth // (2 * cuts)),
        ],
        scratch_shapes=scratch,
        out_shape=[
            jax.ShapeDtypeStruct((half, depth), BF16),
            jax.ShapeDtypeStruct((half, depth), BF16),
            jax.ShapeDtypeStruct((rows, depth), F32),
            jax.ShapeDtypeStruct((rows, depth), BF16),
            jax.ShapeDtypeStruct((2, cuts, rank, units * depth // (2 * cuts)), BF16),
        ],
        compiler_params=pltpu.CompilerParams(vmem_limit_bytes=VMEM_BYTES, **extra),
        name="feed_forward",
    )(info, xa, xb, ca, cb, ctx, gain, wo, w1, w2, late[0], late[1], od, ou, d1, u1, d2, u2)


def split3(x):
    hi = x.astype(BF16)
    rest = x - hi.astype(F32)
    mid = rest.astype(BF16)
    return hi, mid, (rest - mid.astype(F32)).astype(BF16)


def attend_back_kernel(
    plan, q_ref, k_ref, v_ref, k2_ref, v2_ref, g_ref, o_ref, lse_ref, la_ref, lb_ref, grads_ref,
    dq_ref, dkv_ref, far_ref, lo_ref, early_ref,
    ks, vs, qs, gs, acc, far_s, far_send, far_recv, lo_local, lo_send, lo_recv, *pool,
):
    rows = q_ref.shape[0]
    step, steps = pl.program_id(0), pl.num_programs(0)
    me, t = lax.axis_index("dp"), lax.axis_index("tensor")
    route = Route(False, lo_local, lo_send, lo_recv)
    early = Pool(plan, grads_ref, early_ref, *pool).steps
    blocks = (la_ref, lb_ref)

    @pl.when(step == 0)
    def _():
        plan.greet(route.peers)

    for n, one in zip((0, 1, 3, 5, 7), early[:-1]):
        @pl.when(step == n)
        def _():
            one()

    @pl.when(step == 3)
    def _():
        route.start(blocks, lo_ref)

    def far(n):
        return pltpu.make_async_remote_copy(
            src_ref=far_s.at[lax.rem(n, 2)],
            dst_ref=far_ref.at[:, :, pl.ds(pl.multiple_of(n * 128, 128), 128)],
            send_sem=far_send.at[n], recv_sem=far_recv.at[n],
            device_id=(me ^ 1, t), device_id_type=pl.DeviceIdType.MESH,
        )

    zero = BF16(0)
    lane = lax.broadcasted_iota(jnp.int32, (1, 128), 1)
    scale = BF16(HEAD_DIM ** -0.5)
    q2, g2 = q_ref[...] * scale, g_ref[...]
    prod = g2.astype(F32) * o_ref[...].astype(F32)

    def less(parts, b):
        return jnp.where(lane == b, -parts[0], jnp.where(lane == b + 1, -parts[1], jnp.where(lane == b + 2, -parts[2], zero)))

    totals = split3(lse_ref[...])
    for h in range(2):
        mine, b = (lane // HEAD_DIM) == h, HEAD_DIM * h
        s = slice(h * rows, (h + 1) * rows)
        qs[s, 0:128] = jnp.where(mine, q2, zero)
        qs[s, 128:256] = less(totals, b)
        gs[s, 0:128] = jnp.where(mine, g2, zero)
        gs[s, 128:256] = less(split3(jnp.sum(jnp.where(mine, prod, 0.0), axis=1, keepdims=True)), b)
    ones = jnp.broadcast_to((lax.rem(lane, HEAD_DIM) < 3).astype(BF16), (rows, 128))

    @pl.when(step >= 2)
    def _():
        far(step - 2).wait_send()

    slot = lax.rem(step, 2)
    for i, (kr, vr) in enumerate(((k2_ref, v2_ref), (k_ref, v_ref))):
        s = slice(i * rows, (i + 1) * rows)
        ks[s, 0:128] = kr[0]
        vs[s, 0:128] = vr[0]
        ks[s, 128:256] = ones
        vs[s, 128:256] = ones
        p = jnp.exp(mm_nt(ks[s, :], qs[...]))
        ds = (p * mm_nt(vs[s, :], gs[...])).astype(BF16)
        dv = mm(p.astype(BF16), gs[:, 0:128]).astype(BF16)
        dk = mm(ds, qs[:, 0:128]).astype(BF16)
        dq = mm_tn(ds, ks[s, 0:128])
        dq = jnp.where(lane < HEAD_DIM, dq[:rows], dq[rows:])
        if i == 0:
            far_s[slot, 0] = dk
            far_s[slot, 1] = dv
            far(step).start()
            acc[...] = dq
        else:
            dkv_ref[0] = dk
            dkv_ref[1] = dv
            dq_ref[...] = ((acc[...] + dq) * (HEAD_DIM ** -0.5)).astype(BF16)

    @pl.when(step == steps - 1)
    def _():
        early[-1]()
        route.wait(blocks, lo_ref)
        far(step - 1).wait_send()
        far(step).wait_send()
        lax.fori_loop(0, steps, lambda n, c: (far(n).wait_recv(), c)[1], 0)


def attend_back(plan, dps, q, kv, kv2, g, ctx, lse, la, lb, grads, number):
    rows, depth = q.shape
    flat = pl.BlockSpec((rows, 128), lambda i: (0, i))
    part = lambda j: pl.BlockSpec((1, rows, 128), lambda i: (j, 0, i))
    both = pl.BlockSpec((2, rows, 128), lambda i: (0, 0, i))
    hbm = pl.BlockSpec(memory_space=pl.ANY)
    heads = depth // 128
    dma = lambda *shape: pltpu.SemaphoreType.DMA(shape)
    return pl.pallas_call(
        functools.partial(attend_back_kernel, plan),
        grid=(heads,),
        in_specs=[flat, part(0), part(1), part(0), part(1), flat, flat, flat, hbm, hbm,
                  pl.BlockSpec(grads.shape, lambda i: (0, 0, 0, 0), pipeline_mode=pl.Buffered(1))],
        out_specs=[flat, both, hbm, hbm, hbm],
        out_shape=[
            jax.ShapeDtypeStruct((rows, depth), BF16),
            jax.ShapeDtypeStruct((2, rows, depth), BF16),
            jax.ShapeDtypeStruct((2, rows, depth), BF16),
            jax.ShapeDtypeStruct((2,) + la.shape, BF16),
            jax.ShapeDtypeStruct((dps, plan.tens) + grads.shape[1:], BF16),
        ],
        scratch_shapes=[pltpu.VMEM((2 * rows, 256), BF16)] * 4
        + [pltpu.VMEM((rows, 128), F32), pltpu.VMEM((2, 2, rows, 128), BF16), dma(heads), dma(heads),
           *Route.semaphores()]
        + Pool.scratch(plan, grads.shape[1:]),
        compiler_params=pltpu.CompilerParams(
            vmem_limit_bytes=VMEM_BYTES, collective_id=number, has_side_effects=True
        ),
        name="attend_back",
    )(q, kv, kv, kv2, kv2, g, ctx, lse, la, lb, grads)


def low_back_kernel(info, x_ref, gain_ref, dq_ref, dkv_ref, dkv2_ref, low_ref, up_ref, gkv_ref, back_ref, grads_ref):
    half = x_ref.shape[1]
    step, last = pl.program_id(0), pl.num_programs(0) - 1
    cuts = grads_ref.shape[1]

    def go(g, first):
        back = mm_nt(g, up_ref[0, 0])
        back_ref[...] = back if first else back_ref[...] + back
        grads_ref[(step + 1) // cuts, lax.rem(step + 1, cuts)] = mm_tn(low_ref[...].astype(BF16), g).astype(BF16)

    @pl.when(step == 0)
    def _():
        go(dq_ref[...], True)

    @pl.when(step > 0)
    def _():
        g = (dkv_ref[0].astype(F32) + dkv2_ref[0].astype(F32)).astype(BF16)
        gkv_ref[0] = g
        go(g, False)

    @pl.when(step == last)
    def _():
        total = None
        for part in range(2):
            normed, _ = norm_parts(x_ref[part].astype(F32))
            back = back_ref[part * half : (part + 1) * half, :].astype(BF16)
            term = mm_tn(back, (normed * gain_ref[...]).astype(BF16))
            total = term if total is None else total + term
        grads_ref[0, 0] = total.astype(BF16)


def low_back(info, x, gain, dq, dkv, dkv2, low, up):
    _, half, depth = x.shape
    rows, rank = 2 * half, low.shape[1]
    once = lambda *shape: pl.BlockSpec(shape, lambda j, info: (0,) * len(shape), pipeline_mode=pl.Buffered(1))
    pair = pl.BlockSpec((1, rows, depth), lambda j, info: (jnp.maximum(j - 1, 0), 0, 0))
    return pl.pallas_call(
        low_back_kernel,
        grid_spec=pltpu.PrefetchScalarGridSpec(
            num_scalar_prefetch=1,
            grid=(3,),
            in_specs=[
                once(2, half, depth), once(1, depth), once(rows, depth), pair, pair, once(rows, rank),
                pl.BlockSpec((1, 1, rank, depth), lambda j, info: (info[0], j, 0, 0)),
            ],
            out_specs=[
                pair, pl.BlockSpec((rows, rank), lambda j, info: (0, 0)),
                pl.BlockSpec((2, 2, rank, depth), lambda j, info: (0, 0, 0, 0)),
            ],
        ),
        out_shape=[
            jax.ShapeDtypeStruct((2, rows, depth), BF16),
            jax.ShapeDtypeStruct((rows, rank), F32),
            jax.ShapeDtypeStruct((2, 2, rank, depth), BF16),
        ],
        compiler_params=params(),
        name="low_back",
    )(info, x, gain, dq, dkv, dkv2, low, up)


def outro_kernel(
    plan, info, x_ref, gain_ref, dq_ref, gkv_ref, back_ref, gm_ref, w_ref, down_ref, grads_ref,
    ya_ref, yb_ref, late_ref, gn_s, *pool,
):
    half, depth = x_ref.shape[1:]
    parts, width = w_ref.shape[1], w_ref.shape[4]
    step, last = pl.program_id(0), pl.num_programs(0) - 1
    late = Pool(plan, grads_ref, late_ref, *pool).steps

    @pl.when(step == 0)
    def _():
        plan.greet()
        late[0]()

    def go(g, first):
        acc = mm(back_ref[...].astype(BF16), down_ref[info[0]]) if first else gn_s[...]
        for part in range(parts):
            cols = slice(part * width, (part + 1) * width)
            acc = acc + mm_nt(g[:, cols], w_ref[:, part, 0].reshape(depth, width))
        gn_s[...] = acc

    @pl.when(step == 0)
    def _():
        go(dq_ref[...], True)
        late[1]()

    @pl.when(step > 0)
    def _():
        go(gkv_ref[0], False)

    @pl.when(step == 1)
    def _():
        late[2]()

    @pl.when(step == last)
    def _():
        late[3]()
        for part, y_ref in enumerate((ya_ref, yb_ref)):
            s = slice(part * half, (part + 1) * half)
            normed, scale = norm_parts(x_ref[part].astype(F32))
            y_ref[...] = (gm_ref[s, :] + norm_back(normed, scale, gain_ref[...], gn_s[s, :])).astype(BF16)
        for one in late[4:]:
            one()


def outro(plan, dps, info, x, gain, dq, gkv, back, gm, w, down, grads, number):
    _, half, depth = x.shape
    rows = 2 * half
    dp, tens, _, wr, wc = w.shape
    whole = lambda *shape: pl.BlockSpec(shape, lambda j: (0,) * len(shape))
    once = lambda *shape: pl.BlockSpec(shape, lambda j: (0,) * len(shape), pipeline_mode=pl.Buffered(1))
    return pl.pallas_call(
        functools.partial(outro_kernel, plan),
        grid=(3,),
        in_specs=[
            pl.BlockSpec(memory_space=pltpu.SMEM),
            once(2, half, depth), once(1, depth), once(rows, depth),
            pl.BlockSpec((1, rows, depth), lambda j: (jnp.maximum(j - 1, 0), 0, 0)),
            once(*back.shape), once(rows, depth),
            pl.BlockSpec((dp, tens, 1, wr, wc), lambda j: (0, 0, j, 0, 0)),
            once(*down.shape), once(*grads.shape),
        ],
        out_specs=[whole(half, depth), whole(half, depth), pl.BlockSpec(memory_space=pl.ANY)],
        out_shape=[
            jax.ShapeDtypeStruct((half, depth), BF16),
            jax.ShapeDtypeStruct((half, depth), BF16),
            jax.ShapeDtypeStruct((dps, plan.tens) + grads.shape[1:], BF16),
        ],
        scratch_shapes=[pltpu.VMEM((rows, depth), F32)] + Pool.scratch(plan, grads.shape[1:]),
        compiler_params=pltpu.CompilerParams(
            vmem_limit_bytes=VMEM_BYTES, collective_id=number, has_side_effects=True
        ),
        name="outro",
    )(info, x, gain, dq, gkv, back, gm, w, down, grads)


def table_kernel(places, unit, owner, g_ref, *outs):
    _, _, tens, cuts, _, width = g_ref.shape
    pair, per = pl.program_id(0), width // unit

    @pl.when(pair == 0)
    def _():
        for out in outs:
            out[...] = jnp.zeros_like(out)

    for t in range(tens):
        e = owner[pair * tens + t]
        for n, (out, sub, start) in enumerate(places):
            col = n % per * unit
            piece = g_ref[0, n // (per * cuts), t, n // per % cuts, :, col : col + unit].astype(F32)
            if sub is None:
                outs[out][e, :, start : start + unit] += piece
            else:
                outs[out][e, sub, :, start : start + unit] += piece


def tables(owner, gathered, outs, places, unit):
    dps = gathered.shape[0]
    gathered = gathered.reshape((dps // 2, 2) + gathered.shape[1:])
    block = (1,) + gathered.shape[1:]
    return pl.pallas_call(
        functools.partial(table_kernel, places, unit),
        grid_spec=pltpu.PrefetchScalarGridSpec(
            num_scalar_prefetch=1,
            grid=(dps // 2,),
            in_specs=[pl.BlockSpec(block, lambda p, owner: (p, 0, 0, 0, 0, 0))],
            out_specs=[pl.BlockSpec(shape, lambda p, owner, n=len(shape): (0,) * n) for shape in outs],
        ),
        out_shape=[jax.ShapeDtypeStruct(shape, F32) for shape in outs],
        compiler_params=params(),
        name="tables",
    )(owner, gathered)


def per_device(
    tokens, cotangent, clip_live, adapter_index, gain_one, gain_two, weight_qkv, weight_out, weight_fc1, weight_fc2,
    qkv_down, qkv_up, out_down, out_up, fc1_down, fc1_up, fc2_down, fc2_up,
):
    dps, tens = lax.axis_size("dp"), lax.axis_size("tensor")
    slots = tokens.shape[0]
    axes = ("dp", "tensor")
    dp, t = lax.axis_index("dp"), lax.axis_index("tensor")
    assert slots == 2 and tens == 4 and dps % 2 == 0

    def route(flip):
        perm = []
        for a in range(dps):
            for b in range(tens):
                slot = (b % 2) ^ flip
                perm.append((a * tens + b, (a - a % 2 + b // 2) * tens + 2 * (a % 2) + slot))
        return perm

    routes = [route(0), route(1)]
    swap = [(a * tens + b, (a ^ 1) * tens + b) for a in range(dps) for b in range(tens)]
    back_routes = [[(d, s) for s, d in r] for r in routes]

    def spread(field):
        parts = []
        for flip in range(2):
            slot = (t % 2) ^ flip
            parts.append(lax.ppermute(lax.dynamic_index_in_dim(field, slot, 0, False), axes, routes[flip]))
        return parts

    def unspread(parts):
        got = [lax.ppermute(part, axes, r) for part, r in zip(parts, back_routes)]
        return jnp.where(t % 2 == 0, jnp.stack(got), jnp.stack(got[::-1]))

    both = jnp.stack([adapter_index, clip_live], axis=1)
    other = lax.ppermute(both, axes, swap)
    info = jnp.where(t // 2 == dp % 2, both, other)
    info = lax.dynamic_index_in_dim(info, t % 2, 0, False)
    codes = jnp.broadcast_to(adapter_index.reshape(1, 1, 2, 1), (1, 4, 2, 128)).reshape(1, 8, 128)

    def fold(w, dim):
        k = max(1, 128 // w.shape[dim])
        if k == 1:
            return w
        w = jnp.moveaxis(w.reshape((dps // k, k) + w.shape[1:]), 1, dim)
        return w.reshape(w.shape[:dim] + (-1,) + w.shape[dim + 2 :])

    plan = Plan(dps, tens)
    g1, g2 = gain_one.reshape(1, -1), gain_two.reshape(1, -1)
    parts_q = weight_qkv.reshape(-1, 16, weight_qkv.shape[2])
    in_rows = weight_fc1.shape[0]
    parts_1 = weight_fc1.reshape(in_rows, -1, 128).transpose(1, 0, 2)
    parts_2 = weight_fc2.reshape(parts_1.shape[0], -1, weight_fc2.shape[1])
    parts_o = weight_out.reshape(2, -1, weight_out.shape[1])
    late, fine = [], 2
    if dps <= 8:
        fine, n = 8, parts_1.shape[0] * EARLY // 8
        late = [parts_1[n:], parts_2[n:]]
        parts_1, parts_2 = parts_1[:n], parts_2[:n]
    x, q, kv, kv2, low, reach, codes, w_qkv, w_out, w_fc1, w_fc2 = intro(
        plan, dps, info, tokens, codes, g1, parts_q, parts_o, parts_1, parts_2, qkv_down, qkv_up, fine, 0
    )
    owner = codes[:, 0, 0, :2, 0].reshape(-1)
    xa, xb = x[0], x[1]
    w_qkv = fold(w_qkv.reshape((dps, tens) + weight_qkv.shape), 3)
    cotangent, q = lax.optimization_barrier((cotangent, q))
    ca, cb = spread(cotangent)
    ctx, lse = attend(reach, q, kv, kv2)
    w_out, w_fc1, w_fc2 = fold(w_out, 4), fold(w_fc1, 3), fold(w_fc2, 4)
    la, lb, gm, gctx, grads = feed_forward(
        plan, info, xa, xb, ca, cb, ctx, g2, w_out, w_fc1, w_fc2, late,
        out_down, out_up, fc1_down, fc1_up, fc2_down, fc2_up, 2,
    )
    dq, dkv, dkv2, layer_out, early = attend_back(plan, dps, q, kv, kv2, gctx, ctx, lse, la, lb, grads, 3)
    depth, ff = out_down.shape[2], fc1_up.shape[2]
    gkv, back, grads = low_back(info, x, g1, dq, dkv, dkv2, low, qkv_up)
    ya, yb, late_grads = outro(plan, dps, info, x, g1, dq, gkv, back, gm, w_qkv, qkv_down, grads, 4)
    grad_tokens = unspread([ya, yb])
    late_grads, early, owner, ya = lax.optimization_barrier((late_grads, early, owner, ya))
    t_od, t_ou, t_d1, t_u2, t_u1, t_d2 = tables(
        owner, early, [a.shape for a in (out_down, out_up, fc1_down, fc2_up, fc1_up, fc2_down)],
        [(n, None, 0) for n in range(4)] + [(n, None, c) for n in (4, 5) for c in range(0, ff, depth)], depth,
    )
    t_qd, t_qu = tables(
        owner, late_grads, [qkv_down.shape, qkv_up.shape], [(0, None, 0)] + [(1, j, 0) for j in range(3)], depth
    )
    return layer_out, grad_tokens, t_qd, t_qu, t_od, t_ou, t_d1, t_u1, t_d2, t_u2


def solution(mesh):
    rows, whole = P("dp", "tensor", None), P()
    return jax.shard_map(
        per_device,
        mesh=mesh,
        in_specs=(rows, rows, P("dp"), P("dp"), whole, whole, P(None, "dp", "tensor"), P("tensor", "dp"),
                  P("dp", "tensor"), P("tensor", "dp")) + (whole,) * 8,
        out_specs=(rows, rows) + (whole,) * 8,
        check_vma=False,
    )
```
